256 devices in a mesh: user: 16 (over x, y), loader: 16 (over z, core).
Axes of the slice: x: 4, y: 4, z: 8, core: 2. Of those that a mesh axis runs over, the one named last changes fastest.
Arguments:
- history_items: bfloat16 [256, 128, 1024], P(('user', 'loader')), may hold values from -6 to 6
- history_events: int32 [256, 128], P(('user', 'loader')), may hold values from 0 to 63
- history_lengths: int32 [256], P(('user', 'loader')), may hold values from 1 to 128, 20480 in all
- action_table: float32 [64, 1024], replicated, may hold values from -6 to 6
- mix_weight: bfloat16 [1024, 4096], P('loader'), may hold values from -0.1875 to 0.1875
- out_weight: bfloat16 [1024, 1024], P('loader'), may hold values from -0.1875 to 0.1875
- query_weight: bfloat16 [1024, 1024], replicated, may hold values from -0.1875 to 0.1875
- score_weight: float32 [1024], replicated, may hold values from -0.375 to 0.375
- self_weight: float32 [1024], replicated, may hold values from -0.1875 to 0.1875
- candidates: bfloat16 [1024, 128, 1024], P(('user', 'loader')), may hold values from -24 to 24
- block_owner: int32 [1024, 1], P(('user', 'loader')), may hold values from 0 to 15; in each aligned block of 4 rows (0 to 3, 4 to 7, ...) at most 2 rows name the same one
- row_counts: int32 [1024], P(('user', 'loader')), may hold values from 64 to 128
- labels: float32 [1024, 128], P(('user', 'loader')), may hold values from 0 to 1
Outputs:
- scores: float32 [1024, 128], P(('user', 'loader'))
- row_grads: bfloat16 [1024, 128, 1024], P(('user', 'loader'))
- query_grad: float32 [1024, 1024], P('loader')
The draws below stay inside these ranges and needn't reach their ends.
Inputs may be any that keep to these rules, and one draw needn't show every extreme that they name: `block_owner`: no index is named by more than 2 of one device's 4 blocks, and in some device one index is named by exactly 2.
All inputs are finite; a program needn't handle non-finite values. No bound on the sum of `history_lengths` on one device may be relied on, other than what follows from the above.
Results may differ from the reference program's by a relative error of at most 0.017.
Values may be sent and summed in bfloat16 or wider, within the bound.
No kernel may reach another device: no remote copies, remote signals or barrier semaphores. Data moves between devices by JAX's collectives and lax.ppermute only.
A program may use at most 128 MiB of HBM per device.

```python
import math
import jax
import jax.numpy as jnp
import numpy as np
from jax import lax

D = 1024
HEADS = 8
HIST = 128
ACTIONS = 64
BLOCK = 128
BLK_DEV = 4
CAP = 2
USERS = 256
BLOCKS = 1024
N_USER = 16
N_LOADER = 16


def with_ends(entries, rng, smallest, largest):
    longest = entries.shape.index(max(entries.shape))
    spots = []
    for shift in (0, 1):
        where = [jax.random.randint(jax.random.fold_in(rng, axis), (), 0, length) for axis, length in enumerate(entries.shape)]
        where[longest] = (where[longest] + shift) % entries.shape[longest]
        spots.append(tuple(where))
    return entries.at[spots[0]].set(smallest).at[spots[1]].set(largest)


def spiked(result, key, source, target, blocks, factor):
    def block_of(dim):
        return (jnp.arange(result.shape[dim]) // (result.shape[dim] // blocks)).reshape((-1,) + (1,) * (result.ndim - 1 - dim))

    first = jax.random.permutation(key, blocks)[block_of(target)]
    second = (block_of(target) + blocks // 2) % blocks
    return jnp.where((block_of(source) == first) | (block_of(source) == second), factor * result, result)


def shard_levels(stream_key, shape, cuts, smallest, top_value):
    factor_of, own = 1.0, jax.random.fold_in(stream_key, 6)
    for dim, blocks in cuts:
        heights = jnp.exp(jax.random.uniform(jax.random.fold_in(own, dim), (blocks,), jnp.float32, smallest / len(cuts), top_value / len(cuts)))
        factor_of = factor_of * jnp.repeat(heights, shape[dim] // blocks).reshape([-1 if axis == dim else 1 for axis in range(len(shape))])
    return factor_of


def length_profile(amount, total, most, lean):
    loads = [(1 << 20) // math.isqrt(rank ** lean) + 1 for rank in range(2, amount + 1)]
    rest, holding = total - most - (amount - 1), [1] * (amount - 1)
    while rest > 0:
        movable = [i for i in range(amount - 1) if holding[i] < most]
        mass, budget = sum([loads[i] for i in movable]), rest
        for i in movable:
            more = min(most - holding[i], max(1, budget * loads[i] // mass), rest)
            holding[i] = holding[i] + more
            rest = rest - more
    return np.array([most] + holding)


def uneven(stream_key, count, total, reach, lean):
    if count == 2:
        one = jax.random.randint(stream_key, (), max(1, total - reach), min(reach, total - 1) + 1)
        return jnp.stack([one, total - one])
    tallies = jnp.asarray(length_profile(count, total, reach, lean), jnp.int32)
    couples = (count - 1) // 2
    giver, sink = tallies[1:1 + 2 * couples:2], tallies[2:2 + 2 * couples:2]
    margin = jnp.minimum(giver - 1, reach - sink)
    moved = jax.random.randint(jax.random.fold_in(stream_key, 1), (couples,), 0, 1 << 20) % (margin + 1)
    tallies = tallies.at[1:1 + 2 * couples:2].set(giver - moved).at[2:2 + 2 * couples:2].set(sink + moved)
    return tallies[jax.random.permutation(jax.random.fold_in(stream_key, 2), count)]


def deal_out(key, own, number, rows, number_of, top, most, lean):
    sequence = jax.random.permutation(key, number_of)
    crowded, common = shares(number_of, rows * top, most, lean, True), shares(number_of, rows * top, most, lean, False)
    places = jnp.arange(number_of)

    def named(tallies, offset_by):
        used = int((tallies > 0).sum())
        fixed = max(1, used // 4)
        shifted = fixed + (places - fixed + offset_by * (used - fixed)) % max(1, number_of - fixed)
        return jnp.zeros((number_of,), jnp.int32).at[sequence[jnp.where(places < fixed, places, shifted)]].set(jnp.asarray(tallies, jnp.int32))

    tallies = jnp.where(number % 4 == 0, named(crowded, number // 4), named(common, number - number // 4 - 1))
    mixed = jax.random.permutation(jax.random.fold_in(own, 3), number_of)
    giver, taker = mixed[0:number_of // 2 * 2:2], mixed[1:number_of // 2 * 2:2]
    room = jnp.minimum(tallies[giver] - 1, most - tallies[taker]) // 2
    room = jnp.where((giver == sequence[0]) | (taker == sequence[0]) | (tallies[taker] == 0), 0, jnp.maximum(room, 0))
    shifted = jax.random.randint(jax.random.fold_in(own, 4), (number_of // 2,), 0, 1 << 20) % (room + 1)
    tallies = tallies.at[giver].add(-shifted).at[taker].add(shifted)
    items = jnp.searchsorted(jnp.cumsum(tallies), jnp.arange(rows * top), side="right").astype(jnp.int32)
    listing = items.reshape(top, rows).T
    listing = listing[jax.random.permutation(jax.random.fold_in(own, 1), rows)]
    offset_by = jax.random.randint(jax.random.fold_in(own, 2), (rows, 1), 0, top)
    return jnp.take_along_axis(listing, (jnp.arange(top)[None, :] + offset_by) % top, axis=1)


def shares(count, total, limit, skew, full):
    portions = [(1 << 20) // math.isqrt(rank ** skew) + 1 for rank in range(1, count + 1)]
    largest = limit if full else min(limit, max(-(-total // count), total * portions[0] // sum(portions)))
    least = 1 if total - largest >= count - 1 else 0
    holding, rest = [largest] + [least] * (count - 1), total - largest - least * (count - 1)
    while rest > 0:
        free = [i for i in range(1, count) if holding[i] < largest] or [i for i in range(1, count) if holding[i] < limit]
        pool, remaining = sum([portions[i] for i in free]), rest
        for i in free:
            addition = min(limit - holding[i], max(1, remaining * portions[i] // pool), rest)
            holding[i] = holding[i] + addition
            rest = rest - addition
    return np.array(holding)


def noise(stream_key, shape, scale, bound, cuts=(), kind=jnp.bfloat16):
    values = jax.random.normal(stream_key, shape, jnp.float32) * scale
    if len(cuts) > 0:
        values = shard_levels(stream_key, shape, cuts, -0.22, 0.18) * values
    return jnp.clip(values, min=-bound, max=bound).astype(kind)


def noise_with(own_key, dims, spread, most, cuts, heavy, held_as=jnp.bfloat16):
    entries = spread * jax.random.normal(own_key, dims, jnp.float32)
    if cuts:
        entries = entries * shard_levels(own_key, dims, cuts, -0.22, 0.18)
    return jnp.clip(spiked(entries, jax.random.fold_in(own_key, 3), *heavy), -most, most).astype(held_as)


def setup_inputs(seed: int = 0) -> dict:
    arg_keys = jax.random.split(jax.random.key(seed), 14)
    history_items = noise(arg_keys[0], (USERS, HIST, D), 1.0, 6.0, ((0, 256),))
    history_events = with_ends(jax.random.randint(arg_keys[1], (USERS, HIST), 0, ACTIONS), jax.random.fold_in(arg_keys[1], 1), 0, ACTIONS - 1).astype(jnp.int32)
    history_lengths = uneven(arg_keys[2], USERS, USERS * HIST * 5 // 8, HIST, 1).astype(jnp.int32)
    action_table = noise(arg_keys[3], (ACTIONS, D), 1.0, 6.0, (), jnp.float32)
    mix_weight = noise(arg_keys[4], (D, 4 * D), D ** -0.5, 0.1875, ((0, 16),))
    out_weight = noise(arg_keys[5], (D, D), D ** -0.5, 0.1875, ((0, 16),))
    query_weight = noise(arg_keys[6], (D, D), D ** -0.5, 0.1875)
    score_weight = noise(arg_keys[7], (D,), (D // 4) ** -0.5, 0.375, (), jnp.float32)
    self_weight = noise(arg_keys[8], (D,), D ** -0.5, 0.1875, (), jnp.float32)
    candidates = noise_with(arg_keys[9], (BLOCKS, BLOCK, D), 1.0, 24.0, ((0, 256),), (0, 2, 256, 6.0))
    block_owner_keys = jax.random.split(jax.random.fold_in(arg_keys[10], 1), BLOCKS // BLK_DEV)
    block_owner_turns = jax.random.permutation(jax.random.fold_in(arg_keys[10], 3), BLOCKS // BLK_DEV)
    block_owner = jax.vmap(lambda own, number: deal_out(jax.random.fold_in(arg_keys[10], 2), own, number, BLK_DEV, N_USER, 1, CAP, 2))(block_owner_keys, block_owner_turns).reshape((BLOCKS, 1))
    row_counts = with_ends(jax.random.randint(arg_keys[11], (BLOCKS,), BLOCK // 2, BLOCK + 1), jax.random.fold_in(arg_keys[11], 1), BLOCK // 2, BLOCK).astype(jnp.int32)
    labels = jnp.clip(1.0 * jax.random.uniform(arg_keys[12], (BLOCKS, BLOCK), jnp.float32) ** shard_levels(arg_keys[12], (BLOCKS, BLOCK), ((0, 256),), -0.2, 0.2), 0.0, 1.0)
    return dict(history_items=history_items, history_events=history_events, history_lengths=history_lengths, action_table=action_table, mix_weight=mix_weight, out_weight=out_weight, query_weight=query_weight, score_weight=score_weight, self_weight=self_weight, candidates=candidates, block_owner=block_owner, row_counts=row_counts, labels=labels)


def encode_user(items, events, length, action_table, mix_weight, out_weight):
    width = items.shape[1]
    head_dim = width // HEADS
    base = items.astype(jnp.float32) + action_table[events]
    normed = (base * lax.rsqrt(lax.optimization_barrier(jnp.mean(base * base, -1, keepdims=True)) + 1e-06)).astype(jnp.bfloat16)
    projected = jax.nn.silu(jnp.dot(normed, mix_weight, preferred_element_type=jnp.float32))
    gate = projected[:, :width]
    values = projected[:, width:2 * width].astype(jnp.bfloat16).astype(jnp.float32).reshape(HIST, HEADS, head_dim)
    queries = projected[:, 2 * width:3 * width].astype(jnp.bfloat16).astype(jnp.float32).reshape(HIST, HEADS, head_dim)
    keys = projected[:, 3 * width:].astype(jnp.bfloat16).astype(jnp.float32).reshape(HIST, HEADS, head_dim)
    logits = jnp.einsum('ihd,jhd->hij', queries, keys) / math.sqrt(head_dim)
    positions = jnp.arange(HIST, dtype=jnp.int32)
    causal = positions[None, :] <= positions[:, None]
    weights = jnp.where(causal[None], jax.nn.silu(logits) / HIST, 0.0).astype(jnp.bfloat16)
    mixed = jnp.einsum('hij,jhd->ihd', weights.astype(jnp.float32), values).reshape(HIST, width)
    gated = (mixed * lax.rsqrt(lax.optimization_barrier(jnp.mean(mixed * mixed, -1, keepdims=True)) + 1e-06) * gate).astype(jnp.bfloat16)
    encoded = base + jnp.dot(gated, out_weight, preferred_element_type=jnp.float32)
    active = positions < length
    return jnp.where(active[:, None], encoded, 0.0).astype(jnp.bfloat16)

def cross_attend(query_rows, keys, score_weight):
    count, rows, width = query_rows.shape
    head_dim = width // HEADS
    query_heads = query_rows.astype(jnp.float32).reshape(count, rows, HEADS, head_dim)
    key_heads = keys.astype(jnp.float32).reshape(keys.shape[0], HEADS, head_dim)
    logits = jnp.einsum('nrhd,jhd->nhrj', query_heads, key_heads) / math.sqrt(head_dim)
    weights = (jax.nn.silu(logits) / HIST).astype(jnp.bfloat16)
    attended = jnp.einsum('nhrj,jhd->nrhd', weights.astype(jnp.float32), key_heads).reshape(count, rows, width)
    partial_value = lax.optimization_barrier(jnp.sum(attended * score_weight, -1)).astype(jnp.bfloat16)
    along = lax.optimization_barrier(jnp.sum(key_heads * score_weight.reshape(HEADS, head_dim), -1))
    sigmoid_z = jax.nn.sigmoid(logits)
    silu_slope = sigmoid_z * (1.0 + logits * (1.0 - sigmoid_z))
    slope = (silu_slope * jnp.swapaxes(along, -1, -2)[..., None, :] / (HIST * math.sqrt(head_dim))).astype(jnp.bfloat16)
    direction = jnp.einsum('nhrj,jhd->nrhd', slope.astype(jnp.float32), key_heads).reshape(count, rows, width)
    return (partial_value, direction.astype(jnp.bfloat16))

def reference(history_items, history_events, history_lengths, action_table, mix_weight, out_weight, query_weight, score_weight, self_weight, candidates, block_owner, row_counts, labels):

    def encode_one(packed):
        return encode_user(packed[0], packed[1], packed[2], action_table, mix_weight, out_weight)
    encoded = lax.map(encode_one, (history_items, history_events, history_lengths))
    block_index = jnp.arange(BLOCKS, dtype=jnp.int32)
    user_of_block = (block_owner[:, 0] * N_LOADER + block_index // BLK_DEV % N_LOADER).astype(jnp.int32)
    queries_c = jnp.dot(candidates.reshape(-1, D), query_weight, preferred_element_type=jnp.float32)
    queries_c = queries_c.astype(jnp.bfloat16).reshape(BLOCKS, BLOCK, D)

    def cross_one(packed):
        keys = lax.dynamic_index_in_dim(encoded, packed[1].astype(jnp.int32), 0, keepdims=False)
        partial_value, direction = cross_attend(packed[0][None], keys, score_weight)
        return (partial_value[0], direction[0])
    partial_value, direction = lax.map(cross_one, (queries_c, user_of_block))
    active = jnp.arange(BLOCK, dtype=jnp.int32)[None, :] < row_counts[:, None]
    own_term = lax.optimization_barrier(jnp.sum(candidates.astype(jnp.float32) * self_weight, -1))
    scores = jnp.where(active, partial_value.astype(jnp.float32) + own_term, 0.0)
    error = jnp.where(active, jax.nn.sigmoid(scores) - labels, 0.0)
    query_slope = (error[..., None] * direction.astype(jnp.float32)).astype(jnp.bfloat16)
    flat_slope = query_slope.reshape(-1, D)
    back = jnp.dot(flat_slope, query_weight.T, preferred_element_type=jnp.float32).reshape(BLOCKS, BLOCK, D)
    row_grads = (error[..., None] * self_weight + back).astype(jnp.bfloat16)
    query_grad = jnp.dot(candidates.reshape(-1, D).T, flat_slope, preferred_element_type=jnp.float32)
    return (scores, row_grads, query_grad)
```

```python
import functools
import math

import jax
import jax.numpy as jnp
from jax import lax
from jax.experimental import pallas as pl
from jax.experimental.pallas import tpu as pltpu
from jax.sharding import PartitionSpec as P

HEADS = 8
HIST = 128
LANES = 128
BF = jnp.bfloat16
F32 = jnp.float32
VMEM_BYTES = 56 * 1024 * 1024


def sigmoid(v):
    return 0.5 * jnp.tanh(0.5 * v) + 0.5


def dot(a, b):
    return jnp.dot(a, b, preferred_element_type=F32)


def dot_t(a, b):
    return lax.dot_general(a, b, (((1,), (1,)), ((), ())), preferred_element_type=F32)


def split3(v):
    high = v.astype(BF)
    rest = v - high.astype(F32)
    middle = rest.astype(BF)
    low = (rest - middle.astype(F32)).astype(BF)
    return high, middle, low


def prepare_kernel(owner, packed, table, base, normed, mask):
    width = base.shape[1]
    actions = table.shape[0]
    rows = packed[0]
    tail = rows[:, width:].astype(F32)
    lane = lax.broadcasted_iota(jnp.int32, (HIST, actions), 1).astype(F32)
    onehot = jnp.where(tail[:, :actions] == lane, 1.0, 0.0).astype(BF)
    value = rows[:, :width].astype(F32)
    high, middle, low = split3(table[...])
    value = value + ((dot(onehot, low) + dot(onehot, middle)) + dot(onehot, high))
    scale = lax.rsqrt(jnp.mean(value * value, -1, keepdims=True) + 1e-06)
    base[...] = value
    normed[...] = (value * scale).astype(BF)
    position = lax.broadcasted_iota(jnp.int32, (HIST, LANES), 0).astype(F32)
    mask[...] = jnp.where(position < tail[:, LANES - 1 :], 1.0, 0.0)


def prepare(owner, packed, table):
    nblocks = owner.shape[0]
    width = table.shape[1]
    total = nblocks * HIST
    return pl.pallas_call(
        prepare_kernel,
        grid_spec=pltpu.PrefetchScalarGridSpec(
            num_scalar_prefetch=1,
            grid=(nblocks,),
            in_specs=[
                pl.BlockSpec((1, HIST, packed.shape[2]), lambda b, o: (o[b], 0, 0)),
                pl.BlockSpec(table.shape, lambda b, o: (0, 0)),
            ],
            out_specs=[
                pl.BlockSpec((HIST, width), lambda b, o: (b, 0)),
                pl.BlockSpec((HIST, width), lambda b, o: (b, 0)),
                pl.BlockSpec((HIST, LANES), lambda b, o: (b, 0)),
            ],
        ),
        out_shape=[
            jax.ShapeDtypeStruct((total, width), F32),
            jax.ShapeDtypeStruct((total, width), BF),
            jax.ShapeDtypeStruct((total, LANES), F32),
        ],
        compiler_params=pltpu.CompilerParams(vmem_limit_bytes=VMEM_BYTES),
        name="prepare",
    )(owner, packed, table)


def encode_kernel(normed, base, mask, wg, wv, wq, wk, wo, encoded, gate_s, mixed_s, ssq_s, gated_s):
    head = pl.program_id(0)
    total, width = normed.shape
    weights = jnp.concatenate([wg[...], wv[...], wq[...], wk[...]], axis=1)
    projected = dot(normed[...], weights)
    projected = projected * sigmoid(projected)
    gate_s[head] = projected[:, :LANES]
    values = projected[:, LANES : 2 * LANES].astype(BF)
    queries = projected[:, 2 * LANES : 3 * LANES].astype(BF)
    keys = projected[:, 3 * LANES :].astype(BF)
    row = lax.broadcasted_iota(jnp.int32, (HIST, HIST), 0)
    column = lax.broadcasted_iota(jnp.int32, (HIST, HIST), 1)
    causal = column <= row

    @pl.when(head == 0)
    def _():
        ssq_s[...] = jnp.zeros_like(ssq_s)

    for u in range(total // HIST):
        part = slice(u * HIST, (u + 1) * HIST)
        logits = dot_t(queries[part], keys[part]) * (1.0 / math.sqrt(LANES))
        weight = jnp.where(causal, logits * sigmoid(logits) * (1.0 / HIST), 0.0).astype(BF)
        mixed = dot(weight, values[part])
        mixed_s[head, part] = mixed
        ssq_s[part] += mixed * mixed

    @pl.when(head == pl.num_programs(0) - 1)
    def _():
        scale = lax.rsqrt(jnp.sum(ssq_s[...], -1, keepdims=True) * (1.0 / width) + 1e-06)
        for h in range(HEADS):
            gated_s[:, h * LANES : (h + 1) * LANES] = (mixed_s[h] * scale * gate_s[h]).astype(BF)
        active = mask[:, :1] > 0.0
        step = 256
        for n in range(width // step):
            cols = slice(n * step, (n + 1) * step)
            value = base[:, cols] + dot(gated_s[...], wo[:, cols])
            encoded[:, cols] = jnp.where(active, value, 0.0).astype(BF)


def encode(normed, base, mask, weights):
    total, width = normed.shape
    whole = lambda h: (0, 0)
    column = lambda group: pl.BlockSpec((width, LANES), lambda h: (0, group * HEADS + h))
    return pl.pallas_call(
        encode_kernel,
        grid=(HEADS,),
        in_specs=[
            pl.BlockSpec((total, width), whole),
            pl.BlockSpec((total, width), whole),
            pl.BlockSpec((total, LANES), whole),
            column(0),
            column(1),
            column(2),
            column(3),
            pl.BlockSpec((width, width), lambda h: (0, 4)),
        ],
        out_specs=pl.BlockSpec((total, width), whole),
        out_shape=jax.ShapeDtypeStruct((total, width), BF),
        scratch_shapes=[
            pltpu.VMEM((HEADS, total, LANES), F32),
            pltpu.VMEM((HEADS, total, LANES), F32),
            pltpu.VMEM((total, LANES), F32),
            pltpu.VMEM((total, width), BF),
        ],
        compiler_params=pltpu.CompilerParams(vmem_limit_bytes=VMEM_BYTES),
        name="encode",
    )(normed, base, mask, weights, weights, weights, weights, weights)


def cross_kernel(
    counts,
    core,
    queries,
    encoded,
    score_weight,
    own,
    labels,
    cand_t,
    scores,
    error,
    slopes,
    mine,
    other,
    slope_s,
    dir_s,
):
    block = pl.program_id(0)
    width = queries.shape[1]
    lane = lax.broadcasted_iota(jnp.int32, (HEADS, width), 1) // LANES
    head_row = lax.broadcasted_iota(jnp.int32, (HEADS, width), 0)
    spread = jnp.where(lane == head_row, score_weight[...], 0.0)
    high, middle, low = split3(spread)
    keys = encoded[...]
    along = (dot_t(low, keys) + dot_t(middle, keys)) + dot_t(high, keys)
    along_scaled = along * (1.0 / (HIST * math.sqrt(LANES)))
    total = jnp.zeros((queries.shape[0], HIST), F32)
    for h in range(HEADS):
        cols = slice(h * LANES, (h + 1) * LANES)
        key_head = keys[:, cols]
        logits = dot_t(queries[:, cols], key_head) * (1.0 / math.sqrt(LANES))
        gate = sigmoid(logits)
        product = logits * gate
        weight = (product * (1.0 / HIST)).astype(BF).astype(F32)
        total = total + weight * along[h : h + 1]
        slope = (gate + product * (1.0 - gate)) * along_scaled[h : h + 1]
        dir_s[:, cols] = dot(slope.astype(BF), key_head).astype(BF)
    partial = jnp.sum(total, -1, keepdims=True).astype(BF).astype(F32)
    partial_row = jnp.broadcast_to(partial, (HIST, HIST)).T[:1]
    active = lax.broadcasted_iota(jnp.int32, (1, HIST), 1) < counts[block]
    score = jnp.where(active, partial_row + own[0], 0.0)
    err = jnp.where(active, sigmoid(score) - labels[0], 0.0)
    scores[0] = score
    error[0] = err
    err_rows = jnp.broadcast_to(err, (HIST, HIST)).T
    for h in range(HEADS):
        cols = slice(h * LANES, (h + 1) * LANES)
        slope = (err_rows * dir_s[:, cols].astype(F32)).astype(BF)
        slopes[:, cols] = slope
        slope_s[block, :, cols] = slope

    @pl.when(block == pl.num_programs(0) - 1)
    def _():
        step = 256
        pairs, piece = mine.shape[0], mine.shape[1]
        first = core[0] == 0
        for n in range(width // step):
            cols = slice(n * step, (n + 1) * step)
            right = slope_s[:, :, cols].reshape(-1, step)
            grad = dot(cand_t[...], right)
            for p in range(pairs):
                one = grad[2 * p * piece : (2 * p + 1) * piece]
                two = grad[(2 * p + 1) * piece : (2 * p + 2) * piece]
                mine[p, :, cols] = jnp.where(first, one, two)
                other[p, :, cols] = jnp.where(first, two, one).astype(BF)


def cross(counts, core, queries, encoded, score_weight, own, labels, cand_t, pairs):
    nblocks = counts.shape[0]
    total, width = queries.shape
    rows = total // nblocks
    piece = width // (2 * pairs)
    block_rows = pl.BlockSpec((rows, width), lambda b, n, c: (b, 0))
    row = pl.BlockSpec((1, 1, rows), lambda b, n, c: (b, 0, 0))
    whole3 = lambda b, n, c: (0, 0, 0)
    return pl.pallas_call(
        cross_kernel,
        grid_spec=pltpu.PrefetchScalarGridSpec(
            num_scalar_prefetch=2,
            grid=(nblocks,),
            in_specs=[
                block_rows,
                block_rows,
                pl.BlockSpec((1, width), lambda b, n, c: (0, 0)),
                row,
                row,
                pl.BlockSpec((width, total), lambda b, n, c: (0, 0)),
            ],
            out_specs=[
                row,
                row,
                block_rows,
                pl.BlockSpec((pairs, piece, width), whole3),
                pl.BlockSpec((pairs, piece, width), whole3),
            ],
            scratch_shapes=[
                pltpu.VMEM((nblocks, rows, width), BF),
                pltpu.VMEM((rows, width), BF),
            ],
        ),
        out_shape=[
            jax.ShapeDtypeStruct((nblocks, 1, rows), F32),
            jax.ShapeDtypeStruct((nblocks, 1, rows), F32),
            jax.ShapeDtypeStruct((total, width), BF),
            jax.ShapeDtypeStruct((pairs, piece, width), F32),
            jax.ShapeDtypeStruct((pairs, piece, width), BF),
        ],
        compiler_params=pltpu.CompilerParams(vmem_limit_bytes=VMEM_BYTES),
        name="cross",
    )(counts, core, queries, encoded, score_weight, own, labels, cand_t)


def fold_kernel(mine, arrived, out):
    pairs, piece, width = mine.shape
    tall, wide = out.shape[2], out.shape[3]
    down, right = piece // tall, width // wide
    for a in range(down):
        for b in range(right):
            rows, cols = slice(a * tall, (a + 1) * tall), slice(b * wide, (b + 1) * wide)
            value = mine[:, rows, cols] + arrived[:, rows, cols].astype(F32)
            out[a * right + b] = value.astype(BF)


def fold(mine, arrived, users):
    pairs, piece, width = mine.shape
    right = math.isqrt(users)
    down = users // right
    return pl.pallas_call(
        fold_kernel,
        out_shape=jax.ShapeDtypeStruct((users, pairs, piece // down, width // right), BF),
        compiler_params=pltpu.CompilerParams(vmem_limit_bytes=VMEM_BYTES),
        name="fold",
    )(mine, arrived)


def body(
    history_items,
    history_events,
    history_lengths,
    action_table,
    mix_weight,
    out_weight,
    query_weight,
    score_weight,
    self_weight,
    candidates,
    block_owner,
    row_counts,
    labels,
):
    users = lax.axis_size("user")
    loaders = lax.axis_size("loader")
    pairs = loaders // 2
    nblocks, rows, width = candidates.shape

    shard = jnp.concatenate([mix_weight, out_weight], axis=1)
    weights = lax.all_gather(shard, "loader", axis=0, tiled=True)
    actions = action_table.shape[0]
    packed = jnp.concatenate(
        [
            history_items[0],
            jnp.broadcast_to(history_events[0][:, None].astype(BF), (HIST, actions)),
            jnp.broadcast_to(history_lengths[0].astype(BF), (HIST, LANES - actions)),
        ],
        axis=1,
    )
    packed = lax.all_to_all(
        jnp.broadcast_to(packed[None], (users,) + packed.shape), "user", 0, 0, tiled=True
    )

    flat = candidates.reshape(-1, width)
    queries = jnp.dot(flat, query_weight, preferred_element_type=F32).astype(BF)
    cand_t = flat.T
    own = jnp.sum(candidates.astype(F32) * self_weight, -1)

    owner = block_owner[:, 0]
    base, normed, mask = prepare(owner, packed, action_table)
    encoded = encode(normed, base, mask, weights)
    core = lax.rem(lax.axis_index("loader"), 2)[None].astype(jnp.int32)
    scores, error, slopes, mine, other = cross(
        row_counts,
        core,
        queries,
        encoded,
        score_weight[None],
        own[:, None],
        labels[:, None],
        cand_t,
        pairs,
    )

    arrived = lax.ppermute(other, "loader", [(i, i ^ 1) for i in range(loaders)])
    pieces = lax.all_to_all(fold(mine, arrived, users), "user", 0, 0, tiled=True)
    pieces = jnp.sum(pieces.astype(F32), 0).astype(BF)
    groups = [[c + 2 * i for i in range(pairs)] for c in range(2)]
    pieces = lax.all_to_all(pieces, "loader", 0, 0, axis_index_groups=groups, tiled=True)
    piece = jnp.sum(pieces.astype(F32), 0).astype(BF)
    pieces = lax.all_to_all(
        jnp.broadcast_to(piece[None], (users,) + piece.shape), "user", 0, 0, tiled=True
    )
    right = math.isqrt(users)
    tall, wide = piece.shape
    query_grad = pieces.reshape(users // right, right, tall, wide).transpose(0, 2, 1, 3)
    query_grad = query_grad.reshape(users // right * tall, right * wide).astype(F32)

    back = lax.dot_general(slopes, query_weight, (((1,), (1,)), ((), ())), preferred_element_type=F32)
    row_grads = (error.reshape(-1)[:, None] * self_weight + back).astype(BF)
    return (scores[:, 0], row_grads.reshape(nblocks, rows, width), query_grad)


def solution(mesh):
    placed = (
        P(("user", "loader"), None, None),
        P(("user", "loader"), None),
        P(("user", "loader")),
        P(),
        P("loader", None),
        P("loader", None),
        P(),
        P(),
        P(),
        P(("user", "loader"), None, None),
        P(("user", "loader"), None),
        P(("user", "loader")),
        P(("user", "loader"), None),
    )
    return jax.shard_map(
        body,
        mesh=mesh,
        in_specs=placed,
        out_specs=(
            P(("user", "loader"), None),
            P(("user", "loader"), None, None),
            P("loader", None),
        ),
        check_vma=False,
    )
```

```python
import functools
import math

import jax
import jax.numpy as jnp
from jax import lax
from jax.experimental import pallas as pl
from jax.experimental.pallas import tpu as pltpu
from jax.sharding import PartitionSpec as P

HEADS = 8
HIST = 128
LANES = 128
BF = jnp.bfloat16
F32 = jnp.float32
VMEM_BYTES = 56 * 1024 * 1024


def sigmoid(v):
    return 0.5 * jnp.tanh(0.5 * v) + 0.5


def dot(a, b):
    return jnp.dot(a, b, preferred_element_type=F32)


def dot_t(a, b):
    return lax.dot_general(a, b, (((1,), (1,)), ((), ())), preferred_element_type=F32)


def split3(v):
    high = v.astype(BF)
    rest = v - high.astype(F32)
    middle = rest.astype(BF)
    low = (rest - middle.astype(F32)).astype(BF)
    return high, middle, low


def prepare_kernel(place_a, place_b, half_a, half_b, table, base, normed, mask):
    width = base.shape[1]
    actions = table.shape[0]
    rows = jnp.concatenate([half_a[0], half_b[0]], axis=0)
    tail = rows[:, width:].astype(F32)
    lane = lax.broadcasted_iota(jnp.int32, (HIST, actions), 1).astype(F32)
    onehot = jnp.where(tail[:, :actions] == lane, 1.0, 0.0).astype(BF)
    value = rows[:, :width].astype(F32)
    high, middle, low = split3(table[...])
    value = value + ((dot(onehot, low) + dot(onehot, middle)) + dot(onehot, high))
    scale = lax.rsqrt(jnp.mean(value * value, -1, keepdims=True) + 1e-06)
    base[...] = value
    normed[...] = (value * scale).astype(BF)
    position = lax.broadcasted_iota(jnp.int32, (HIST, LANES), 0).astype(F32)
    mask[...] = jnp.where(position < tail[:, LANES - 1 :], 1.0, 0.0)


def prepare(place_a, place_b, half_a, half_b, table):
    nblocks = place_a.shape[0]
    width = table.shape[1]
    total = nblocks * HIST
    return pl.pallas_call(
        prepare_kernel,
        grid_spec=pltpu.PrefetchScalarGridSpec(
            num_scalar_prefetch=2,
            grid=(nblocks,),
            in_specs=[
                pl.BlockSpec((1,) + half_a.shape[1:], lambda b, p, q: (p[b], 0, 0)),
                pl.BlockSpec((1,) + half_b.shape[1:], lambda b, p, q: (q[b], 0, 0)),
                pl.BlockSpec(table.shape, lambda b, p, q: (0, 0)),
            ],
            out_specs=[
                pl.BlockSpec((HIST, width), lambda b, p, q: (b, 0)),
                pl.BlockSpec((HIST, width), lambda b, p, q: (b, 0)),
                pl.BlockSpec((HIST, LANES), lambda b, p, q: (b, 0)),
            ],
        ),
        out_shape=[
            jax.ShapeDtypeStruct((total, width), F32),
            jax.ShapeDtypeStruct((total, width), BF),
            jax.ShapeDtypeStruct((total, LANES), F32),
        ],
        compiler_params=pltpu.CompilerParams(vmem_limit_bytes=VMEM_BYTES),
        name="prepare",
    )(place_a, place_b, half_a, half_b, table)


def encode_kernel(normed, base, mask, wg, wv, wq, wk, wo, encoded, gate_s, mixed_s, ssq_s, gated_s):
    head = pl.program_id(0)
    total, width = normed.shape
    weights = jnp.concatenate([wg[...], wv[...], wq[...], wk[...]], axis=1)
    projected = dot(normed[...], weights)
    projected = projected * sigmoid(projected)
    gate_s[head] = projected[:, :LANES]
    values = projected[:, LANES : 2 * LANES].astype(BF)
    queries = projected[:, 2 * LANES : 3 * LANES].astype(BF)
    keys = projected[:, 3 * LANES :].astype(BF)
    row = lax.broadcasted_iota(jnp.int32, (HIST, HIST), 0)
    column = lax.broadcasted_iota(jnp.int32, (HIST, HIST), 1)
    causal = column <= row

    @pl.when(head == 0)
    def _():
        ssq_s[...] = jnp.zeros_like(ssq_s)

    for u in range(total // HIST):
        part = slice(u * HIST, (u + 1) * HIST)
        logits = dot_t(queries[part], keys[part]) * (1.0 / math.sqrt(LANES))
        weight = jnp.where(causal, logits * sigmoid(logits) * (1.0 / HIST), 0.0).astype(BF)
        mixed = dot(weight, values[part])
        mixed_s[head, part] = mixed
        ssq_s[part] += mixed * mixed

    @pl.when(head == pl.num_programs(0) - 1)
    def _():
        scale = lax.rsqrt(jnp.sum(ssq_s[...], -1, keepdims=True) * (1.0 / width) + 1e-06)
        for h in range(HEADS):
            gated_s[:, h * LANES : (h + 1) * LANES] = (mixed_s[h] * scale * gate_s[h]).astype(BF)
        active = mask[:, :1] > 0.0
        step = 256
        for n in range(width // step):
            cols = slice(n * step, (n + 1) * step)
            value = base[:, cols] + dot(gated_s[...], wo[:, cols])
            encoded[:, cols] = jnp.where(active, value, 0.0).astype(BF)


def encode(normed, base, mask, weights):
    total, width = normed.shape
    whole = lambda h: (0, 0)
    column = lambda group: pl.BlockSpec((width, LANES), lambda h: (0, group * HEADS + h))
    return pl.pallas_call(
        encode_kernel,
        grid=(HEADS,),
        in_specs=[
            pl.BlockSpec((total, width), whole),
            pl.BlockSpec((total, width), whole),
            pl.BlockSpec((total, LANES), whole),
            column(0),
            column(1),
            column(2),
            column(3),
            pl.BlockSpec((width, width), lambda h: (0, 4)),
        ],
        out_specs=pl.BlockSpec((total, width), whole),
        out_shape=jax.ShapeDtypeStruct((total, width), BF),
        scratch_shapes=[
            pltpu.VMEM((HEADS, total, LANES), F32),
            pltpu.VMEM((HEADS, total, LANES), F32),
            pltpu.VMEM((total, LANES), F32),
            pltpu.VMEM((total, width), BF),
        ],
        compiler_params=pltpu.CompilerParams(vmem_limit_bytes=VMEM_BYTES),
        name="encode",
    )(normed, base, mask, weights, weights, weights, weights, weights)


def cross_kernel(
    counts,
    core,
    queries,
    encoded,
    score_weight,
    own,
    labels,
    cand_t,
    scores,
    error,
    slopes,
    mine,
    other,
    slope_s,
    dir_s,
):
    block = pl.program_id(0)
    width = queries.shape[1]
    lane = lax.broadcasted_iota(jnp.int32, (HEADS, width), 1) // LANES
    head_row = lax.broadcasted_iota(jnp.int32, (HEADS, width), 0)
    spread = jnp.where(lane == head_row, score_weight[...], 0.0)
    high, middle, low = split3(spread)
    keys = encoded[...]
    along = (dot_t(low, keys) + dot_t(middle, keys)) + dot_t(high, keys)
    along_scaled = along * (1.0 / (HIST * math.sqrt(LANES)))
    total = jnp.zeros((queries.shape[0], HIST), F32)
    for h in range(HEADS):
        cols = slice(h * LANES, (h + 1) * LANES)
        key_head = keys[:, cols]
        logits = dot_t(queries[:, cols], key_head) * (1.0 / math.sqrt(LANES))
        gate = sigmoid(logits)
        product = logits * gate
        weight = (product * (1.0 / HIST)).astype(BF).astype(F32)
        total = total + weight * along[h : h + 1]
        slope = (gate + product * (1.0 - gate)) * along_scaled[h : h + 1]
        dir_s[:, cols] = dot(slope.astype(BF), key_head).astype(BF)
    partial = jnp.sum(total, -1, keepdims=True).astype(BF).astype(F32)
    partial_row = jnp.broadcast_to(partial, (HIST, HIST)).T[:1]
    active = lax.broadcasted_iota(jnp.int32, (1, HIST), 1) < counts[block]
    score = jnp.where(active, partial_row + own[0], 0.0)
    err = jnp.where(active, sigmoid(score) - labels[0], 0.0)
    scores[0] = score
    error[0] = err
    err_rows = jnp.broadcast_to(err, (HIST, HIST)).T
    for h in range(HEADS):
        cols = slice(h * LANES, (h + 1) * LANES)
        slope = (err_rows * dir_s[:, cols].astype(F32)).astype(BF)
        slopes[:, cols] = slope
        slope_s[block, :, cols] = slope

    @pl.when(block == pl.num_programs(0) - 1)
    def _():
        step = 256
        pairs, piece = mine.shape[0], mine.shape[1]
        first = core[0] == 0
        for n in range(width // step):
            cols = slice(n * step, (n + 1) * step)
            right = slope_s[:, :, cols].reshape(-1, step)
            grad = dot(cand_t[...], right)
            for p in range(pairs):
                one = grad[2 * p * piece : (2 * p + 1) * piece]
                two = grad[(2 * p + 1) * piece : (2 * p + 2) * piece]
                mine[p, :, cols] = jnp.where(first, one, two)
                other[p, :, cols] = jnp.where(first, two, one).astype(BF)


def cross(counts, core, queries, encoded, score_weight, own, labels, cand_t, pairs):
    nblocks = counts.shape[0]
    total, width = queries.shape
    rows = total // nblocks
    piece = width // (2 * pairs)
    block_rows = pl.BlockSpec((rows, width), lambda b, n, c: (b, 0))
    row = pl.BlockSpec((1, 1, rows), lambda b, n, c: (b, 0, 0))
    whole3 = lambda b, n, c: (0, 0, 0)
    return pl.pallas_call(
        cross_kernel,
        grid_spec=pltpu.PrefetchScalarGridSpec(
            num_scalar_prefetch=2,
            grid=(nblocks,),
            in_specs=[
                block_rows,
                block_rows,
                pl.BlockSpec((1, width), lambda b, n, c: (0, 0)),
                row,
                row,
                pl.BlockSpec((width, total), lambda b, n, c: (0, 0)),
            ],
            out_specs=[
                row,
                row,
                block_rows,
                pl.BlockSpec((pairs, piece, width), whole3),
                pl.BlockSpec((pairs, piece, width), whole3),
            ],
            scratch_shapes=[
                pltpu.VMEM((nblocks, rows, width), BF),
                pltpu.VMEM((rows, width), BF),
            ],
        ),
        out_shape=[
            jax.ShapeDtypeStruct((nblocks, 1, rows), F32),
            jax.ShapeDtypeStruct((nblocks, 1, rows), F32),
            jax.ShapeDtypeStruct((total, width), BF),
            jax.ShapeDtypeStruct((pairs, piece, width), F32),
            jax.ShapeDtypeStruct((pairs, piece, width), BF),
        ],
        compiler_params=pltpu.CompilerParams(vmem_limit_bytes=VMEM_BYTES),
        name="cross",
    )(counts, core, queries, encoded, score_weight, own, labels, cand_t)


def fold_kernel(mine, arrived, out):
    pairs, piece, width = mine.shape
    tall, wide = out.shape[2], out.shape[3]
    down, right = piece // tall, width // wide
    for a in range(down):
        for b in range(right):
            rows, cols = slice(a * tall, (a + 1) * tall), slice(b * wide, (b + 1) * wide)
            value = mine[:, rows, cols] + arrived[:, rows, cols].astype(F32)
            out[a * right + b] = value.astype(BF)


def fold(mine, arrived, users):
    pairs, piece, width = mine.shape
    right = math.isqrt(users)
    down = users // right
    return pl.pallas_call(
        fold_kernel,
        out_shape=jax.ShapeDtypeStruct((users, pairs, piece // down, width // right), BF),
        compiler_params=pltpu.CompilerParams(vmem_limit_bytes=VMEM_BYTES),
        name="fold",
    )(mine, arrived)


def shift(array, side, dx, dy):
    moves = []
    for x in range(side):
        for y in range(side):
            moves.append(((x + dx) % side * side + (y + dy) % side, x * side + y))
    return lax.ppermute(array, "user", moves)


def ring(array, side, along_x):
    move = lambda a, d: shift(a, side, d if along_x else 0, 0 if along_x else d)
    half = array.shape[1] // 2
    after = move(array, 1)
    before = move(array, -1)
    first = move(after[:, :half], 1)
    second = move(before[:, half:], -1)
    return jnp.stack([array, after, jnp.concatenate([first, second], axis=1), before])


def body(
    history_items,
    history_events,
    history_lengths,
    action_table,
    mix_weight,
    out_weight,
    query_weight,
    score_weight,
    self_weight,
    candidates,
    block_owner,
    row_counts,
    labels,
):
    users = lax.axis_size("user")
    loaders = lax.axis_size("loader")
    pairs = loaders // 2
    nblocks, rows, width = candidates.shape

    shard = jnp.concatenate([mix_weight, out_weight], axis=1)
    weights = lax.all_gather(shard, "loader", axis=0, tiled=True)
    actions = action_table.shape[0]
    packed = jnp.concatenate(
        [
            history_items[0],
            jnp.broadcast_to(history_events[0][:, None].astype(BF), (HIST, actions)),
            jnp.broadcast_to(history_lengths[0].astype(BF), (HIST, LANES - actions)),
        ],
        axis=1,
    )
    side = math.isqrt(users)
    half = HIST // 2
    half_a = ring(packed[None, :half], side, True).reshape(side, half, -1)
    half_b = ring(packed[None, half:], side, False).reshape(side, half, -1)
    half_a = ring(half_a, side, False).reshape(users, half, -1)
    half_b = ring(half_b, side, True).reshape(users, half, -1)

    flat = candidates.reshape(-1, width)
    queries = jnp.dot(flat, query_weight, preferred_element_type=F32).astype(BF)
    cand_t = flat.T
    own = jnp.sum(candidates.astype(F32) * self_weight, -1)

    owner = block_owner[:, 0]
    here = lax.axis_index("user").astype(jnp.int32)
    far_x = lax.rem(owner // side - here // side + side, side)
    far_y = lax.rem(lax.rem(owner, side) - lax.rem(here, side) + side, side)
    base, normed, mask = prepare(
        far_y * side + far_x, far_x * side + far_y, half_a, half_b, action_table
    )
    encoded = encode(normed, base, mask, weights)
    core = lax.rem(lax.axis_index("loader"), 2)[None].astype(jnp.int32)
    scores, error, slopes, mine, other = cross(
        row_counts,
        core,
        queries,
        encoded,
        score_weight[None],
        own[:, None],
        labels[:, None],
        cand_t,
        pairs,
    )

    arrived = lax.ppermute(other, "loader", [(i, i ^ 1) for i in range(loaders)])
    pieces = lax.all_to_all(fold(mine, arrived, users), "user", 0, 0, tiled=True)
    pieces = jnp.sum(pieces.astype(F32), 0).astype(BF)
    groups = [[c + 2 * i for i in range(pairs)] for c in range(2)]
    pieces = lax.all_to_all(pieces, "loader", 0, 0, axis_index_groups=groups, tiled=True)
    piece = jnp.sum(pieces.astype(F32), 0).astype(BF)
    pieces = lax.all_to_all(
        jnp.broadcast_to(piece[None], (users,) + piece.shape), "user", 0, 0, tiled=True
    )
    right = math.isqrt(users)
    tall, wide = piece.shape
    query_grad = pieces.reshape(users // right, right, tall, wide).transpose(0, 2, 1, 3)
    query_grad = query_grad.reshape(users // right * tall, right * wide).astype(F32)

    back = lax.dot_general(slopes, query_weight, (((1,), (1,)), ((), ())), preferred_element_type=F32)
    row_grads = (error.reshape(-1)[:, None] * self_weight + back).astype(BF)
    return (scores[:, 0], row_grads.reshape(nblocks, rows, width), query_grad)


def solution(mesh):
    placed = (
        P(("user", "loader"), None, None),
        P(("user", "loader"), None),
        P(("user", "loader")),
        P(),
        P("loader", None),
        P("loader", None),
        P(),
        P(),
        P(),
        P(("user", "loader"), None, None),
        P(("user", "loader"), None),
        P(("user", "loader")),
        P(("user", "loader"), None),
    )
    return jax.shard_map(
        body,
        mesh=mesh,
        in_specs=placed,
        out_specs=(
            P(("user", "loader"), None),
            P(("user", "loader"), None, None),
            P("loader", None),
        ),
        check_vma=False,
    )
```

```python
import functools
import math

import jax
import jax.numpy as jnp
from jax import lax
from jax.experimental import pallas as pl
from jax.experimental.pallas import tpu as pltpu
from jax.sharding import PartitionSpec as P

HEADS = 8
HIST = 128
LANES = 128
BF = jnp.bfloat16
F32 = jnp.float32
VMEM_BYTES = 56 * 1024 * 1024


def sigmoid(v):
    return 0.5 * jnp.tanh(0.5 * v) + 0.5


def dot(a, b):
    return jnp.dot(a, b, preferred_element_type=F32)


def dot_t(a, b):
    return lax.dot_general(a, b, (((1,), (1,)), ((), ())), preferred_element_type=F32)


def split3(v):
    high = v.astype(BF)
    rest = v - high.astype(F32)
    middle = rest.astype(BF)
    low = (rest - middle.astype(F32)).astype(BF)
    return high, middle, low


def prepare_kernel(nblocks, place_a, place_b, *refs):
    count = (len(refs) - 6) // 2
    halves = ((place_a, refs[:count]), (place_b, refs[count : 2 * count]))
    table, base, normed, mask, rows_s, sems = refs[2 * count :]
    block = pl.program_id(0)
    width = base.shape[1]
    actions = table.shape[0]
    half = HIST // 2

    def fetch(which, b, source):
        return pltpu.make_async_copy(
            source, rows_s.at[b, pl.ds(which * half, half)], sems.at[which, b]
        )

    @pl.when(block == 0)
    def _():
        for b in range(nblocks):
            for which, (place, arrays) in enumerate(halves):
                for k, array in enumerate(arrays):

                    @pl.when(place[b] // 2 == k)
                    def _():
                        fetch(which, b, array.at[lax.rem(place[b], 2)]).start()

    for which, (place, arrays) in enumerate(halves):
        fetch(which, block, arrays[0].at[0]).wait()
    rows = rows_s[block]
    tail = rows[:, width:].astype(F32)
    lane = lax.broadcasted_iota(jnp.int32, (HIST, actions), 1).astype(F32)
    onehot = jnp.where(tail[:, :actions] == lane, 1.0, 0.0).astype(BF)
    value = rows[:, :width].astype(F32)
    high, middle, low = split3(table[...])
    value = value + ((dot(onehot, low) + dot(onehot, middle)) + dot(onehot, high))
    scale = lax.rsqrt(jnp.mean(value * value, -1, keepdims=True) + 1e-06)
    base[...] = value
    normed[...] = (value * scale).astype(BF)
    position = lax.broadcasted_iota(jnp.int32, (HIST, LANES), 0).astype(F32)
    mask[...] = jnp.where(position < tail[:, LANES - 1 :], 1.0, 0.0)


def prepare(place_a, place_b, halves_a, halves_b, table):
    nblocks = place_a.shape[0]
    width = table.shape[1]
    total = nblocks * HIST
    arrays = list(halves_a) + list(halves_b)
    return pl.pallas_call(
        functools.partial(prepare_kernel, nblocks),
        grid_spec=pltpu.PrefetchScalarGridSpec(
            num_scalar_prefetch=2,
            grid=(nblocks,),
            in_specs=[pl.BlockSpec(memory_space=pl.ANY)] * len(arrays)
            + [pl.BlockSpec(table.shape, lambda b, p, q: (0, 0))],
            out_specs=[
                pl.BlockSpec((HIST, width), lambda b, p, q: (b, 0)),
                pl.BlockSpec((HIST, width), lambda b, p, q: (b, 0)),
                pl.BlockSpec((HIST, LANES), lambda b, p, q: (b, 0)),
            ],
            scratch_shapes=[
                pltpu.VMEM((nblocks, HIST, arrays[0].shape[-1]), BF),
                pltpu.SemaphoreType.DMA((2, nblocks)),
            ],
        ),
        out_shape=[
            jax.ShapeDtypeStruct((total, width), F32),
            jax.ShapeDtypeStruct((total, width), BF),
            jax.ShapeDtypeStruct((total, LANES), F32),
        ],
        compiler_params=pltpu.CompilerParams(vmem_limit_bytes=VMEM_BYTES),
        name="prepare",
    )(place_a, place_b, *arrays, table)


def encode_kernel(
    place,
    normed,
    wg,
    wv,
    wq,
    wk,
    mask,
    base,
    out_own,
    out_other,
    encoded,
    gate_s,
    mixed_s,
    even_s,
    odd_s,
    gated_s,
    base_s,
    wo_s,
    sems,
):
    step = pl.program_id(0)
    last = pl.num_programs(0) - 1
    total, width = normed.shape
    base_copy = pltpu.make_async_copy(base, base_s, sems.at[0])
    pairs, piece = out_own.shape[0], out_own.shape[1]
    wo_copies = []
    for d in range(pairs):
        first = 2 * lax.rem(place[0] + d, pairs)
        for k, (source, core) in enumerate(((out_own, place[1]), (out_other, 1 - place[1]))):
            start = pl.multiple_of((first + core) * piece, piece)
            wo_copies.append(
                pltpu.make_async_copy(
                    source.at[d], wo_s.at[pl.ds(start, piece)], sems.at[1 + 2 * d + k]
                )
            )
    row = lax.broadcasted_iota(jnp.int32, (HIST, HIST), 0)
    column = lax.broadcasted_iota(jnp.int32, (HIST, HIST), 1)
    causal = column <= row

    def project(which, head, store):
        cols = slice(which * LANES, (which + 1) * LANES)
        columns = jnp.concatenate([wg[:, cols], wv[:, cols], wq[:, cols], wk[:, cols]], axis=1)
        projected = dot(normed[...], columns)
        projected = projected * sigmoid(projected)
        gate_s[head] = projected[:, :LANES]
        store[...] = projected[:, LANES:].astype(BF)

    def attend(head, store):
        for u in range(total // HIST):
            part = slice(u * HIST, (u + 1) * HIST)
            queries = store[part, LANES : 2 * LANES]
            keys = store[part, 2 * LANES :]
            logits = dot_t(queries, keys) * (1.0 / math.sqrt(LANES))
            weight = jnp.where(causal, logits * sigmoid(logits) * (1.0 / HIST), 0.0).astype(BF)
            mixed_s[head, part] = dot(weight, store[part, :LANES])

    @pl.when(step == 0)
    def _():
        base_copy.start()
        for copy in wo_copies:
            copy.start()
        project(0, 0, even_s)
        attend(0, even_s)
        project(1, 1, odd_s)

    @pl.when(step > 0)
    def _():
        attend(2 * step - 1, odd_s)
        project(0, 2 * step, even_s)
        attend(2 * step, even_s)
        project(1, 2 * step + 1, odd_s)

    @pl.when(step == last)
    def _():
        attend(HEADS - 1, odd_s)
        square = mixed_s[0] * mixed_s[0]
        for h in range(1, HEADS):
            square = square + mixed_s[h] * mixed_s[h]
        scale = lax.rsqrt(jnp.sum(square, -1, keepdims=True) * (1.0 / width) + 1e-06)
        for h in range(HEADS):
            gated_s[:, h * LANES : (h + 1) * LANES] = (mixed_s[h] * scale * gate_s[h]).astype(BF)
        active = mask[:, :1] > 0.0
        base_copy.wait()
        for copy in wo_copies:
            copy.wait()
        size = 256
        for n in range(width // size):
            cols = slice(n * size, (n + 1) * size)
            value = base_s[:, cols] + dot(gated_s[...], wo_s[:, cols])
            encoded[:, cols] = jnp.where(active, value, 0.0).astype(BF)


def encode(place, normed, base, mask, weights, out_own, out_other):
    total, width = normed.shape
    pairs = out_own.shape[0]
    whole = lambda h, p: (0, 0)
    column = lambda group: pl.BlockSpec(
        (width, 2 * LANES), lambda h, p: (0, group * HEADS // 2 + h)
    )
    anywhere = pl.BlockSpec(memory_space=pl.ANY)
    return pl.pallas_call(
        encode_kernel,
        grid_spec=pltpu.PrefetchScalarGridSpec(
            num_scalar_prefetch=1,
            grid=(HEADS // 2,),
            in_specs=[
                pl.BlockSpec((total, width), whole),
                column(0),
                column(1),
                column(2),
                column(3),
                pl.BlockSpec((total, LANES), whole),
                anywhere,
                anywhere,
                anywhere,
            ],
            out_specs=pl.BlockSpec((total, width), whole),
            scratch_shapes=[
                pltpu.VMEM((HEADS, total, LANES), F32),
                pltpu.VMEM((HEADS, total, LANES), F32),
                pltpu.VMEM((total, 3 * LANES), BF),
                pltpu.VMEM((total, 3 * LANES), BF),
                pltpu.VMEM((total, width), BF),
                pltpu.VMEM((total, width), F32),
                pltpu.VMEM((width, width), BF),
                pltpu.SemaphoreType.DMA((1 + 2 * pairs,)),
            ],
        ),
        out_shape=jax.ShapeDtypeStruct((total, width), BF),
        compiler_params=pltpu.CompilerParams(vmem_limit_bytes=VMEM_BYTES),
        name="encode",
    )(place, normed, weights, weights, weights, weights, mask, base, out_own, out_other)


GROUP = 2


def cross_kernel(
    counts,
    core,
    queries,
    encoded,
    score_weight,
    own,
    labels,
    cand_t,
    scores,
    error,
    slopes,
    mine,
    other,
    slope_s,
    dir_s,
):
    step = pl.program_id(0)
    width = queries.shape[1]
    lane = lax.broadcasted_iota(jnp.int32, (HEADS, width), 1) // LANES
    head_row = lax.broadcasted_iota(jnp.int32, (HEADS, width), 0)
    spread = jnp.where(lane == head_row, score_weight[...], 0.0)
    high, middle, low = split3(spread)
    parts = [slice(g * HIST, (g + 1) * HIST) for g in range(GROUP)]
    along, along_scaled, totals = [], [], []
    for part in parts:
        keys = encoded[part]
        value = (dot_t(low, keys) + dot_t(middle, keys)) + dot_t(high, keys)
        along.append(value)
        along_scaled.append(value * (1.0 / (HIST * math.sqrt(LANES))))
        totals.append(jnp.zeros((HIST, HIST), F32))
    for h in range(HEADS):
        cols = slice(h * LANES, (h + 1) * LANES)
        for g, part in enumerate(parts):
            key_head = encoded[part, cols]
            logits = dot_t(queries[part, cols], key_head) * (1.0 / math.sqrt(LANES))
            gate = sigmoid(logits)
            product = logits * gate
            weight = (product * (1.0 / HIST)).astype(BF).astype(F32)
            totals[g] = totals[g] + weight * along[g][h : h + 1]
            slope = (gate + product * (1.0 - gate)) * along_scaled[g][h : h + 1]
            dir_s[part, cols] = dot(slope.astype(BF), key_head).astype(BF)
    for g, part in enumerate(parts):
        partial = jnp.sum(totals[g], -1, keepdims=True).astype(BF).astype(F32)
        partial_row = jnp.broadcast_to(partial, (HIST, HIST)).T[:1]
        active = lax.broadcasted_iota(jnp.int32, (1, HIST), 1) < counts[step * GROUP + g]
        score = jnp.where(active, partial_row + own[g], 0.0)
        err = jnp.where(active, sigmoid(score) - labels[g], 0.0)
        scores[g] = score
        error[g] = err
        err_rows = jnp.broadcast_to(err, (HIST, HIST)).T
        for h in range(HEADS):
            cols = slice(h * LANES, (h + 1) * LANES)
            slope = (err_rows * dir_s[part, cols].astype(F32)).astype(BF)
            slopes[part, cols] = slope
            slope_s[step, part, cols] = slope

    @pl.when(step == pl.num_programs(0) - 1)
    def _():
        _, pairs, tall, wide = mine.shape
        right = width // wide
        down = mine.shape[0] // right
        piece = tall * down
        first = core[0] == 0
        for n in range(right):
            cols = slice(n * wide, (n + 1) * wide)
            grad = dot(cand_t[...], slope_s[:, :, cols].reshape(-1, wide))
            for p in range(pairs):
                one = grad[2 * p * piece : (2 * p + 1) * piece]
                two = grad[(2 * p + 1) * piece : (2 * p + 2) * piece]
                kept = jnp.where(first, one, two).astype(BF)
                sent = jnp.where(first, two, one).astype(BF)
                for a in range(down):
                    rows = slice(a * tall, (a + 1) * tall)
                    mine[a * right + n, p] = kept[rows]
                    other[a * right + n, p] = sent[rows]


def cross(counts, core, queries, encoded, score_weight, own, labels, cand_t, pairs, users):
    nblocks = counts.shape[0]
    total, width = queries.shape
    rows = total // nblocks
    side = math.isqrt(users)
    shape = (users, pairs, width // (2 * pairs * side), width // side)
    block_rows = pl.BlockSpec((GROUP * rows, width), lambda b, n, c: (b, 0))
    row = pl.BlockSpec((GROUP, 1, rows), lambda b, n, c: (b, 0, 0))
    whole4 = lambda b, n, c: (0, 0, 0, 0)
    return pl.pallas_call(
        cross_kernel,
        grid_spec=pltpu.PrefetchScalarGridSpec(
            num_scalar_prefetch=2,
            grid=(nblocks // GROUP,),
            in_specs=[
                block_rows,
                block_rows,
                pl.BlockSpec((1, width), lambda b, n, c: (0, 0)),
                row,
                row,
                pl.BlockSpec((width, total), lambda b, n, c: (0, 0)),
            ],
            out_specs=[
                row,
                row,
                block_rows,
                pl.BlockSpec(shape, whole4),
                pl.BlockSpec(shape, whole4),
            ],
            scratch_shapes=[
                pltpu.VMEM((nblocks // GROUP, GROUP * rows, width), BF),
                pltpu.VMEM((GROUP * rows, width), BF),
            ],
        ),
        out_shape=[
            jax.ShapeDtypeStruct((nblocks, 1, rows), F32),
            jax.ShapeDtypeStruct((nblocks, 1, rows), F32),
            jax.ShapeDtypeStruct((total, width), BF),
            jax.ShapeDtypeStruct(shape, BF),
            jax.ShapeDtypeStruct(shape, BF),
        ],
        compiler_params=pltpu.CompilerParams(vmem_limit_bytes=VMEM_BYTES),
        name="cross",
    )(counts, core, queries, encoded, score_weight, own, labels, cand_t)


def shift(array, side, dx, dy):
    moves = []
    for x in range(side):
        for y in range(side):
            moves.append(((x + dx) % side * side + (y + dy) % side, x * side + y))
    return lax.ppermute(array, "user", moves)


def spread(piece, side, x_first):
    first = lambda a, d: shift(a, side, d, 0) if x_first else shift(a, side, 0, d)
    second = lambda a, d: shift(a, side, 0, d) if x_first else shift(a, side, d, 0)
    low = jnp.stack([piece, first(piece, 1)])
    high = jnp.stack([first(piece, 2), first(piece, -1)])
    low_after, high_before = second(low, 1), second(high, -1)
    high_after, low_before = second(high, 1), second(low, -1)
    low_two, high_two = second(low_after, 1), second(high_before, -1)
    return (low, high, low_after, high_after, low_two, high_two, low_before, high_before)


def around(array, loaders):
    move = lambda a, d: lax.ppermute(
        a, "loader", [((i + 2 * d) % loaders, i) for i in range(loaders)]
    )
    pairs = loaders // 2
    after, before = [array], [array]
    for d in range(pairs // 2):
        after.append(move(after[-1], 1))
        if d < pairs // 2 - 1:
            before.append(move(before[-1], -1))
    own = jnp.stack(after + before[:0:-1])
    return own, lax.ppermute(own, "loader", [(i, i ^ 1) for i in range(loaders)])


def body(
    history_items,
    history_events,
    history_lengths,
    action_table,
    mix_weight,
    out_weight,
    query_weight,
    score_weight,
    self_weight,
    candidates,
    block_owner,
    row_counts,
    labels,
):
    users = lax.axis_size("user")
    loaders = lax.axis_size("loader")
    pairs = loaders // 2
    nblocks, rows, width = candidates.shape

    weights = lax.all_gather(mix_weight, "loader", axis=0, tiled=True)
    out_own, out_other = around(out_weight, loaders)
    actions = action_table.shape[0]
    packed = jnp.concatenate(
        [
            history_items[0],
            jnp.broadcast_to(history_events[0][:, None].astype(BF), (HIST, actions)),
            jnp.broadcast_to(history_lengths[0].astype(BF), (HIST, LANES - actions)),
        ],
        axis=1,
    )
    side = math.isqrt(users)
    half = HIST // 2
    halves_a = spread(packed[:half], side, True)
    halves_b = spread(packed[half:], side, False)

    flat = candidates.reshape(-1, width)
    queries = jnp.dot(flat, query_weight, preferred_element_type=F32).astype(BF)
    cand_t = flat.T
    own = jnp.sum(candidates.astype(F32) * self_weight, -1)

    owner = block_owner[:, 0]
    here = lax.axis_index("user").astype(jnp.int32)
    far_x = lax.rem(owner // side - here // side + side, side)
    far_y = lax.rem(lax.rem(owner, side) - lax.rem(here, side) + side, side)
    base, normed, mask = prepare(
        far_y * side + far_x, far_x * side + far_y, halves_a, halves_b, action_table
    )
    loader = lax.axis_index("loader").astype(jnp.int32)
    core = lax.rem(loader, 2)[None]
    place = jnp.stack([loader // 2, lax.rem(loader, 2)])
    encoded = encode(place, normed, base, mask, weights, out_own, out_other)
    scores, error, slopes, mine, other = cross(
        row_counts,
        core,
        queries,
        encoded,
        score_weight[None],
        own[:, None],
        labels[:, None],
        cand_t,
        pairs,
        users,
    )

    arrived = lax.ppermute(other, "loader", [(i, i ^ 1) for i in range(loaders)])
    pieces = (mine.astype(F32) + arrived.astype(F32)).astype(BF)
    pieces = lax.all_to_all(pieces, "user", 0, 0, tiled=True)
    pieces = jnp.sum(pieces.astype(F32), 0).astype(BF)
    groups = [[c + 2 * i for i in range(pairs)] for c in range(2)]
    pieces = lax.all_to_all(pieces, "loader", 0, 0, axis_index_groups=groups, tiled=True)
    piece = jnp.sum(pieces.astype(F32), 0).astype(BF)
    pieces = lax.all_to_all(
        jnp.broadcast_to(piece[None], (users,) + piece.shape), "user", 0, 0, tiled=True
    )
    right = math.isqrt(users)
    tall, wide = piece.shape
    query_grad = pieces.reshape(users // right, right, tall, wide).transpose(0, 2, 1, 3)
    query_grad = query_grad.reshape(users // right * tall, right * wide).astype(F32)

    back = lax.dot_general(slopes, query_weight, (((1,), (1,)), ((), ())), preferred_element_type=F32)
    row_grads = (error.reshape(-1)[:, None] * self_weight + back).astype(BF)
    return (scores[:, 0], row_grads.reshape(nblocks, rows, width), query_grad)


def solution(mesh):
    placed = (
        P(("user", "loader"), None, None),
        P(("user", "loader"), None),
        P(("user", "loader")),
        P(),
        P("loader", None),
        P("loader", None),
        P(),
        P(),
        P(),
        P(("user", "loader"), None, None),
        P(("user", "loader"), None),
        P(("user", "loader")),
        P(("user", "loader"), None),
    )
    return jax.shard_map(
        body,
        mesh=mesh,
        in_specs=placed,
        out_specs=(
            P(("user", "loader"), None),
            P(("user", "loader"), None, None),
            P("loader", None),
        ),
        check_vma=False,
    )
```

```python
import functools
import math

import jax
import jax.numpy as jnp
from jax import lax
from jax.experimental import pallas as pl
from jax.experimental.pallas import tpu as pltpu
from jax.sharding import PartitionSpec as P

HEADS = 8
HIST = 128
LANES = 128
BF = jnp.bfloat16
F32 = jnp.float32
VMEM_BYTES = 56 * 1024 * 1024


def sigmoid(v):
    return 0.5 * jnp.tanh(0.5 * v) + 0.5


def dot(a, b):
    return jnp.dot(a, b, preferred_element_type=F32)


def dot_t(a, b):
    return lax.dot_general(a, b, (((1,), (1,)), ((), ())), preferred_element_type=F32)


def split3(v):
    high = v.astype(BF)
    rest = v - high.astype(F32)
    middle = rest.astype(BF)
    low = (rest - middle.astype(F32)).astype(BF)
    return high, middle, low


def prepare_kernel(nblocks, place_a, place_b, *refs):
    count = (len(refs) - 6) // 2
    halves = ((place_a, refs[:count]), (place_b, refs[count : 2 * count]))
    table, base, normed, mask, rows_s, sems = refs[2 * count :]
    block = pl.program_id(0)
    width = base.shape[1]
    actions = table.shape[0]
    half = HIST // 2

    def fetch(which, b, source):
        return pltpu.make_async_copy(
            source, rows_s.at[b, pl.ds(which * half, half)], sems.at[which, b]
        )

    @pl.when(block == 0)
    def _():
        for b in range(nblocks):
            for which, (place, arrays) in enumerate(halves):
                for k, array in enumerate(arrays):

                    @pl.when(place[b] // 2 == k)
                    def _():
                        fetch(which, b, array.at[lax.rem(place[b], 2)]).start()

    for which, (place, arrays) in enumerate(halves):
        fetch(which, block, arrays[0].at[0]).wait()
    rows = rows_s[block]
    tail = rows[:, width:].astype(F32)
    lane = lax.broadcasted_iota(jnp.int32, (HIST, actions), 1).astype(F32)
    onehot = jnp.where(tail[:, :actions] == lane, 1.0, 0.0).astype(BF)
    value = rows[:, :width].astype(F32)
    high, middle, low = split3(table[...])
    value = value + ((dot(onehot, low) + dot(onehot, middle)) + dot(onehot, high))
    scale = lax.rsqrt(jnp.mean(value * value, -1, keepdims=True) + 1e-06)
    base[...] = value
    normed[...] = (value * scale).astype(BF)
    position = lax.broadcasted_iota(jnp.int32, (HIST, LANES), 0).astype(F32)
    mask[...] = jnp.where(position < tail[:, LANES - 1 :], 1.0, 0.0)


def prepare(place_a, place_b, halves_a, halves_b, table):
    nblocks = place_a.shape[0]
    width = table.shape[1]
    total = nblocks * HIST
    arrays = list(halves_a) + list(halves_b)
    return pl.pallas_call(
        functools.partial(prepare_kernel, nblocks),
        grid_spec=pltpu.PrefetchScalarGridSpec(
            num_scalar_prefetch=2,
            grid=(nblocks,),
            in_specs=[pl.BlockSpec(memory_space=pl.ANY)] * len(arrays)
            + [pl.BlockSpec(table.shape, lambda b, p, q: (0, 0))],
            out_specs=[
                pl.BlockSpec((HIST, width), lambda b, p, q: (b, 0)),
                pl.BlockSpec((HIST, width), lambda b, p, q: (b, 0)),
                pl.BlockSpec((HIST, LANES), lambda b, p, q: (b, 0)),
            ],
            scratch_shapes=[
                pltpu.VMEM((nblocks, HIST, arrays[0].shape[-1]), BF),
                pltpu.SemaphoreType.DMA((2, nblocks)),
            ],
        ),
        out_shape=[
            jax.ShapeDtypeStruct((total, width), F32),
            jax.ShapeDtypeStruct((total, width), BF),
            jax.ShapeDtypeStruct((total, LANES), F32),
        ],
        compiler_params=pltpu.CompilerParams(vmem_limit_bytes=VMEM_BYTES),
        name="prepare",
    )(place_a, place_b, *arrays, table)


ENCODE_STEPS = HEADS // 2
GROUP = 2


def attention_kernel(
    counts,
    core,
    normed,
    base,
    weights,
    queries,
    cand_t,
    mask,
    score_weight,
    own,
    labels,
    scores,
    error,
    slopes,
    mine,
    other,
    normed_s,
    base_s,
    mix_s,
    out_s,
    queries_s,
    cand_s,
    gate_s,
    mixed_s,
    qkv_s,
    gated_s,
    encoded_s,
    logit_s,
    weight_s,
    slope_s,
    sems,
    mix_sems,
):
    step = pl.program_id(0)
    total, width = normed_s.shape
    pair = 2 * LANES

    def mix_copy(i, group):
        start = pl.multiple_of(group * width + i * pair, pair)
        return pltpu.make_async_copy(
            weights.at[:, pl.ds(start, pair)], mix_s.at[i, group], mix_sems.at[i, group]
        )

    normed_copy = pltpu.make_async_copy(normed, normed_s, sems.at[0])
    base_copy = pltpu.make_async_copy(base, base_s, sems.at[1])
    out_copy = pltpu.make_async_copy(weights.at[:, pl.ds(4 * width, width)], out_s, sems.at[2])
    query_copy = pltpu.make_async_copy(queries, queries_s, sems.at[3])
    cand_copy = pltpu.make_async_copy(cand_t, cand_s, sems.at[4])

    @pl.when(step == 0)
    def _():
        normed_copy.start()
        for i in range(ENCODE_STEPS):
            for group in range(4):
                mix_copy(i, group).start()
        for copy in (base_copy, out_copy, query_copy, cand_copy):
            copy.start()
        normed_copy.wait()

    @pl.when(step < ENCODE_STEPS)
    def _():
        for group in range(4):
            mix_copy(step, group).wait()
        users = total // HIST
        for k in range(2):
            cols = slice(k * LANES, (k + 1) * LANES)
            columns = jnp.concatenate([mix_s[step, g, :, cols] for g in range(4)], axis=1)
            projected = dot(normed_s[...], columns)
            projected = projected * sigmoid(projected)
            gate_s[2 * step + k] = projected[:, :LANES]
            qkv_s[k] = projected[:, LANES:].astype(BF)
        units = [(k, slice(u * HIST, (u + 1) * HIST)) for k in range(2) for u in range(users)]
        for n, (k, part) in enumerate(units):
            logit_s[n] = dot_t(qkv_s[k, part, LANES : 2 * LANES], qkv_s[k, part, 2 * LANES :])
        row = lax.broadcasted_iota(jnp.int32, (HIST, HIST), 0)
        column = lax.broadcasted_iota(jnp.int32, (HIST, HIST), 1)
        causal = column <= row
        for n in range(len(units)):
            logits = logit_s[n] * (1.0 / math.sqrt(LANES))
            weight = jnp.where(causal, logits * sigmoid(logits) * (1.0 / HIST), 0.0)
            weight_s[n] = weight.astype(BF)
        for n, (k, part) in enumerate(units):
            mixed_s[2 * step + k, part] = dot(weight_s[n], qkv_s[k, part, :LANES])

    @pl.when(step == ENCODE_STEPS - 1)
    def _():
        square = mixed_s[0] * mixed_s[0]
        for h in range(1, HEADS):
            square = square + mixed_s[h] * mixed_s[h]
        scale = lax.rsqrt(jnp.sum(square, -1, keepdims=True) * (1.0 / width) + 1e-06)
        for h in range(HEADS):
            gated_s[:, h * LANES : (h + 1) * LANES] = (mixed_s[h] * scale * gate_s[h]).astype(BF)
        active = mask[:, :1] > 0.0
        base_copy.wait()
        out_copy.wait()
        for n in range(width // pair):
            cols = slice(n * pair, (n + 1) * pair)
            value = base_s[:, cols] + dot(gated_s[...], out_s[:, cols])
            value = jnp.where(active, value, 0.0).astype(BF)
            encoded_s[:, :, cols] = value.reshape(total // (GROUP * HIST), GROUP * HIST, pair)
        query_copy.wait()
        cand_copy.wait()

    @pl.when(step >= ENCODE_STEPS)
    def _():
        now = step - ENCODE_STEPS
        lane = lax.broadcasted_iota(jnp.int32, (HEADS, width), 1) // LANES
        head_row = lax.broadcasted_iota(jnp.int32, (HEADS, width), 0)
        spread_weight = jnp.where(lane == head_row, score_weight[...], 0.0)
        high, middle, low = split3(spread_weight)
        parts = [slice(g * HIST, (g + 1) * HIST) for g in range(GROUP)]
        units = [(h, g) for g in range(GROUP) for h in range(HEADS)]
        heads = [slice(h * LANES, (h + 1) * LANES) for h in range(HEADS)]
        for n, (h, g) in enumerate(units):
            logit_s[n] = dot_t(
                queries_s[now, parts[g], heads[h]], encoded_s[now, parts[g], heads[h]]
            )
        along = []
        for part in parts:
            keys = encoded_s[now, part]
            along.append((dot_t(low, keys) + dot_t(middle, keys)) + dot_t(high, keys))
        totals = [jnp.zeros((HIST, HIST), F32) for _ in range(GROUP)]
        for n, (h, g) in enumerate(units):
            row = along[g][h : h + 1]
            logits = logit_s[n] * (1.0 / math.sqrt(LANES))
            gate = sigmoid(logits)
            product = logits * gate
            weight = (product * (1.0 / HIST)).astype(BF).astype(F32)
            totals[g] = totals[g] + weight * row
            slope = gate + product * (1.0 - gate)
            weight_s[n] = (slope * (row * (1.0 / (HIST * math.sqrt(LANES))))).astype(BF)
        for n, (h, g) in enumerate(units):
            logit_s[n] = dot(weight_s[n], encoded_s[now, parts[g], heads[h]])
        for g, part in enumerate(parts):
            partial = jnp.sum(totals[g], -1, keepdims=True).astype(BF).astype(F32)
            partial_row = jnp.broadcast_to(partial, (HIST, HIST)).T[:1]
            active = lax.broadcasted_iota(jnp.int32, (1, HIST), 1) < counts[now * GROUP + g]
            score = jnp.where(active, partial_row + own[g], 0.0)
            err = jnp.where(active, sigmoid(score) - labels[g], 0.0)
            scores[g] = score
            error[g] = err
            err_rows = jnp.broadcast_to(err, (HIST, HIST)).T
            for h in range(HEADS):
                direction = logit_s[g * HEADS + h].astype(BF).astype(F32)
                slope = (err_rows * direction).astype(BF)
                slopes[part, heads[h]] = slope
                slope_s[now, part, heads[h]] = slope

    @pl.when(step == pl.num_programs(0) - 1)
    def _():
        _, pairs, tall, wide = mine.shape
        right = width // wide
        down = mine.shape[0] // right
        piece = tall * down
        first = core[0] == 0
        for n in range(right):
            cols = slice(n * wide, (n + 1) * wide)
            grad = dot(cand_s[...], slope_s[:, :, cols].reshape(-1, wide))
            for p in range(pairs):
                one = grad[2 * p * piece : (2 * p + 1) * piece]
                two = grad[(2 * p + 1) * piece : (2 * p + 2) * piece]
                kept = jnp.where(first, one, two).astype(BF)
                sent = jnp.where(first, two, one).astype(BF)
                for a in range(down):
                    rows = slice(a * tall, (a + 1) * tall)
                    mine[a * right + n, p] = kept[rows]
                    other[a * right + n, p] = sent[rows]


def attention(
    counts,
    core,
    normed,
    base,
    mask,
    weights,
    queries,
    cand_t,
    score_weight,
    own,
    labels,
    pairs,
    users,
):
    nblocks = counts.shape[0]
    total, width = queries.shape
    rows = total // nblocks
    groups = nblocks // GROUP
    side = math.isqrt(users)
    shape = (users, pairs, width // (2 * pairs * side), width // side)
    current = lambda i: jnp.maximum(i - ENCODE_STEPS, 0)
    row = pl.BlockSpec((GROUP, 1, rows), lambda i, n, c: (current(i), 0, 0))
    whole = lambda i, n, c: (0, 0)
    whole4 = lambda i, n, c: (0, 0, 0, 0)
    anywhere = pl.BlockSpec(memory_space=pl.ANY)
    return pl.pallas_call(
        attention_kernel,
        grid_spec=pltpu.PrefetchScalarGridSpec(
            num_scalar_prefetch=2,
            grid=(ENCODE_STEPS + groups,),
            in_specs=[anywhere] * 5
            + [
                pl.BlockSpec((total, LANES), whole),
                pl.BlockSpec((1, width), whole),
                row,
                row,
            ],
            out_specs=[
                row,
                row,
                pl.BlockSpec((GROUP * rows, width), lambda i, n, c: (current(i), 0)),
                pl.BlockSpec(shape, whole4),
                pl.BlockSpec(shape, whole4),
            ],
            scratch_shapes=[
                pltpu.VMEM((total, width), BF),
                pltpu.VMEM((total, width), F32),
                pltpu.VMEM((ENCODE_STEPS, 4, width, 2 * LANES), BF),
                pltpu.VMEM((width, width), BF),
                pltpu.VMEM((groups, GROUP * rows, width), BF),
                pltpu.VMEM((width, total), BF),
                pltpu.VMEM((HEADS, total, LANES), F32),
                pltpu.VMEM((HEADS, total, LANES), F32),
                pltpu.VMEM((2, total, 3 * LANES), BF),
                pltpu.VMEM((total, width), BF),
                pltpu.VMEM((groups, GROUP * rows, width), BF),
                pltpu.VMEM((GROUP * HEADS, HIST, HIST), F32),
                pltpu.VMEM((GROUP * HEADS, HIST, HIST), BF),
                pltpu.VMEM((groups, GROUP * rows, width), BF),
                pltpu.SemaphoreType.DMA((5,)),
                pltpu.SemaphoreType.DMA((ENCODE_STEPS, 4)),
            ],
        ),
        out_shape=[
            jax.ShapeDtypeStruct((nblocks, 1, rows), F32),
            jax.ShapeDtypeStruct((nblocks, 1, rows), F32),
            jax.ShapeDtypeStruct((total, width), BF),
            jax.ShapeDtypeStruct(shape, BF),
            jax.ShapeDtypeStruct(shape, BF),
        ],
        compiler_params=pltpu.CompilerParams(vmem_limit_bytes=VMEM_BYTES),
        name="attention",
    )(
        counts,
        core,
        normed,
        base,
        weights,
        queries.reshape(groups, GROUP * rows, width),
        cand_t,
        mask,
        score_weight,
        own,
        labels,
    )


def shift(array, side, dx, dy):
    moves = []
    for x in range(side):
        for y in range(side):
            moves.append(((x + dx) % side * side + (y + dy) % side, x * side + y))
    return lax.ppermute(array, "user", moves)


def spread(piece, side, x_first):
    first = lambda a, d: shift(a, side, d, 0) if x_first else shift(a, side, 0, d)
    second = lambda a, d: shift(a, side, 0, d) if x_first else shift(a, side, d, 0)
    low = jnp.stack([piece, first(piece, 1)])
    high = jnp.stack([first(piece, 2), first(piece, -1)])
    low_after, high_before = second(low, 1), second(high, -1)
    high_after, low_before = second(high, 1), second(low, -1)
    low_two, high_two = second(low_after, 1), second(high_before, -1)
    return (low, high, low_after, high_after, low_two, high_two, low_before, high_before)


def join_kernel(left, right, out, sems):
    wide = left.shape[1]
    first = pltpu.make_async_copy(left, out.at[:, pl.ds(0, wide)], sems.at[0])
    second = pltpu.make_async_copy(right, out.at[:, pl.ds(wide, right.shape[1])], sems.at[1])
    first.start()
    second.start()
    first.wait()
    second.wait()


def join(left, right):
    anywhere = pl.BlockSpec(memory_space=pl.ANY)
    return pl.pallas_call(
        join_kernel,
        in_specs=[anywhere, anywhere],
        out_specs=anywhere,
        out_shape=jax.ShapeDtypeStruct((left.shape[0], left.shape[1] + right.shape[1]), left.dtype),
        scratch_shapes=[pltpu.SemaphoreType.DMA((2,))],
        name="join",
    )(left, right)


def assemble_kernel(pieces, out):
    count, tall, wide = pieces.shape
    right = out.shape[1] // wide
    for k in range(count):
        a, b = k // right, k % right
        rows, cols = slice(a * tall, (a + 1) * tall), slice(b * wide, (b + 1) * wide)
        out[rows, cols] = pieces[k].astype(F32)


def assemble(pieces, right):
    count, tall, wide = pieces.shape
    return pl.pallas_call(
        assemble_kernel,
        out_shape=jax.ShapeDtypeStruct((count // right * tall, right * wide), F32),
        name="assemble",
    )(pieces)


def body(
    history_items,
    history_events,
    history_lengths,
    action_table,
    mix_weight,
    out_weight,
    query_weight,
    score_weight,
    self_weight,
    candidates,
    block_owner,
    row_counts,
    labels,
):
    users = lax.axis_size("user")
    loaders = lax.axis_size("loader")
    pairs = loaders // 2
    nblocks, rows, width = candidates.shape

    weights = lax.all_gather(join(mix_weight, out_weight), "loader", axis=0, tiled=True)
    actions = action_table.shape[0]
    packed = jnp.concatenate(
        [
            history_items[0],
            jnp.broadcast_to(history_events[0][:, None].astype(BF), (HIST, actions)),
            jnp.broadcast_to(history_lengths[0].astype(BF), (HIST, LANES - actions)),
        ],
        axis=1,
    )
    side = math.isqrt(users)
    half = HIST // 2
    halves_a = spread(packed[:half], side, True)
    halves_b = spread(packed[half:], side, False)

    flat = candidates.reshape(-1, width)
    queries = jnp.dot(flat, query_weight, preferred_element_type=F32).astype(BF)
    cand_t = flat.T
    own = jnp.sum(candidates.astype(F32) * self_weight, -1)

    owner = block_owner[:, 0]
    here = lax.axis_index("user").astype(jnp.int32)
    far_x = lax.rem(owner // side - here // side + side, side)
    far_y = lax.rem(lax.rem(owner, side) - lax.rem(here, side) + side, side)
    base, normed, mask = prepare(
        far_y * side + far_x, far_x * side + far_y, halves_a, halves_b, action_table
    )
    core = lax.rem(lax.axis_index("loader").astype(jnp.int32), 2)[None]
    scores, error, slopes, mine, other = attention(
        row_counts,
        core,
        normed,
        base,
        mask,
        weights,
        queries,
        cand_t,
        score_weight[None],
        own[:, None],
        labels[:, None],
        pairs,
        users,
    )

    arrived = lax.ppermute(other, "loader", [(i, i ^ 1) for i in range(loaders)])
    pieces = (mine.astype(F32) + arrived.astype(F32)).astype(BF)
    pieces = lax.all_to_all(pieces, "user", 0, 0, tiled=True)
    pieces = jnp.sum(pieces.astype(F32), 0).astype(BF)
    groups = [[c + 2 * i for i in range(pairs)] for c in range(2)]
    pieces = lax.all_to_all(pieces, "loader", 0, 0, axis_index_groups=groups, tiled=True)
    piece = jnp.sum(pieces.astype(F32), 0).astype(BF)
    pieces = lax.all_to_all(
        jnp.broadcast_to(piece[None], (users,) + piece.shape), "user", 0, 0, tiled=True
    )
    query_grad = assemble(pieces, side)

    back = lax.dot_general(slopes, query_weight, (((1,), (1,)), ((), ())), preferred_element_type=F32)
    row_grads = (error.reshape(-1)[:, None] * self_weight + back).astype(BF)
    return (scores[:, 0], row_grads.reshape(nblocks, rows, width), query_grad)


def solution(mesh):
    placed = (
        P(("user", "loader"), None, None),
        P(("user", "loader"), None),
        P(("user", "loader")),
        P(),
        P("loader", None),
        P("loader", None),
        P(),
        P(),
        P(),
        P(("user", "loader"), None, None),
        P(("user", "loader"), None),
        P(("user", "loader")),
        P(("user", "loader"), None),
    )
    return jax.shard_map(
        body,
        mesh=mesh,
        in_specs=placed,
        out_specs=(
            P(("user", "loader"), None),
            P(("user", "loader"), None, None),
            P("loader", None),
        ),
        check_vma=False,
    )
```

```python
import functools
import math

import jax
import jax.numpy as jnp
from jax import lax
from jax.experimental import pallas as pl
from jax.experimental.pallas import tpu as pltpu
from jax.sharding import PartitionSpec as P

HEADS = 8
HIST = 128
LANES = 128
BF = jnp.bfloat16
F32 = jnp.float32
VMEM_BYTES = 56 * 1024 * 1024


def sigmoid(v):
    return 0.5 * jnp.tanh(0.5 * v) + 0.5


def dot(a, b):
    return jnp.dot(a, b, preferred_element_type=F32)


def dot_t(a, b):
    return lax.dot_general(a, b, (((1,), (1,)), ((), ())), preferred_element_type=F32)


def split3(v):
    high = v.astype(BF)
    rest = v - high.astype(F32)
    middle = rest.astype(BF)
    low = (rest - middle.astype(F32)).astype(BF)
    return high, middle, low


def prepare_kernel(nblocks, place_a, place_b, *refs):
    count = (len(refs) - 6) // 2
    halves = ((place_a, refs[:count]), (place_b, refs[count : 2 * count]))
    table, base, normed, mask, rows_s, sems = refs[2 * count :]
    block = pl.program_id(0)
    width = base.shape[1]
    actions = table.shape[0]
    half = HIST // 2

    def fetch(which, b, source):
        return pltpu.make_async_copy(
            source, rows_s.at[b, pl.ds(which * half, half)], sems.at[which, b]
        )

    @pl.when(block == 0)
    def _():
        for b in range(nblocks):
            for which, (place, arrays) in enumerate(halves):
                for k, array in enumerate(arrays):

                    @pl.when(place[b] // 2 == k)
                    def _():
                        fetch(which, b, array.at[lax.rem(place[b], 2)]).start()

    for which, (place, arrays) in enumerate(halves):
        fetch(which, block, arrays[0].at[0]).wait()
    rows = rows_s[block]
    tail = rows[:, width:].astype(F32)
    lane = lax.broadcasted_iota(jnp.int32, (HIST, actions), 1).astype(F32)
    onehot = jnp.where(tail[:, :actions] == lane, 1.0, 0.0).astype(BF)
    value = rows[:, :width].astype(F32)
    high, middle, low = split3(table[...])
    value = value + ((dot(onehot, low) + dot(onehot, middle)) + dot(onehot, high))
    scale = lax.rsqrt(jnp.mean(value * value, -1, keepdims=True) + 1e-06)
    base[...] = value
    normed[...] = (value * scale).astype(BF)
    position = lax.broadcasted_iota(jnp.int32, (HIST, LANES), 0).astype(F32)
    mask[...] = jnp.where(position < tail[:, LANES - 1 :], 1.0, 0.0)


def prepare(place_a, place_b, halves_a, halves_b, table):
    nblocks = place_a.shape[0]
    width = table.shape[1]
    total = nblocks * HIST
    arrays = list(halves_a) + list(halves_b)
    return pl.pallas_call(
        functools.partial(prepare_kernel, nblocks),
        grid_spec=pltpu.PrefetchScalarGridSpec(
            num_scalar_prefetch=2,
            grid=(nblocks,),
            in_specs=[pl.BlockSpec(memory_space=pl.ANY)] * len(arrays)
            + [pl.BlockSpec(table.shape, lambda b, p, q: (0, 0))],
            out_specs=[
                pl.BlockSpec((HIST, width), lambda b, p, q: (b, 0)),
                pl.BlockSpec((HIST, width), lambda b, p, q: (b, 0)),
                pl.BlockSpec((HIST, LANES), lambda b, p, q: (b, 0)),
            ],
            scratch_shapes=[
                pltpu.VMEM((nblocks, HIST, arrays[0].shape[-1]), BF),
                pltpu.SemaphoreType.DMA((2, nblocks)),
            ],
        ),
        out_shape=[
            jax.ShapeDtypeStruct((total, width), F32),
            jax.ShapeDtypeStruct((total, width), BF),
            jax.ShapeDtypeStruct((total, LANES), F32),
        ],
        compiler_params=pltpu.CompilerParams(vmem_limit_bytes=VMEM_BYTES),
        name="prepare",
    )(place_a, place_b, *arrays, table)


ENCODE_STEPS = HEADS // 2
GROUP = 2


def attention_kernel(
    counts,
    core,
    normed,
    base,
    weights,
    queries,
    cand_t,
    mask,
    score_weight,
    own,
    labels,
    scores,
    error,
    slopes,
    mine,
    other,
    normed_s,
    base_s,
    mix_s,
    out_s,
    queries_s,
    cand_s,
    gate_s,
    mixed_s,
    qkv_s,
    gated_s,
    encoded_s,
    logit_s,
    weight_s,
    slope_s,
    mine_s,
    other_s,
    sems,
    mix_sems,
    grad_sems,
):
    step = pl.program_id(0)
    total, width = normed_s.shape
    pair = 2 * LANES

    def mix_copy(i, group):
        start = pl.multiple_of(group * width + i * pair, pair)
        return pltpu.make_async_copy(
            weights.at[:, pl.ds(start, pair)], mix_s.at[i, group], mix_sems.at[i, group]
        )

    normed_copy = pltpu.make_async_copy(normed, normed_s, sems.at[0])
    base_copy = pltpu.make_async_copy(base, base_s, sems.at[1])
    out_copy = pltpu.make_async_copy(weights.at[:, pl.ds(4 * width, width)], out_s, sems.at[2])
    query_copy = pltpu.make_async_copy(queries, queries_s, sems.at[3])
    cand_copy = pltpu.make_async_copy(cand_t, cand_s, sems.at[4])

    @pl.when(step == 0)
    def _():
        normed_copy.start()
        for group in range(4):
            mix_copy(0, group).start()
        normed_copy.wait()

    @pl.when(step < ENCODE_STEPS)
    def _():
        for group in range(4):
            mix_copy(step, group).wait()

        @pl.when(step + 1 < ENCODE_STEPS)
        def _():
            for group in range(4):
                mix_copy(step + 1, group).start()

        @pl.when(step == 1)
        def _():
            base_copy.start()

        @pl.when(step == 2)
        def _():
            out_copy.start()

        @pl.when(step == 3)
        def _():
            query_copy.start()
            cand_copy.start()

        users = total // HIST
        for k in range(2):
            cols = slice(k * LANES, (k + 1) * LANES)
            columns = jnp.concatenate([mix_s[step, g, :, cols] for g in range(4)], axis=1)
            projected = dot(normed_s[...], columns)
            projected = projected * sigmoid(projected)
            gate_s[2 * step + k] = projected[:, :LANES]
            qkv_s[k] = projected[:, LANES:].astype(BF)
        units = [(k, slice(u * HIST, (u + 1) * HIST)) for k in range(2) for u in range(users)]
        for n, (k, part) in enumerate(units):
            logit_s[n] = dot_t(qkv_s[k, part, LANES : 2 * LANES], qkv_s[k, part, 2 * LANES :])
        row = lax.broadcasted_iota(jnp.int32, (HIST, HIST), 0)
        column = lax.broadcasted_iota(jnp.int32, (HIST, HIST), 1)
        causal = column <= row
        for n in range(len(units)):
            logits = logit_s[n] * (1.0 / math.sqrt(LANES))
            weight = jnp.where(causal, logits * sigmoid(logits) * (1.0 / HIST), 0.0)
            weight_s[n] = weight.astype(BF)
        for n, (k, part) in enumerate(units):
            mixed_s[2 * step + k, part] = dot(weight_s[n], qkv_s[k, part, :LANES])

    @pl.when(step == ENCODE_STEPS - 1)
    def _():
        square = mixed_s[0] * mixed_s[0]
        for h in range(1, HEADS):
            square = square + mixed_s[h] * mixed_s[h]
        scale = lax.rsqrt(jnp.sum(square, -1, keepdims=True) * (1.0 / width) + 1e-06)
        for h in range(HEADS):
            gated_s[:, h * LANES : (h + 1) * LANES] = (mixed_s[h] * scale * gate_s[h]).astype(BF)
        active = mask[:, :1] > 0.0
        base_copy.wait()
        out_copy.wait()
        for n in range(width // pair):
            cols = slice(n * pair, (n + 1) * pair)
            value = base_s[:, cols] + dot(gated_s[...], out_s[:, cols])
            value = jnp.where(active, value, 0.0).astype(BF)
            encoded_s[:, :, cols] = value.reshape(total // (GROUP * HIST), GROUP * HIST, pair)
        query_copy.wait()
        cand_copy.wait()

    @pl.when(step >= ENCODE_STEPS)
    def _():
        now = step - ENCODE_STEPS
        lane = lax.broadcasted_iota(jnp.int32, (HEADS, width), 1) // LANES
        head_row = lax.broadcasted_iota(jnp.int32, (HEADS, width), 0)
        spread_weight = jnp.where(lane == head_row, score_weight[...], 0.0)
        high, middle, low = split3(spread_weight)
        parts = [slice(g * HIST, (g + 1) * HIST) for g in range(GROUP)]
        units = [(h, g) for g in range(GROUP) for h in range(HEADS)]
        heads = [slice(h * LANES, (h + 1) * LANES) for h in range(HEADS)]
        for n, (h, g) in enumerate(units):
            logit_s[n] = dot_t(
                queries_s[now, parts[g], heads[h]], encoded_s[now, parts[g], heads[h]]
            )
        along = []
        for part in parts:
            keys = encoded_s[now, part]
            along.append((dot_t(low, keys) + dot_t(middle, keys)) + dot_t(high, keys))
        totals = [jnp.zeros((HIST, HIST), F32) for _ in range(GROUP)]
        for n, (h, g) in enumerate(units):
            row = along[g][h : h + 1]
            logits = logit_s[n] * (1.0 / math.sqrt(LANES))
            gate = sigmoid(logits)
            product = logits * gate
            weight = (product * (1.0 / HIST)).astype(BF).astype(F32)
            totals[g] = totals[g] + weight * row
            slope = gate + product * (1.0 - gate)
            weight_s[n] = (slope * (row * (1.0 / (HIST * math.sqrt(LANES))))).astype(BF)
        for n, (h, g) in enumerate(units):
            logit_s[n] = dot(weight_s[n], encoded_s[now, parts[g], heads[h]])
        for g, part in enumerate(parts):
            partial = jnp.sum(totals[g], -1, keepdims=True).astype(BF).astype(F32)
            partial_row = jnp.broadcast_to(partial, (HIST, HIST)).T[:1]
            active = lax.broadcasted_iota(jnp.int32, (1, HIST), 1) < counts[now * GROUP + g]
            score = jnp.where(active, partial_row + own[g], 0.0)
            err = jnp.where(active, sigmoid(score) - labels[g], 0.0)
            scores[g] = score
            error[g] = err
            err_rows = jnp.broadcast_to(err, (HIST, HIST)).T
            for h in range(HEADS):
                direction = logit_s[g * HEADS + h].astype(BF).astype(F32)
                slope = (err_rows * direction).astype(BF)
                slopes[part, heads[h]] = slope
                slope_s[now, part, heads[h]] = slope

    @pl.when(step == pl.num_programs(0) - 1)
    def _():
        _, pairs, tall, wide = mine.shape
        right = width // wide
        down = mine.shape[0] // right
        piece = tall * down
        copies = []
        for n in range(right):
            cols = slice(n * wide, (n + 1) * wide)
            slope = slope_s[:, :, cols].reshape(-1, wide)
            for which, store in ((core[0], mine_s), (1 - core[0], other_s)):
                rows = cand_s[:, which].reshape(pairs * piece, -1)
                grad = dot(rows, slope).astype(BF)
                for p in range(pairs):
                    for a in range(down):
                        start = p * piece + a * tall
                        store[n * down + a, p] = grad[start : start + tall]
            chunk = pl.ds(n * down, down)
            for k, (source, target) in enumerate(((mine_s, mine), (other_s, other))):
                copy = pltpu.make_async_copy(
                    source.at[chunk], target.at[chunk], grad_sems.at[k, n]
                )
                copy.start()
                copies.append(copy)
        for copy in copies:
            copy.wait()


def attention(
    counts,
    core,
    normed,
    base,
    mask,
    weights,
    queries,
    cand_t,
    score_weight,
    own,
    labels,
    pairs,
    users,
):
    nblocks = counts.shape[0]
    total, width = queries.shape
    rows = total // nblocks
    groups = nblocks // GROUP
    side = math.isqrt(users)
    shape = (users, pairs, width // (2 * pairs * side), width // side)
    current = lambda i: jnp.maximum(i - ENCODE_STEPS, 0)
    row = pl.BlockSpec((GROUP, 1, rows), lambda i, n, c: (current(i), 0, 0))
    whole = lambda i, n, c: (0, 0)
    anywhere = pl.BlockSpec(memory_space=pl.ANY)
    return pl.pallas_call(
        attention_kernel,
        grid_spec=pltpu.PrefetchScalarGridSpec(
            num_scalar_prefetch=2,
            grid=(ENCODE_STEPS + groups,),
            in_specs=[anywhere] * 5
            + [
                pl.BlockSpec((total, LANES), whole),
                pl.BlockSpec((1, width), whole),
                row,
                row,
            ],
            out_specs=[
                row,
                row,
                pl.BlockSpec((GROUP * rows, width), lambda i, n, c: (current(i), 0)),
                anywhere,
                anywhere,
            ],
            scratch_shapes=[
                pltpu.VMEM((total, width), BF),
                pltpu.VMEM((total, width), F32),
                pltpu.VMEM((ENCODE_STEPS, 4, width, 2 * LANES), BF),
                pltpu.VMEM((width, width), BF),
                pltpu.VMEM((groups, GROUP * rows, width), BF),
                pltpu.VMEM((pairs, 2, width // (2 * pairs), total), BF),
                pltpu.VMEM((HEADS, total, LANES), F32),
                pltpu.VMEM((HEADS, total, LANES), F32),
                pltpu.VMEM((2, total, 3 * LANES), BF),
                pltpu.VMEM((total, width), BF),
                pltpu.VMEM((groups, GROUP * rows, width), BF),
                pltpu.VMEM((GROUP * HEADS, HIST, HIST), F32),
                pltpu.VMEM((GROUP * HEADS, HIST, HIST), BF),
                pltpu.VMEM((groups, GROUP * rows, width), BF),
                pltpu.VMEM(shape, BF),
                pltpu.VMEM(shape, BF),
                pltpu.SemaphoreType.DMA((5,)),
                pltpu.SemaphoreType.DMA((ENCODE_STEPS, 4)),
                pltpu.SemaphoreType.DMA((2, side)),
            ],
        ),
        out_shape=[
            jax.ShapeDtypeStruct((nblocks, 1, rows), F32),
            jax.ShapeDtypeStruct((nblocks, 1, rows), F32),
            jax.ShapeDtypeStruct((total, width), BF),
            jax.ShapeDtypeStruct(shape, BF),
            jax.ShapeDtypeStruct(shape, BF),
        ],
        compiler_params=pltpu.CompilerParams(vmem_limit_bytes=VMEM_BYTES),
        name="attention",
    )(
        counts,
        core,
        normed,
        base,
        weights,
        queries.reshape(groups, GROUP * rows, width),
        cand_t.reshape(pairs, 2, width // (2 * pairs), total),
        mask,
        score_weight,
        own,
        labels,
    )


def shift(array, side, dx, dy):
    moves = []
    for x in range(side):
        for y in range(side):
            moves.append(((x + dx) % side * side + (y + dy) % side, x * side + y))
    return lax.ppermute(array, "user", moves)


def spread(piece, side, x_first):
    first = lambda a, d: shift(a, side, d, 0) if x_first else shift(a, side, 0, d)
    second = lambda a, d: shift(a, side, 0, d) if x_first else shift(a, side, d, 0)
    low = jnp.stack([piece, first(piece, 1)])
    high = jnp.stack([first(piece, 2), first(piece, -1)])
    low_after, high_before = second(low, 1), second(high, -1)
    high_after, low_before = second(high, 1), second(low, -1)
    low_two, high_two = second(low_after, 1), second(high_before, -1)
    return (low, high, low_after, high_after, low_two, high_two, low_before, high_before)


def join_kernel(left, right, out):
    wide = left.shape[1]
    out[:, :wide] = left[...]
    out[:, wide:] = right[...]


def join(left, right):
    return pl.pallas_call(
        join_kernel,
        out_shape=jax.ShapeDtypeStruct((left.shape[0], left.shape[1] + right.shape[1]), left.dtype),
        name="join",
    )(left, right)


def assemble_kernel(pieces, out):
    count, tall, wide = pieces.shape
    down = out.shape[0] // tall
    for k in range(count):
        a, b = k % down, k // down
        rows, cols = slice(a * tall, (a + 1) * tall), slice(b * wide, (b + 1) * wide)
        out[rows, cols] = pieces[k].astype(F32)


def assemble(pieces, right):
    count, tall, wide = pieces.shape
    return pl.pallas_call(
        assemble_kernel,
        out_shape=jax.ShapeDtypeStruct((count // right * tall, right * wide), F32),
        name="assemble",
    )(pieces)


def body(
    history_items,
    history_events,
    history_lengths,
    action_table,
    mix_weight,
    out_weight,
    query_weight,
    score_weight,
    self_weight,
    candidates,
    block_owner,
    row_counts,
    labels,
):
    users = lax.axis_size("user")
    loaders = lax.axis_size("loader")
    pairs = loaders // 2
    nblocks, rows, width = candidates.shape

    weights = lax.all_gather(join(mix_weight, out_weight), "loader", axis=0, tiled=True)
    actions = action_table.shape[0]
    packed = jnp.concatenate(
        [
            history_items[0],
            jnp.broadcast_to(history_events[0][:, None].astype(BF), (HIST, actions)),
            jnp.broadcast_to(history_lengths[0].astype(BF), (HIST, LANES - actions)),
        ],
        axis=1,
    )
    side = math.isqrt(users)
    half = HIST // 2
    halves_a = spread(packed[:half], side, True)
    halves_b = spread(packed[half:], side, False)

    flat = candidates.reshape(-1, width)
    queries = jnp.dot(flat, query_weight, preferred_element_type=F32).astype(BF)
    cand_t = flat.T
    own = jnp.sum(candidates.astype(F32) * self_weight, -1)

    owner = block_owner[:, 0]
    here = lax.axis_index("user").astype(jnp.int32)
    far_x = lax.rem(owner // side - here // side + side, side)
    far_y = lax.rem(lax.rem(owner, side) - lax.rem(here, side) + side, side)
    base, normed, mask = prepare(
        far_y * side + far_x, far_x * side + far_y, halves_a, halves_b, action_table
    )
    core = lax.rem(lax.axis_index("loader").astype(jnp.int32), 2)[None]
    scores, error, slopes, mine, other = attention(
        row_counts,
        core,
        normed,
        base,
        mask,
        weights,
        queries,
        cand_t,
        score_weight[None],
        own[:, None],
        labels[:, None],
        pairs,
        users,
    )

    arrived = lax.ppermute(other, "loader", [(i, i ^ 1) for i in range(loaders)])
    back = lax.dot_general(slopes, query_weight, (((1,), (1,)), ((), ())), preferred_element_type=F32)
    row_grads = (error.reshape(-1)[:, None] * self_weight + back).astype(BF)
    mine, row_grads = lax.optimization_barrier((mine, row_grads))
    pieces = (mine.astype(F32) + arrived.astype(F32)).astype(BF)
    pieces = lax.all_to_all(pieces, "user", 0, 0, tiled=True)
    pieces = jnp.sum(pieces.astype(F32), 0).astype(BF)
    groups = [[c + 2 * i for i in range(pairs)] for c in range(2)]
    pieces = lax.all_to_all(pieces, "loader", 0, 0, axis_index_groups=groups, tiled=True)
    piece = jnp.sum(pieces.astype(F32), 0).astype(BF)
    pieces = lax.all_to_all(
        jnp.broadcast_to(piece[None], (users,) + piece.shape), "user", 0, 0, tiled=True
    )
    query_grad = assemble(pieces, side)

    return (scores[:, 0], row_grads.reshape(nblocks, rows, width), query_grad)


def solution(mesh):
    placed = (
        P(("user", "loader"), None, None),
        P(("user", "loader"), None),
        P(("user", "loader")),
        P(),
        P("loader", None),
        P("loader", None),
        P(),
        P(),
        P(),
        P(("user", "loader"), None, None),
        P(("user", "loader"), None),
        P(("user", "loader")),
        P(("user", "loader"), None),
    )
    return jax.shard_map(
        body,
        mesh=mesh,
        in_specs=placed,
        out_specs=(
            P(("user", "loader"), None),
            P(("user", "loader"), None, None),
            P("loader", None),
        ),
        check_vma=False,
    )
```

```python
import functools
import math

import jax
import jax.numpy as jnp
from jax import lax
from jax.experimental import pallas as pl
from jax.experimental.pallas import tpu as pltpu
from jax.sharding import PartitionSpec as P

HEADS = 8
HIST = 128
LANES = 128
BF = jnp.bfloat16
F32 = jnp.float32
VMEM_BYTES = 56 * 1024 * 1024


def sigmoid(v):
    return 0.5 * jnp.tanh(0.5 * v) + 0.5


def dot(a, b):
    return jnp.dot(a, b, preferred_element_type=F32)


def dot_t(a, b):
    return lax.dot_general(a, b, (((1,), (1,)), ((), ())), preferred_element_type=F32)


def split3(v):
    high = v.astype(BF)
    rest = v - high.astype(F32)
    middle = rest.astype(BF)
    low = (rest - middle.astype(F32)).astype(BF)
    return high, middle, low


def prepare_kernel(nblocks, place_a, place_b, *refs):
    count = (len(refs) - 6) // 2
    halves = ((place_a, refs[:count]), (place_b, refs[count : 2 * count]))
    table, base, normed, mask, rows_s, sems = refs[2 * count :]
    block = pl.program_id(0)
    width = base.shape[1]
    actions = table.shape[0]
    half = HIST // 2

    def fetch(which, b, source):
        return pltpu.make_async_copy(
            source, rows_s.at[b, pl.ds(which * half, half)], sems.at[which, b]
        )

    @pl.when(block == 0)
    def _():
        for b in range(nblocks):
            for which, (place, arrays) in enumerate(halves):
                for k, array in enumerate(arrays):

                    @pl.when(place[b] // 2 == k)
                    def _():
                        fetch(which, b, array.at[lax.rem(place[b], 2)]).start()

    for which, (place, arrays) in enumerate(halves):
        fetch(which, block, arrays[0].at[0]).wait()
    rows = rows_s[block]
    tail = rows[:, width:].astype(F32)
    lane = lax.broadcasted_iota(jnp.int32, (HIST, actions), 1).astype(F32)
    onehot = jnp.where(tail[:, :actions] == lane, 1.0, 0.0).astype(BF)
    value = rows[:, :width].astype(F32)
    high, middle, low = split3(table[...])
    value = value + ((dot(onehot, low) + dot(onehot, middle)) + dot(onehot, high))
    scale = lax.rsqrt(jnp.mean(value * value, -1, keepdims=True) + 1e-06)
    base[...] = value
    normed[...] = (value * scale).astype(BF)
    position = lax.broadcasted_iota(jnp.int32, (HIST, LANES), 0).astype(F32)
    mask[...] = jnp.where(position < tail[:, LANES - 1 :], 1.0, 0.0)


def prepare(place_a, place_b, halves_a, halves_b, table):
    nblocks = place_a.shape[0]
    width = table.shape[1]
    total = nblocks * HIST
    arrays = list(halves_a) + list(halves_b)
    return pl.pallas_call(
        functools.partial(prepare_kernel, nblocks),
        grid_spec=pltpu.PrefetchScalarGridSpec(
            num_scalar_prefetch=2,
            grid=(nblocks,),
            in_specs=[pl.BlockSpec(memory_space=pl.ANY)] * len(arrays)
            + [pl.BlockSpec(table.shape, lambda b, p, q: (0, 0))],
            out_specs=[
                pl.BlockSpec((HIST, width), lambda b, p, q: (b, 0)),
                pl.BlockSpec((HIST, width), lambda b, p, q: (b, 0)),
                pl.BlockSpec((HIST, LANES), lambda b, p, q: (b, 0)),
            ],
            scratch_shapes=[
                pltpu.VMEM((nblocks, HIST, arrays[0].shape[-1]), BF),
                pltpu.SemaphoreType.DMA((2, nblocks)),
            ],
        ),
        out_shape=[
            jax.ShapeDtypeStruct((total, width), F32),
            jax.ShapeDtypeStruct((total, width), BF),
            jax.ShapeDtypeStruct((total, LANES), F32),
        ],
        compiler_params=pltpu.CompilerParams(vmem_limit_bytes=VMEM_BYTES),
        name="prepare",
    )(place_a, place_b, *arrays, table)


ENCODE_STEPS = HEADS // 2
GROUP = 2


def attention_kernel(
    pairs,
    counts,
    core,
    *refs,
):
    shards = refs[:pairs], refs[pairs : 2 * pairs]
    attention_steps(pairs, shards, counts, core, *refs[2 * pairs :])


def attention_steps(
    pairs,
    shards,
    counts,
    core,
    normed,
    base,
    queries,
    cand_t,
    mask,
    score_weight,
    own,
    labels,
    scores,
    error,
    slopes,
    mine,
    other,
    normed_s,
    base_s,
    mix_s,
    out_s,
    queries_s,
    cand_s,
    gate_s,
    mixed_s,
    qkv_s,
    gated_s,
    encoded_s,
    logit_s,
    weight_s,
    slope_s,
    mine_s,
    other_s,
    sems,
    mix_sems,
    out_sems,
    grad_sems,
):
    step = pl.program_id(0)
    total, width = normed_s.shape
    pair = 2 * LANES

    piece = shards[0][0].shape[1]

    def starts():
        for k in range(2):
            for d in range(pairs):
                which = jnp.where(k == 0, core[0], 1 - core[0])
                start = (2 * lax.rem(core[1] + d, pairs) + which) * piece
                yield 2 * d + k, shards[k][d], pl.multiple_of(start, piece)

    def mix_copies(i):
        cols = pl.ds(pl.multiple_of(i * pair, pair), pair)
        return [
            pltpu.make_async_copy(
                shard.at[pl.ds(0, 4), :, cols],
                mix_s.at[i, :, pl.ds(start, piece)],
                mix_sems.at[i, n],
            )
            for n, shard, start in starts()
        ]

    def out_copies():
        return [
            pltpu.make_async_copy(shard.at[4], out_s.at[pl.ds(start, piece)], out_sems.at[n])
            for n, shard, start in starts()
        ]

    normed_copy = pltpu.make_async_copy(normed, normed_s, sems.at[0])
    base_copy = pltpu.make_async_copy(base, base_s, sems.at[1])
    query_copy = pltpu.make_async_copy(queries, queries_s, sems.at[3])
    cand_copy = pltpu.make_async_copy(cand_t, cand_s, sems.at[4])

    @pl.when(step == 0)
    def _():
        normed_copy.start()
        for copy in mix_copies(0):
            copy.start()
        normed_copy.wait()

    @pl.when(step < ENCODE_STEPS)
    def _():
        for copy in mix_copies(step):
            copy.wait()

        @pl.when(step + 1 < ENCODE_STEPS)
        def _():
            for copy in mix_copies(step + 1):
                copy.start()

        @pl.when(step == 1)
        def _():
            base_copy.start()

        @pl.when(step == 2)
        def _():
            for copy in out_copies():
                copy.start()

        @pl.when(step == 3)
        def _():
            query_copy.start()
            cand_copy.start()

        users = total // HIST
        for k in range(2):
            cols = slice(k * LANES, (k + 1) * LANES)
            columns = jnp.concatenate([mix_s[step, g, :, cols] for g in range(4)], axis=1)
            projected = dot(normed_s[...], columns)
            projected = projected * sigmoid(projected)
            gate_s[2 * step + k] = projected[:, :LANES]
            qkv_s[k] = projected[:, LANES:].astype(BF)
        units = [(k, slice(u * HIST, (u + 1) * HIST)) for k in range(2) for u in range(users)]
        for n, (k, part) in enumerate(units):
            logit_s[n] = dot_t(qkv_s[k, part, LANES : 2 * LANES], qkv_s[k, part, 2 * LANES :])
        row = lax.broadcasted_iota(jnp.int32, (HIST, HIST), 0)
        column = lax.broadcasted_iota(jnp.int32, (HIST, HIST), 1)
        causal = column <= row
        for n in range(len(units)):
            logits = logit_s[n] * (1.0 / math.sqrt(LANES))
            weight = jnp.where(causal, logits * sigmoid(logits) * (1.0 / HIST), 0.0)
            weight_s[n] = weight.astype(BF)
        for n, (k, part) in enumerate(units):
            mixed_s[2 * step + k, part] = dot(weight_s[n], qkv_s[k, part, :LANES])

    @pl.when(step == ENCODE_STEPS - 1)
    def _():
        square = mixed_s[0] * mixed_s[0]
        for h in range(1, HEADS):
            square = square + mixed_s[h] * mixed_s[h]
        scale = lax.rsqrt(jnp.sum(square, -1, keepdims=True) * (1.0 / width) + 1e-06)
        for h in range(HEADS):
            gated_s[:, h * LANES : (h + 1) * LANES] = (mixed_s[h] * scale * gate_s[h]).astype(BF)
        active = mask[:, :1] > 0.0
        base_copy.wait()
        for copy in out_copies():
            copy.wait()
        for n in range(width // pair):
            cols = slice(n * pair, (n + 1) * pair)
            value = base_s[:, cols] + dot(gated_s[...], out_s[:, cols])
            value = jnp.where(active, value, 0.0).astype(BF)
            encoded_s[:, :, cols] = value.reshape(total // (GROUP * HIST), GROUP * HIST, pair)
        query_copy.wait()
        cand_copy.wait()

    @pl.when(step >= ENCODE_STEPS)
    def _():
        now = step - ENCODE_STEPS
        lane = lax.broadcasted_iota(jnp.int32, (HEADS, width), 1) // LANES
        head_row = lax.broadcasted_iota(jnp.int32, (HEADS, width), 0)
        spread_weight = jnp.where(lane == head_row, score_weight[...], 0.0)
        high, middle, low = split3(spread_weight)
        parts = [slice(g * HIST, (g + 1) * HIST) for g in range(GROUP)]
        units = [(h, g) for g in range(GROUP) for h in range(HEADS)]
        heads = [slice(h * LANES, (h + 1) * LANES) for h in range(HEADS)]
        for n, (h, g) in enumerate(units):
            logit_s[n] = dot_t(
                queries_s[now, parts[g], heads[h]], encoded_s[now, parts[g], heads[h]]
            )
        along = []
        for part in parts:
            keys = encoded_s[now, part]
            along.append((dot_t(low, keys) + dot_t(middle, keys)) + dot_t(high, keys))
        totals = [jnp.zeros((HIST, HIST), F32) for _ in range(GROUP)]
        for n, (h, g) in enumerate(units):
            row = along[g][h : h + 1]
            logits = logit_s[n] * (1.0 / math.sqrt(LANES))
            gate = sigmoid(logits)
            product = logits * gate
            weight = (product * (1.0 / HIST)).astype(BF).astype(F32)
            totals[g] = totals[g] + weight * row
            slope = gate + product * (1.0 - gate)
            weight_s[n] = (slope * (row * (1.0 / (HIST * math.sqrt(LANES))))).astype(BF)
        for n, (h, g) in enumerate(units):
            logit_s[n] = dot(weight_s[n], encoded_s[now, parts[g], heads[h]])
        for g, part in enumerate(parts):
            partial = jnp.sum(totals[g], -1, keepdims=True).astype(BF).astype(F32)
            partial_row = jnp.broadcast_to(partial, (HIST, HIST)).T[:1]
            active = lax.broadcasted_iota(jnp.int32, (1, HIST), 1) < counts[now * GROUP + g]
            score = jnp.where(active, partial_row + own[g], 0.0)
            err = jnp.where(active, sigmoid(score) - labels[g], 0.0)
            scores[g] = score
            error[g] = err
            err_rows = jnp.broadcast_to(err, (HIST, HIST)).T
            for h in range(HEADS):
                direction = logit_s[g * HEADS + h].astype(BF).astype(F32)
                slope = (err_rows * direction).astype(BF)
                slopes[part, heads[h]] = slope
                slope_s[now, part, heads[h]] = slope

    @pl.when(step == pl.num_programs(0) - 1)
    def _():
        _, pairs, tall, wide = mine.shape
        right = width // wide
        down = mine.shape[0] // right
        tall_piece = tall * down
        copies = []
        for n in range(right):
            cols = slice(n * wide, (n + 1) * wide)
            slope = slope_s[:, :, cols].reshape(-1, wide)
            for which, store in ((core[0], mine_s), (1 - core[0], other_s)):
                rows = cand_s[:, which].reshape(pairs * tall_piece, -1)
                grad = dot(rows, slope).astype(BF)
                for p in range(pairs):
                    for a in range(down):
                        start = p * tall_piece + a * tall
                        store[n * down + a, p] = grad[start : start + tall]
            chunk = pl.ds(n * down, down)
            for k, (source, target) in enumerate(((mine_s, mine), (other_s, other))):
                copy = pltpu.make_async_copy(
                    source.at[chunk], target.at[chunk], grad_sems.at[k, n]
                )
                copy.start()
                copies.append(copy)
        for copy in copies:
            copy.wait()


def attention(
    counts,
    core,
    normed,
    base,
    mask,
    shards,
    other_shards,
    queries,
    cand_t,
    score_weight,
    own,
    labels,
    pairs,
    users,
):
    nblocks = counts.shape[0]
    total, width = queries.shape
    rows = total // nblocks
    groups = nblocks // GROUP
    side = math.isqrt(users)
    shape = (users, pairs, width // (2 * pairs * side), width // side)
    current = lambda i: jnp.maximum(i - ENCODE_STEPS, 0)
    row = pl.BlockSpec((GROUP, 1, rows), lambda i, n, c: (current(i), 0, 0))
    whole = lambda i, n, c: (0, 0)
    anywhere = pl.BlockSpec(memory_space=pl.ANY)
    return pl.pallas_call(
        functools.partial(attention_kernel, pairs),
        grid_spec=pltpu.PrefetchScalarGridSpec(
            num_scalar_prefetch=2,
            grid=(ENCODE_STEPS + groups,),
            in_specs=[anywhere] * (2 * pairs + 4)
            + [
                pl.BlockSpec((total, LANES), whole),
                pl.BlockSpec((1, width), whole),
                row,
                row,
            ],
            out_specs=[
                row,
                row,
                pl.BlockSpec((GROUP * rows, width), lambda i, n, c: (current(i), 0)),
                anywhere,
                anywhere,
            ],
            scratch_shapes=[
                pltpu.VMEM((total, width), BF),
                pltpu.VMEM((total, width), F32),
                pltpu.VMEM((ENCODE_STEPS, 4, width, 2 * LANES), BF),
                pltpu.VMEM((width, width), BF),
                pltpu.VMEM((groups, GROUP * rows, width), BF),
                pltpu.VMEM((pairs, 2, width // (2 * pairs), total), BF),
                pltpu.VMEM((HEADS, total, LANES), F32),
                pltpu.VMEM((HEADS, total, LANES), F32),
                pltpu.VMEM((2, total, 3 * LANES), BF),
                pltpu.VMEM((total, width), BF),
                pltpu.VMEM((groups, GROUP * rows, width), BF),
                pltpu.VMEM((GROUP * HEADS, HIST, HIST), F32),
                pltpu.VMEM((GROUP * HEADS, HIST, HIST), BF),
                pltpu.VMEM((groups, GROUP * rows, width), BF),
                pltpu.VMEM(shape, BF),
                pltpu.VMEM(shape, BF),
                pltpu.SemaphoreType.DMA((5,)),
                pltpu.SemaphoreType.DMA((ENCODE_STEPS, 2 * pairs)),
                pltpu.SemaphoreType.DMA((2 * pairs,)),
                pltpu.SemaphoreType.DMA((2, side)),
            ],
        ),
        out_shape=[
            jax.ShapeDtypeStruct((nblocks, 1, rows), F32),
            jax.ShapeDtypeStruct((nblocks, 1, rows), F32),
            jax.ShapeDtypeStruct((total, width), BF),
            jax.ShapeDtypeStruct(shape, BF),
            jax.ShapeDtypeStruct(shape, BF),
        ],
        compiler_params=pltpu.CompilerParams(vmem_limit_bytes=VMEM_BYTES),
        name="attention",
    )(
        counts,
        core,
        *shards,
        *other_shards,
        normed,
        base,
        queries.reshape(groups, GROUP * rows, width),
        cand_t.reshape(pairs, 2, width // (2 * pairs), total),
        mask,
        score_weight,
        own,
        labels,
    )


def shift(array, side, dx, dy):
    moves = []
    for x in range(side):
        for y in range(side):
            moves.append(((x + dx) % side * side + (y + dy) % side, x * side + y))
    return lax.ppermute(array, "user", moves)


def travel(piece, shard, side, loaders):
    along_x = lambda a, d: shift(a, side, d, 0)
    along_y = lambda a, d: shift(a, side, 0, d)
    along_z = lambda a, d: lax.ppermute(
        a, "loader", [((i + 2 * d) % loaders, i) for i in range(loaders)]
    )
    swap = lambda a: lax.ppermute(a, "loader", [(i, i ^ 1) for i in range(loaders)])
    half = piece.shape[0] // 2
    halves = ((piece[:half], along_x, along_y), (piece[half:], along_y, along_x))
    pairs = loaders // 2

    after, before = [shard], [shard]
    after.append(along_z(shard, 1))
    before.append(along_z(shard, -1))
    near = [[first(p, d) for d in (1, 2, -1)] for p, first, _ in halves]
    others = [swap(shard)]
    after, before, near, others = lax.optimization_barrier((after, before, near, others))

    after.append(along_z(after[1], 1))
    before.append(along_z(before[1], -1))
    results = []
    for (p, _, second), (one, two, three) in zip(halves, near):
        low, high = jnp.stack([p, one]), jnp.stack([two, three])
        results.append([low, high, second(low, 1), second(high, 1), second(low, -1), second(high, -1)])
    after, before, results = lax.optimization_barrier((after, before, results))

    after.append(along_z(after[2], 1))
    before.append(along_z(before[2], -1))
    spreads = []
    for (p, _, second), (low, high, low1, high1, low3, high3) in zip(halves, results):
        spreads.append((low, high, low1, high1, second(low1, 1), second(high3, -1), low3, high3))
    others_after = [swap(a) for a in after[1:3]]
    others_before = [swap(a) for a in before[1:3]]
    after, before, spreads, others_after, others_before = lax.optimization_barrier(
        (after, before, spreads, others_after, others_before)
    )
    cut = (shard.shape[0] + 1) // 2
    middle = jnp.concatenate([along_z(after[3][:cut], 1), along_z(before[3][cut:], -1)])
    others_after.append(swap(after[3]))
    others_before.append(swap(before[3]))
    own = after + [middle] + before[:0:-1]
    others = others + others_after + [swap(middle)] + others_before[::-1]
    assert len(own) == pairs and len(others) == pairs
    return spreads[0], spreads[1], own, others


def join_kernel(left, right, out):
    wide = right.shape[1]
    for g in range(out.shape[0] - 1):
        out[g] = left[:, g * wide : (g + 1) * wide]
    out[out.shape[0] - 1] = right[...]


def join(left, right):
    groups = left.shape[1] // right.shape[1] + 1
    return pl.pallas_call(
        join_kernel,
        out_shape=jax.ShapeDtypeStruct((groups,) + right.shape, left.dtype),
        name="join",
    )(left, right)


def assemble_kernel(pieces, out):
    count, tall, wide = pieces.shape
    down = out.shape[0] // tall
    for k in range(count):
        a, b = k % down, k // down
        rows, cols = slice(a * tall, (a + 1) * tall), slice(b * wide, (b + 1) * wide)
        out[rows, cols] = pieces[k].astype(F32)


def assemble(pieces, right):
    count, tall, wide = pieces.shape
    return pl.pallas_call(
        assemble_kernel,
        out_shape=jax.ShapeDtypeStruct((count // right * tall, right * wide), F32),
        name="assemble",
    )(pieces)


def body(
    history_items,
    history_events,
    history_lengths,
    action_table,
    mix_weight,
    out_weight,
    query_weight,
    score_weight,
    self_weight,
    candidates,
    block_owner,
    row_counts,
    labels,
):
    users = lax.axis_size("user")
    loaders = lax.axis_size("loader")
    pairs = loaders // 2
    nblocks, rows, width = candidates.shape

    actions = action_table.shape[0]
    packed = jnp.concatenate(
        [
            history_items[0],
            jnp.broadcast_to(history_events[0][:, None].astype(BF), (HIST, actions)),
            jnp.broadcast_to(history_lengths[0].astype(BF), (HIST, LANES - actions)),
        ],
        axis=1,
    )
    side = math.isqrt(users)
    half = HIST // 2
    halves_a, halves_b, shards, other_shards = travel(
        packed, join(mix_weight, out_weight), side, loaders
    )

    flat = candidates.reshape(-1, width)
    queries = jnp.dot(flat, query_weight, preferred_element_type=F32).astype(BF)
    cand_t = flat.T
    own = jnp.sum(candidates.astype(F32) * self_weight, -1)

    owner = block_owner[:, 0]
    here = lax.axis_index("user").astype(jnp.int32)
    far_x = lax.rem(owner // side - here // side + side, side)
    far_y = lax.rem(lax.rem(owner, side) - lax.rem(here, side) + side, side)
    base, normed, mask = prepare(
        far_y * side + far_x, far_x * side + far_y, halves_a, halves_b, action_table
    )
    loader = lax.axis_index("loader").astype(jnp.int32)
    place = jnp.stack([lax.rem(loader, 2), loader // 2])
    scores, error, slopes, mine, other = attention(
        row_counts,
        place,
        normed,
        base,
        mask,
        shards,
        other_shards,
        queries,
        cand_t,
        score_weight[None],
        own[:, None],
        labels[:, None],
        pairs,
        users,
    )

    arrived = lax.ppermute(other, "loader", [(i, i ^ 1) for i in range(loaders)])
    pieces = (mine.astype(F32) + arrived.astype(F32)).astype(BF)
    pieces = lax.all_to_all(pieces, "user", 0, 0, tiled=True)
    pieces = jnp.sum(pieces.astype(F32), 0).astype(BF)
    groups = [[c + 2 * i for i in range(pairs)] for c in range(2)]
    pieces = lax.all_to_all(pieces, "loader", 0, 0, axis_index_groups=groups, tiled=True)
    piece = jnp.sum(pieces.astype(F32), 0).astype(BF)
    pieces = lax.all_to_all(
        jnp.broadcast_to(piece[None], (users,) + piece.shape), "user", 0, 0, tiled=True
    )
    query_grad = assemble(pieces, side)

    back = lax.dot_general(slopes, query_weight, (((1,), (1,)), ((), ())), preferred_element_type=F32)
    row_grads = (error.reshape(-1)[:, None] * self_weight + back).astype(BF)
    return (scores[:, 0], row_grads.reshape(nblocks, rows, width), query_grad)


def solution(mesh):
    placed = (
        P(("user", "loader"), None, None),
        P(("user", "loader"), None),
        P(("user", "loader")),
        P(),
        P("loader", None),
        P("loader", None),
        P(),
        P(),
        P(),
        P(("user", "loader"), None, None),
        P(("user", "loader"), None),
        P(("user", "loader")),
        P(("user", "loader"), None),
    )
    return jax.shard_map(
        body,
        mesh=mesh,
        in_specs=placed,
        out_specs=(
            P(("user", "loader"), None),
            P(("user", "loader"), None, None),
            P("loader", None),
        ),
        check_vma=False,
    )
```

```python
import functools
import math

import jax
import jax.numpy as jnp
from jax import lax
from jax.experimental import pallas as pl
from jax.experimental.pallas import tpu as pltpu
from jax.sharding import PartitionSpec as P

HEADS = 8
HIST = 128
LANES = 128
BF = jnp.bfloat16
F32 = jnp.float32
VMEM_BYTES = 56 * 1024 * 1024


def sigmoid(v):
    return 0.5 * jnp.tanh(0.5 * v) + 0.5


def dot(a, b):
    return jnp.dot(a, b, preferred_element_type=F32)


def dot_t(a, b):
    return lax.dot_general(a, b, (((1,), (1,)), ((), ())), preferred_element_type=F32)


def split3(v):
    high = v.astype(BF)
    rest = v - high.astype(F32)
    middle = rest.astype(BF)
    low = (rest - middle.astype(F32)).astype(BF)
    return high, middle, low


def prepare_kernel(nblocks, place_a, place_b, *refs):
    count = (len(refs) - 6) // 2
    halves = ((place_a, refs[:count]), (place_b, refs[count : 2 * count]))
    table, base, normed, mask, rows_s, sems = refs[2 * count :]
    block = pl.program_id(0)
    width = base.shape[1]
    actions = table.shape[0]
    half = HIST // 2

    def fetch(which, b, source):
        return pltpu.make_async_copy(
            source, rows_s.at[b, pl.ds(which * half, half)], sems.at[which, b]
        )

    @pl.when(block == 0)
    def _():
        for b in range(nblocks):
            for which, (place, arrays) in enumerate(halves):
                for k, array in enumerate(arrays):

                    @pl.when(place[b] // 2 == k)
                    def _():
                        fetch(which, b, array.at[lax.rem(place[b], 2)]).start()

    for which, (place, arrays) in enumerate(halves):
        fetch(which, block, arrays[0].at[0]).wait()
    rows = rows_s[block]
    tail = rows[:, width:].astype(F32)
    lane = lax.broadcasted_iota(jnp.int32, (HIST, actions), 1).astype(F32)
    onehot = jnp.where(tail[:, :actions] == lane, 1.0, 0.0).astype(BF)
    value = rows[:, :width].astype(F32)
    high, middle, low = split3(table[...])
    value = value + ((dot(onehot, low) + dot(onehot, middle)) + dot(onehot, high))
    scale = lax.rsqrt(jnp.mean(value * value, -1, keepdims=True) + 1e-06)
    base[...] = value
    normed[...] = (value * scale).astype(BF)
    position = lax.broadcasted_iota(jnp.int32, (HIST, LANES), 0).astype(F32)
    mask[...] = jnp.where(position < tail[:, LANES - 1 :], 1.0, 0.0)


def prepare(place_a, place_b, halves_a, halves_b, table):
    nblocks = place_a.shape[0]
    width = table.shape[1]
    total = nblocks * HIST
    arrays = list(halves_a) + list(halves_b)
    return pl.pallas_call(
        functools.partial(prepare_kernel, nblocks),
        grid_spec=pltpu.PrefetchScalarGridSpec(
            num_scalar_prefetch=2,
            grid=(nblocks,),
            in_specs=[pl.BlockSpec(memory_space=pl.ANY)] * len(arrays)
            + [pl.BlockSpec(table.shape, lambda b, p, q: (0, 0))],
            out_specs=[
                pl.BlockSpec((HIST, width), lambda b, p, q: (b, 0)),
                pl.BlockSpec((HIST, width), lambda b, p, q: (b, 0)),
                pl.BlockSpec((HIST, LANES), lambda b, p, q: (b, 0)),
            ],
            scratch_shapes=[
                pltpu.VMEM((nblocks, HIST, arrays[0].shape[-1]), BF),
                pltpu.SemaphoreType.DMA((2, nblocks)),
            ],
        ),
        out_shape=[
            jax.ShapeDtypeStruct((total, width), F32),
            jax.ShapeDtypeStruct((total, width), BF),
            jax.ShapeDtypeStruct((total, LANES), F32),
        ],
        compiler_params=pltpu.CompilerParams(vmem_limit_bytes=VMEM_BYTES),
        name="prepare",
    )(place_a, place_b, *arrays, table)


ENCODE_STEPS = HEADS // 2
GROUP = 2


def attention_kernel(
    counts,
    core,
    normed,
    base,
    weights,
    queries,
    cand_t,
    mask,
    score_weight,
    own,
    labels,
    scores,
    error,
    slopes,
    mine,
    other,
    normed_s,
    base_s,
    mix_s,
    out_s,
    queries_s,
    cand_s,
    gate_s,
    mixed_s,
    qkv_s,
    gated_s,
    encoded_s,
    logit_s,
    weight_s,
    slope_s,
    mine_s,
    other_s,
    sems,
    mix_sems,
    grad_sems,
):
    step = pl.program_id(0)
    total, width = normed_s.shape
    pair = 2 * LANES

    def mix_copy(i, group):
        start = pl.multiple_of(group * width + i * pair, pair)
        return pltpu.make_async_copy(
            weights.at[:, pl.ds(start, pair)], mix_s.at[i, group], mix_sems.at[i, group]
        )

    normed_copy = pltpu.make_async_copy(normed, normed_s, sems.at[0])
    base_copy = pltpu.make_async_copy(base, base_s, sems.at[1])
    out_copy = pltpu.make_async_copy(weights.at[:, pl.ds(4 * width, width)], out_s, sems.at[2])
    query_copy = pltpu.make_async_copy(queries, queries_s, sems.at[3])
    cand_copy = pltpu.make_async_copy(cand_t, cand_s, sems.at[4])

    @pl.when(step == 0)
    def _():
        normed_copy.start()
        for group in range(4):
            mix_copy(0, group).start()
        normed_copy.wait()

    @pl.when(step < ENCODE_STEPS)
    def _():
        for group in range(4):
            mix_copy(step, group).wait()

        @pl.when(step + 1 < ENCODE_STEPS)
        def _():
            for group in range(4):
                mix_copy(step + 1, group).start()

        @pl.when(step == 1)
        def _():
            base_copy.start()

        @pl.when(step == 2)
        def _():
            out_copy.start()

        @pl.when(step == 3)
        def _():
            query_copy.start()
            cand_copy.start()

        users = total // HIST
        for k in range(2):
            cols = slice(k * LANES, (k + 1) * LANES)
            columns = jnp.concatenate([mix_s[step, g, :, cols] for g in range(4)], axis=1)
            projected = dot(normed_s[...], columns)
            projected = projected * sigmoid(projected)
            gate_s[2 * step + k] = projected[:, :LANES]
            qkv_s[k] = projected[:, LANES:].astype(BF)
        units = [(k, slice(u * HIST, (u + 1) * HIST)) for k in range(2) for u in range(users)]
        for n, (k, part) in enumerate(units):
            logit_s[n] = dot_t(qkv_s[k, part, LANES : 2 * LANES], qkv_s[k, part, 2 * LANES :])
        row = lax.broadcasted_iota(jnp.int32, (HIST, HIST), 0)
        column = lax.broadcasted_iota(jnp.int32, (HIST, HIST), 1)
        causal = column <= row
        for n in range(len(units)):
            logits = logit_s[n] * (1.0 / math.sqrt(LANES))
            weight = jnp.where(causal, logits * sigmoid(logits) * (1.0 / HIST), 0.0)
            weight_s[n] = weight.astype(BF)
        for n, (k, part) in enumerate(units):
            mixed_s[2 * step + k, part] = dot(weight_s[n], qkv_s[k, part, :LANES])

    @pl.when(step == ENCODE_STEPS - 1)
    def _():
        square = mixed_s[0] * mixed_s[0]
        for h in range(1, HEADS):
            square = square + mixed_s[h] * mixed_s[h]
        scale = lax.rsqrt(jnp.sum(square, -1, keepdims=True) * (1.0 / width) + 1e-06)
        for h in range(HEADS):
            gated_s[:, h * LANES : (h + 1) * LANES] = (mixed_s[h] * scale * gate_s[h]).astype(BF)
        active = mask[:, :1] > 0.0
        base_copy.wait()
        out_copy.wait()
        for n in range(width // pair):
            cols = slice(n * pair, (n + 1) * pair)
            value = base_s[:, cols] + dot(gated_s[...], out_s[:, cols])
            value = jnp.where(active, value, 0.0).astype(BF)
            encoded_s[:, :, cols] = value.reshape(total // (GROUP * HIST), GROUP * HIST, pair)
        query_copy.wait()
        cand_copy.wait()

    @pl.when(step >= ENCODE_STEPS)
    def _():
        now = step - ENCODE_STEPS
        lane = lax.broadcasted_iota(jnp.int32, (HEADS, width), 1) // LANES
        head_row = lax.broadcasted_iota(jnp.int32, (HEADS, width), 0)
        spread_weight = jnp.where(lane == head_row, score_weight[...], 0.0)
        high, middle, low = split3(spread_weight)
        parts = [slice(g * HIST, (g + 1) * HIST) for g in range(GROUP)]
        units = [(h, g) for g in range(GROUP) for h in range(HEADS)]
        heads = [slice(h * LANES, (h + 1) * LANES) for h in range(HEADS)]
        for n, (h, g) in enumerate(units):
            logit_s[n] = dot_t(
                queries_s[now, parts[g], heads[h]], encoded_s[now, parts[g], heads[h]]
            )
        along = []
        for part in parts:
            keys = encoded_s[now, part]
            along.append((dot_t(low, keys) + dot_t(middle, keys)) + dot_t(high, keys))
        totals = [jnp.zeros((HIST, HIST), F32) for _ in range(GROUP)]
        for n, (h, g) in enumerate(units):
            row = along[g][h : h + 1]
            logits = logit_s[n] * (1.0 / math.sqrt(LANES))
            gate = sigmoid(logits)
            product = logits * gate
            weight = (product * (1.0 / HIST)).astype(BF).astype(F32)
            totals[g] = totals[g] + weight * row
            slope = gate + product * (1.0 - gate)
            weight_s[n] = (slope * (row * (1.0 / (HIST * math.sqrt(LANES))))).astype(BF)
        for n, (h, g) in enumerate(units):
            logit_s[n] = dot(weight_s[n], encoded_s[now, parts[g], heads[h]])
        for g, part in enumerate(parts):
            partial = jnp.sum(totals[g], -1, keepdims=True).astype(BF).astype(F32)
            partial_row = jnp.broadcast_to(partial, (HIST, HIST)).T[:1]
            active = lax.broadcasted_iota(jnp.int32, (1, HIST), 1) < counts[now * GROUP + g]
            score = jnp.where(active, partial_row + own[g], 0.0)
            err = jnp.where(active, sigmoid(score) - labels[g], 0.0)
            scores[g] = score
            error[g] = err
            err_rows = jnp.broadcast_to(err, (HIST, HIST)).T
            for h in range(HEADS):
                direction = logit_s[g * HEADS + h].astype(BF).astype(F32)
                slope = (err_rows * direction).astype(BF)
                slopes[part, heads[h]] = slope
                slope_s[now, part, heads[h]] = slope

    @pl.when(step == pl.num_programs(0) - 1)
    def _():
        _, pairs, tall, wide = mine.shape
        right = width // wide
        down = mine.shape[0] // right
        piece = tall * down
        copies = []
        for n in range(right):
            cols = slice(n * wide, (n + 1) * wide)
            slope = slope_s[:, :, cols].reshape(-1, wide)
            for which, store in ((core[0], mine_s), (1 - core[0], other_s)):
                rows = cand_s[:, which].reshape(pairs * piece, -1)
                grad = dot(rows, slope).astype(BF)
                for p in range(pairs):
                    for a in range(down):
                        start = p * piece + a * tall
                        store[n * down + a, p] = grad[start : start + tall]
            chunk = pl.ds(n * down, down)
            for k, (source, target) in enumerate(((mine_s, mine), (other_s, other))):
                copy = pltpu.make_async_copy(
                    source.at[chunk], target.at[chunk], grad_sems.at[k, n]
                )
                copy.start()
                copies.append(copy)
        for copy in copies:
            copy.wait()


def attention(
    counts,
    core,
    normed,
    base,
    mask,
    weights,
    queries,
    cand_t,
    score_weight,
    own,
    labels,
    pairs,
    users,
):
    nblocks = counts.shape[0]
    total, width = queries.shape
    rows = total // nblocks
    groups = nblocks // GROUP
    side = math.isqrt(users)
    shape = (users, pairs, width // (2 * pairs * side), width // side)
    current = lambda i: jnp.maximum(i - ENCODE_STEPS, 0)
    row = pl.BlockSpec((GROUP, 1, rows), lambda i, n, c: (current(i), 0, 0))
    whole = lambda i, n, c: (0, 0)
    anywhere = pl.BlockSpec(memory_space=pl.ANY)
    return pl.pallas_call(
        attention_kernel,
        grid_spec=pltpu.PrefetchScalarGridSpec(
            num_scalar_prefetch=2,
            grid=(ENCODE_STEPS + groups,),
            in_specs=[anywhere] * 5
            + [
                pl.BlockSpec((total, LANES), whole),
                pl.BlockSpec((1, width), whole),
                row,
                row,
            ],
            out_specs=[
                row,
                row,
                pl.BlockSpec((GROUP * rows, width), lambda i, n, c: (current(i), 0)),
                anywhere,
                anywhere,
            ],
            scratch_shapes=[
                pltpu.VMEM((total, width), BF),
                pltpu.VMEM((total, width), F32),
                pltpu.VMEM((ENCODE_STEPS, 4, width, 2 * LANES), BF),
                pltpu.VMEM((width, width), BF),
                pltpu.VMEM((groups, GROUP * rows, width), BF),
                pltpu.VMEM((pairs, 2, width // (2 * pairs), total), BF),
                pltpu.VMEM((HEADS, total, LANES), F32),
                pltpu.VMEM((HEADS, total, LANES), F32),
                pltpu.VMEM((2, total, 3 * LANES), BF),
                pltpu.VMEM((total, width), BF),
                pltpu.VMEM((groups, GROUP * rows, width), BF),
                pltpu.VMEM((GROUP * HEADS, HIST, HIST), F32),
                pltpu.VMEM((GROUP * HEADS, HIST, HIST), BF),
                pltpu.VMEM((groups, GROUP * rows, width), BF),
                pltpu.VMEM(shape, BF),
                pltpu.VMEM(shape, BF),
                pltpu.SemaphoreType.DMA((5,)),
                pltpu.SemaphoreType.DMA((ENCODE_STEPS, 4)),
                pltpu.SemaphoreType.DMA((2, side)),
            ],
        ),
        out_shape=[
            jax.ShapeDtypeStruct((nblocks, 1, rows), F32),
            jax.ShapeDtypeStruct((nblocks, 1, rows), F32),
            jax.ShapeDtypeStruct((total, width), BF),
            jax.ShapeDtypeStruct(shape, BF),
            jax.ShapeDtypeStruct(shape, BF),
        ],
        compiler_params=pltpu.CompilerParams(vmem_limit_bytes=42 * 1024 * 1024),
        name="attention",
    )(
        counts,
        core,
        normed,
        base,
        weights,
        queries.reshape(groups, GROUP * rows, width),
        cand_t.reshape(pairs, 2, width // (2 * pairs), total),
        mask,
        score_weight,
        own,
        labels,
    )


def shift(array, side, dx, dy):
    moves = []
    for x in range(side):
        for y in range(side):
            moves.append(((x + dx) % side * side + (y + dy) % side, x * side + y))
    return lax.ppermute(array, "user", moves)


def spread(piece, side, x_first):
    first = lambda a, d: shift(a, side, d, 0) if x_first else shift(a, side, 0, d)
    second = lambda a, d: shift(a, side, 0, d) if x_first else shift(a, side, d, 0)
    low = jnp.stack([piece, first(piece, 1)])
    high = jnp.stack([first(piece, 2), first(piece, -1)])
    low_after, high_before = second(low, 1), second(high, -1)
    high_after, low_before = second(high, 1), second(low, -1)
    low_two, high_two = second(low_after, 1), second(high_before, -1)
    return (low, high, low_after, high_after, low_two, high_two, low_before, high_before)


def join_kernel(left, right, out):
    wide = left.shape[1]
    out[:, :wide] = left[...]
    out[:, wide:] = right[...]


def join(left, right):
    return pl.pallas_call(
        join_kernel,
        out_shape=jax.ShapeDtypeStruct((left.shape[0], left.shape[1] + right.shape[1]), left.dtype),
        name="join",
    )(left, right)


def assemble_kernel(pieces, out):
    count, tall, wide = pieces.shape
    down = out.shape[0] // tall
    for k in range(count):
        a, b = k % down, k // down
        rows, cols = slice(a * tall, (a + 1) * tall), slice(b * wide, (b + 1) * wide)
        out[rows, cols] = pieces[k].astype(F32)


def assemble(pieces, right):
    count, tall, wide = pieces.shape
    return pl.pallas_call(
        assemble_kernel,
        out_shape=jax.ShapeDtypeStruct((count // right * tall, right * wide), F32),
        name="assemble",
    )(pieces)


def body(
    history_items,
    history_events,
    history_lengths,
    action_table,
    mix_weight,
    out_weight,
    query_weight,
    score_weight,
    self_weight,
    candidates,
    block_owner,
    row_counts,
    labels,
):
    users = lax.axis_size("user")
    loaders = lax.axis_size("loader")
    pairs = loaders // 2
    nblocks, rows, width = candidates.shape

    weights = lax.all_gather(join(mix_weight, out_weight), "loader", axis=0, tiled=True)
    actions = action_table.shape[0]
    packed = jnp.concatenate(
        [
            history_items[0],
            jnp.broadcast_to(history_events[0][:, None].astype(BF), (HIST, actions)),
            jnp.broadcast_to(history_lengths[0].astype(BF), (HIST, LANES - actions)),
        ],
        axis=1,
    )
    side = math.isqrt(users)
    half = HIST // 2
    halves_a = spread(packed[:half], side, True)
    halves_b = spread(packed[half:], side, False)

    flat = candidates.reshape(-1, width)
    queries = jnp.dot(flat, query_weight, preferred_element_type=F32).astype(BF)
    cand_t = flat.T
    own = jnp.sum(candidates.astype(F32) * self_weight, -1)

    owner = block_owner[:, 0]
    here = lax.axis_index("user").astype(jnp.int32)
    far_x = lax.rem(owner // side - here // side + side, side)
    far_y = lax.rem(lax.rem(owner, side) - lax.rem(here, side) + side, side)
    base, normed, mask = prepare(
        far_y * side + far_x, far_x * side + far_y, halves_a, halves_b, action_table
    )
    core = lax.rem(lax.axis_index("loader").astype(jnp.int32), 2)[None]
    scores, error, slopes, mine, other = attention(
        row_counts,
        core,
        normed,
        base,
        mask,
        weights,
        queries,
        cand_t,
        score_weight[None],
        own[:, None],
        labels[:, None],
        pairs,
        users,
    )

    arrived = lax.ppermute(other, "loader", [(i, i ^ 1) for i in range(loaders)])
    pieces = (mine.astype(F32) + arrived.astype(F32)).astype(BF)
    pieces = lax.all_to_all(pieces, "user", 0, 0, tiled=True)
    pieces = jnp.sum(pieces.astype(F32), 0).astype(BF)
    groups = [[c + 2 * i for i in range(pairs)] for c in range(2)]
    pieces = lax.all_to_all(pieces, "loader", 0, 0, axis_index_groups=groups, tiled=True)
    piece = jnp.sum(pieces.astype(F32), 0).astype(BF)
    pieces = lax.all_to_all(
        jnp.broadcast_to(piece[None], (users,) + piece.shape), "user", 0, 0, tiled=True
    )
    query_grad = assemble(pieces, side)

    back = lax.dot_general(slopes, query_weight, (((1,), (1,)), ((), ())), preferred_element_type=F32)
    row_grads = (error.reshape(-1)[:, None] * self_weight + back).astype(BF)
    return (scores[:, 0], row_grads.reshape(nblocks, rows, width), query_grad)


def solution(mesh):
    placed = (
        P(("user", "loader"), None, None),
        P(("user", "loader"), None),
        P(("user", "loader")),
        P(),
        P("loader", None),
        P("loader", None),
        P(),
        P(),
        P(),
        P(("user", "loader"), None, None),
        P(("user", "loader"), None),
        P(("user", "loader")),
        P(("user", "loader"), None),
    )
    return jax.shard_map(
        body,
        mesh=mesh,
        in_specs=placed,
        out_specs=(
            P(("user", "loader"), None),
            P(("user", "loader"), None, None),
            P("loader", None),
        ),
        check_vma=False,
    )
```

```python
import functools
import math

import jax
import jax.numpy as jnp
from jax import lax
from jax.experimental import pallas as pl
from jax.experimental.pallas import tpu as pltpu
from jax.sharding import PartitionSpec as P

HEADS = 8
HIST = 128
LANES = 128
BF = jnp.bfloat16
F32 = jnp.float32
VMEM_BYTES = 56 * 1024 * 1024


def sigmoid(v):
    return 0.5 * jnp.tanh(0.5 * v) + 0.5


def dot(a, b):
    return jnp.dot(a, b, preferred_element_type=F32)


def dot_t(a, b):
    return lax.dot_general(a, b, (((1,), (1,)), ((), ())), preferred_element_type=F32)


def split3(v):
    high = v.astype(BF)
    rest = v - high.astype(F32)
    middle = rest.astype(BF)
    low = (rest - middle.astype(F32)).astype(BF)
    return high, middle, low


def prepare_kernel(nblocks, place_a, place_b, *refs):
    count = (len(refs) - 5) // 2
    halves = ((place_a, refs[:count]), (place_b, refs[count : 2 * count]))
    table, base, normed, rows_s, sems = refs[2 * count :]
    block = pl.program_id(0)
    width = base.shape[1]
    actions = table.shape[0]
    half = HIST // 2

    def fetch(which, b, source):
        return pltpu.make_async_copy(
            source, rows_s.at[b, pl.ds(which * half, half)], sems.at[which, b]
        )

    @pl.when(block == 0)
    def _():
        for b in range(nblocks):
            for which, (place, arrays) in enumerate(halves):
                for k, array in enumerate(arrays):

                    @pl.when(place[b] // 2 == k)
                    def _():
                        fetch(which, b, array.at[lax.rem(place[b], 2)]).start()

    for which, (place, arrays) in enumerate(halves):
        fetch(which, block, arrays[0].at[0]).wait()
    rows = rows_s[block]
    tail = rows[:, width:].astype(F32)
    lane = lax.broadcasted_iota(jnp.int32, (HIST, actions), 1).astype(F32)
    onehot = jnp.where(tail[:, :actions] == lane, 1.0, 0.0).astype(BF)
    value = rows[:, :width].astype(F32)
    high, middle, low = split3(table[...])
    value = value + ((dot(onehot, low) + dot(onehot, middle)) + dot(onehot, high))
    position = lax.broadcasted_iota(jnp.int32, (HIST, 1), 0).astype(F32)
    value = jnp.where(position < tail[:, LANES - 1 :], value, 0.0)
    scale = lax.rsqrt(jnp.mean(value * value, -1, keepdims=True) + 1e-06)
    base[...] = value
    normed[...] = (value * scale).astype(BF)


def prepare(place_a, place_b, halves_a, halves_b, table):
    nblocks = place_a.shape[0]
    width = table.shape[1]
    total = nblocks * HIST
    arrays = list(halves_a) + list(halves_b)
    return pl.pallas_call(
        functools.partial(prepare_kernel, nblocks),
        grid_spec=pltpu.PrefetchScalarGridSpec(
            num_scalar_prefetch=2,
            grid=(nblocks,),
            in_specs=[pl.BlockSpec(memory_space=pl.ANY)] * len(arrays)
            + [pl.BlockSpec(table.shape, lambda b, p, q: (0, 0))],
            out_specs=[
                pl.BlockSpec((HIST, width), lambda b, p, q: (b, 0)),
                pl.BlockSpec((HIST, width), lambda b, p, q: (b, 0)),
            ],
            scratch_shapes=[
                pltpu.VMEM((nblocks, HIST, arrays[0].shape[-1]), BF),
                pltpu.SemaphoreType.DMA((2, nblocks)),
            ],
        ),
        out_shape=[
            jax.ShapeDtypeStruct((total, width), F32),
            jax.ShapeDtypeStruct((total, width), BF),
        ],
        compiler_params=pltpu.CompilerParams(vmem_limit_bytes=VMEM_BYTES),
        name="prepare",
    )(place_a, place_b, *arrays, table)


ENCODE_STEPS = HEADS // 2
GROUP = 2


def attention_kernel(
    counts,
    core,
    normed,
    base,
    weights,
    queries,
    cand_t,
    score_weight,
    own,
    labels,
    scores,
    error,
    slopes,
    mine,
    other,
    normed_s,
    base_s,
    mix_s,
    out_s,
    queries_s,
    cand_s,
    gate_s,
    mixed_s,
    qkv_s,
    gated_s,
    encoded_s,
    logit_s,
    weight_s,
    slope_s,
    mine_s,
    other_s,
    sems,
    mix_sems,
    grad_sems,
):
    step = pl.program_id(0)
    total, width = normed_s.shape
    pair = 2 * LANES

    def mix_copy(i, group):
        start = pl.multiple_of(group * width + i * pair, pair)
        return pltpu.make_async_copy(
            weights.at[:, pl.ds(start, pair)], mix_s.at[i, group], mix_sems.at[i, group]
        )

    normed_copy = pltpu.make_async_copy(normed, normed_s, sems.at[0])
    base_copy = pltpu.make_async_copy(base, base_s, sems.at[1])
    out_copy = pltpu.make_async_copy(weights.at[:, pl.ds(4 * width, width)], out_s, sems.at[2])
    query_copy = pltpu.make_async_copy(queries, queries_s, sems.at[3])
    cand_copy = pltpu.make_async_copy(cand_t, cand_s, sems.at[4])

    @pl.when(step == 0)
    def _():
        normed_copy.start()
        for group in range(4):
            mix_copy(0, group).start()
        normed_copy.wait()

    @pl.when(step < ENCODE_STEPS)
    def _():
        for group in range(4):
            mix_copy(step, group).wait()

        @pl.when(step + 1 < ENCODE_STEPS)
        def _():
            for group in range(4):
                mix_copy(step + 1, group).start()

        @pl.when(step == 1)
        def _():
            base_copy.start()

        @pl.when(step == 2)
        def _():
            out_copy.start()

        @pl.when(step == 3)
        def _():
            query_copy.start()
            cand_copy.start()

        users = total // HIST
        for k in range(2):
            cols = slice(k * LANES, (k + 1) * LANES)
            columns = jnp.concatenate([mix_s[step, g, :, cols] for g in range(4)], axis=1)
            projected = dot(normed_s[...], columns)
            projected = projected * sigmoid(projected)
            gate_s[2 * step + k] = projected[:, :LANES]
            qkv_s[k] = projected[:, LANES:].astype(BF)
        units = [(k, slice(u * HIST, (u + 1) * HIST)) for k in range(2) for u in range(users)]
        for n, (k, part) in enumerate(units):
            logit_s[n] = dot_t(qkv_s[k, part, LANES : 2 * LANES], qkv_s[k, part, 2 * LANES :])
        row = lax.broadcasted_iota(jnp.int32, (HIST, HIST), 0)
        column = lax.broadcasted_iota(jnp.int32, (HIST, HIST), 1)
        causal = column <= row
        for n in range(len(units)):
            logits = logit_s[n] * (1.0 / math.sqrt(LANES))
            weight = jnp.where(causal, logits * sigmoid(logits) * (1.0 / HIST), 0.0)
            weight_s[n] = weight.astype(BF)
        for n, (k, part) in enumerate(units):
            mixed_s[2 * step + k, part] = dot(weight_s[n], qkv_s[k, part, :LANES])

    @pl.when(step == ENCODE_STEPS - 1)
    def _():
        square = mixed_s[0] * mixed_s[0]
        for h in range(1, HEADS):
            square = square + mixed_s[h] * mixed_s[h]
        scale = lax.rsqrt(jnp.sum(square, -1, keepdims=True) * (1.0 / width) + 1e-06)
        for h in range(HEADS):
            gated_s[:, h * LANES : (h + 1) * LANES] = (mixed_s[h] * scale * gate_s[h]).astype(BF)
        base_copy.wait()
        out_copy.wait()
        for n in range(width // pair):
            cols = slice(n * pair, (n + 1) * pair)
            value = (base_s[:, cols] + dot(gated_s[...], out_s[:, cols])).astype(BF)
            encoded_s[:, :, cols] = value.reshape(total // (GROUP * HIST), GROUP * HIST, pair)
        query_copy.wait()
        cand_copy.wait()

    @pl.when(step >= ENCODE_STEPS)
    def _():
        now = step - ENCODE_STEPS
        lane = lax.broadcasted_iota(jnp.int32, (HEADS, width), 1) // LANES
        head_row = lax.broadcasted_iota(jnp.int32, (HEADS, width), 0)
        spread_weight = jnp.where(lane == head_row, score_weight[...], 0.0)
        high, middle, low = split3(spread_weight)
        parts = [slice(g * HIST, (g + 1) * HIST) for g in range(GROUP)]
        units = [(h, g) for g in range(GROUP) for h in range(HEADS)]
        heads = [slice(h * LANES, (h + 1) * LANES) for h in range(HEADS)]
        for n, (h, g) in enumerate(units):
            logit_s[n] = dot_t(
                queries_s[now, parts[g], heads[h]], encoded_s[now, parts[g], heads[h]]
            )
        along = []
        for part in parts:
            keys = encoded_s[now, part]
            along.append((dot_t(low, keys) + dot_t(middle, keys)) + dot_t(high, keys))
        totals = [jnp.zeros((HIST, HIST), F32) for _ in range(GROUP)]
        for n, (h, g) in enumerate(units):
            row = along[g][h : h + 1]
            logits = logit_s[n] * (1.0 / math.sqrt(LANES))
            gate = sigmoid(logits)
            product = logits * gate
            weight = (product * (1.0 / HIST)).astype(BF).astype(F32)
            totals[g] = totals[g] + weight * row
            slope = gate + product * (1.0 - gate)
            weight_s[n] = (slope * (row * (1.0 / (HIST * math.sqrt(LANES))))).astype(BF)
        for n, (h, g) in enumerate(units):
            logit_s[n] = dot(weight_s[n], encoded_s[now, parts[g], heads[h]])
        for g, part in enumerate(parts):
            partial = jnp.sum(totals[g], -1, keepdims=True).astype(BF).astype(F32)
            partial_row = jnp.broadcast_to(partial, (HIST, HIST)).T[:1]
            active = lax.broadcasted_iota(jnp.int32, (1, HIST), 1) < counts[now * GROUP + g]
            score = jnp.where(active, partial_row + own[g], 0.0)
            err = jnp.where(active, sigmoid(score) - labels[g], 0.0)
            scores[g] = score
            error[g] = err
            err_rows = jnp.broadcast_to(err, (HIST, HIST)).T
            for h in range(HEADS):
                direction = logit_s[g * HEADS + h].astype(BF).astype(F32)
                slope = (err_rows * direction).astype(BF)
                slopes[part, heads[h]] = slope
                slope_s[now, part, heads[h]] = slope

    @pl.when(step == pl.num_programs(0) - 1)
    def _():
        _, pairs, tall, wide = mine.shape
        right = width // wide
        down = mine.shape[0] // right
        piece = tall * down
        copies = []
        for n in range(right):
            cols = slice(n * wide, (n + 1) * wide)
            slope = slope_s[:, :, cols].reshape(-1, wide)
            for which, store in ((core[0], mine_s), (1 - core[0], other_s)):
                rows = cand_s[:, which].reshape(pairs * piece, -1)
                grad = dot(rows, slope).astype(BF)
                for p in range(pairs):
                    for a in range(down):
                        start = p * piece + a * tall
                        store[n * down + a, p] = grad[start : start + tall]
            chunk = pl.ds(n * down, down)
            for k, (source, target) in enumerate(((mine_s, mine), (other_s, other))):
                copy = pltpu.make_async_copy(
                    source.at[chunk], target.at[chunk], grad_sems.at[k, n]
                )
                copy.start()
                copies.append(copy)
        for copy in copies:
            copy.wait()


def attention(
    counts,
    core,
    normed,
    base,
    weights,
    queries,
    cand_t,
    score_weight,
    own,
    labels,
    pairs,
    users,
):
    nblocks = counts.shape[0]
    total, width = queries.shape
    rows = total // nblocks
    groups = nblocks // GROUP
    side = math.isqrt(users)
    shape = (users, pairs, width // (2 * pairs * side), width // side)
    current = lambda i: jnp.maximum(i - ENCODE_STEPS, 0)
    row = pl.BlockSpec((GROUP, 1, rows), lambda i, n, c: (current(i), 0, 0))
    whole = lambda i, n, c: (0, 0)
    anywhere = pl.BlockSpec(memory_space=pl.ANY)
    return pl.pallas_call(
        attention_kernel,
        grid_spec=pltpu.PrefetchScalarGridSpec(
            num_scalar_prefetch=2,
            grid=(ENCODE_STEPS + groups,),
            in_specs=[anywhere] * 5
            + [
                pl.BlockSpec((1, width), whole),
                row,
                row,
            ],
            out_specs=[
                row,
                row,
                pl.BlockSpec((GROUP * rows, width), lambda i, n, c: (current(i), 0)),
                anywhere,
                anywhere,
            ],
            scratch_shapes=[
                pltpu.VMEM((total, width), BF),
                pltpu.VMEM((total, width), F32),
                pltpu.VMEM((ENCODE_STEPS, 4, width, 2 * LANES), BF),
                pltpu.VMEM((width, width), BF),
                pltpu.VMEM((groups, GROUP * rows, width), BF),
                pltpu.VMEM((pairs, 2, width // (2 * pairs), total), BF),
                pltpu.VMEM((HEADS, total, LANES), F32),
                pltpu.VMEM((HEADS, total, LANES), F32),
                pltpu.VMEM((2, total, 3 * LANES), BF),
                pltpu.VMEM((total, width), BF),
                pltpu.VMEM((groups, GROUP * rows, width), BF),
                pltpu.VMEM((GROUP * HEADS, HIST, HIST), F32),
                pltpu.VMEM((GROUP * HEADS, HIST, HIST), BF),
                pltpu.VMEM((groups, GROUP * rows, width), BF),
                pltpu.VMEM(shape, BF),
                pltpu.VMEM(shape, BF),
                pltpu.SemaphoreType.DMA((5,)),
                pltpu.SemaphoreType.DMA((ENCODE_STEPS, 4)),
                pltpu.SemaphoreType.DMA((2, side)),
            ],
        ),
        out_shape=[
            jax.ShapeDtypeStruct((nblocks, 1, rows), F32),
            jax.ShapeDtypeStruct((nblocks, 1, rows), F32),
            jax.ShapeDtypeStruct((total, width), BF),
            jax.ShapeDtypeStruct(shape, BF),
            jax.ShapeDtypeStruct(shape, BF),
        ],
        compiler_params=pltpu.CompilerParams(vmem_limit_bytes=50 * 1024 * 1024),
        name="attention",
    )(
        counts,
        core,
        normed,
        base,
        weights,
        queries.reshape(groups, GROUP * rows, width),
        cand_t.reshape(pairs, 2, width // (2 * pairs), total),
            score_weight,
        own,
        labels,
    )


def shift(array, side, dx, dy):
    moves = []
    for x in range(side):
        for y in range(side):
            moves.append(((x + dx) % side * side + (y + dy) % side, x * side + y))
    return lax.ppermute(array, "user", moves)


def spread(piece, side, x_first):
    first = lambda a, d: shift(a, side, d, 0) if x_first else shift(a, side, 0, d)
    second = lambda a, d: shift(a, side, 0, d) if x_first else shift(a, side, d, 0)
    low = jnp.stack([piece, first(piece, 1)])
    high = jnp.stack([first(piece, 2), first(piece, -1)])
    low_after, high_before = second(low, 1), second(high, -1)
    high_after, low_before = second(high, 1), second(low, -1)
    low_two, high_two = second(low_after, 1), second(high_before, -1)
    return (low, high, low_after, high_after, low_two, high_two, low_before, high_before)


def join_kernel(left, right, out):
    last = pl.program_id(0) == pl.num_programs(0) - 1

    @pl.when(last)
    def _():
        out[...] = right[...]

    @pl.when(jnp.logical_not(last))
    def _():
        out[...] = left[...]


def join(left, right):
    rows, wide = right.shape
    groups = left.shape[1] // wide
    return pl.pallas_call(
        join_kernel,
        grid=(groups + 1,),
        in_specs=[
            pl.BlockSpec((rows, wide), lambda g: (0, jnp.minimum(g, groups - 1))),
            pl.BlockSpec((rows, wide), lambda g: (0, 0)),
        ],
        out_specs=pl.BlockSpec((rows, wide), lambda g: (0, g)),
        out_shape=jax.ShapeDtypeStruct((rows, (groups + 1) * wide), left.dtype),
        name="join",
    )(left, right)


def assemble_kernel(pieces, out, out_s, sems):
    count, tall, wide = pieces.shape
    down = out.shape[0] // tall
    copies = []
    for k in range(count):
        a, b = k % down, k // down
        copies.append(
            pltpu.make_async_copy(
                pieces.at[k],
                out_s.at[pl.ds(a * tall, tall), pl.ds(b * wide, wide)],
                sems.at[k],
            )
        )
    for copy in copies:
        copy.start()
    for copy in copies:
        copy.wait()
    out[...] = out_s[...].astype(F32)


def assemble(pieces, right):
    count, tall, wide = pieces.shape
    shape = (count // right * tall, right * wide)
    return pl.pallas_call(
        assemble_kernel,
        in_specs=[pl.BlockSpec(memory_space=pl.ANY)],
        out_shape=jax.ShapeDtypeStruct(shape, F32),
        scratch_shapes=[pltpu.VMEM(shape, BF), pltpu.SemaphoreType.DMA((count,))],
        name="assemble",
    )(pieces)


def body(
    history_items,
    history_events,
    history_lengths,
    action_table,
    mix_weight,
    out_weight,
    query_weight,
    score_weight,
    self_weight,
    candidates,
    block_owner,
    row_counts,
    labels,
):
    users = lax.axis_size("user")
    loaders = lax.axis_size("loader")
    pairs = loaders // 2
    nblocks, rows, width = candidates.shape

    weights = lax.all_gather(join(mix_weight, out_weight), "loader", axis=0, tiled=True)
    actions = action_table.shape[0]
    packed = jnp.concatenate(
        [
            history_items[0],
            jnp.broadcast_to(history_events[0][:, None].astype(BF), (HIST, actions)),
            jnp.broadcast_to(history_lengths[0].astype(BF), (HIST, LANES - actions)),
        ],
        axis=1,
    )
    side = math.isqrt(users)
    half = HIST // 2
    halves_a = spread(packed[:half], side, True)
    halves_b = spread(packed[half:], side, False)

    flat = candidates.reshape(-1, width)
    queries = jnp.dot(flat, query_weight, preferred_element_type=F32).astype(BF)
    cand_t = flat.T
    own = jnp.sum(candidates.astype(F32) * self_weight, -1)

    owner = block_owner[:, 0]
    here = lax.axis_index("user").astype(jnp.int32)
    far_x = lax.rem(owner // side - here // side + side, side)
    far_y = lax.rem(lax.rem(owner, side) - lax.rem(here, side) + side, side)
    base, normed = prepare(
        far_y * side + far_x, far_x * side + far_y, halves_a, halves_b, action_table
    )
    core = lax.rem(lax.axis_index("loader").astype(jnp.int32), 2)[None]
    scores, error, slopes, mine, other = attention(
        row_counts,
        core,
        normed,
        base,
            weights,
        queries,
        cand_t,
        score_weight[None],
        own[:, None],
        labels[:, None],
        pairs,
        users,
    )

    arrived = lax.ppermute(other, "loader", [(i, i ^ 1) for i in range(loaders)])
    pieces = (mine.astype(F32) + arrived.astype(F32)).astype(BF)
    pieces = lax.all_to_all(pieces, "user", 0, 0, tiled=True)
    pieces = jnp.sum(pieces.astype(F32), 0).astype(BF)
    groups = [[c + 2 * i for i in range(pairs)] for c in range(2)]
    pieces = lax.all_to_all(pieces, "loader", 0, 0, axis_index_groups=groups, tiled=True)
    piece = jnp.sum(pieces.astype(F32), 0).astype(BF)
    pieces = lax.all_to_all(
        jnp.broadcast_to(piece[None], (users,) + piece.shape), "user", 0, 0, tiled=True
    )
    query_grad = assemble(pieces, side)

    back = lax.dot_general(slopes, query_weight, (((1,), (1,)), ((), ())), preferred_element_type=F32)
    row_grads = (error.reshape(-1)[:, None] * self_weight + back).astype(BF)
    return (scores[:, 0], row_grads.reshape(nblocks, rows, width), query_grad)


def solution(mesh):
    placed = (
        P(("user", "loader"), None, None),
        P(("user", "loader"), None),
        P(("user", "loader")),
        P(),
        P("loader", None),
        P("loader", None),
        P(),
        P(),
        P(),
        P(("user", "loader"), None, None),
        P(("user", "loader"), None),
        P(("user", "loader")),
        P(("user", "loader"), None),
    )
    return jax.shard_map(
        body,
        mesh=mesh,
        in_specs=placed,
        out_specs=(
            P(("user", "loader"), None),
            P(("user", "loader"), None, None),
            P("loader", None),
        ),
        check_vma=False,
    )
```

```python
import functools
import math

import jax
import jax.numpy as jnp
from jax import lax
from jax.experimental import pallas as pl
from jax.experimental.pallas import tpu as pltpu
from jax.sharding import PartitionSpec as P

HEADS = 8
HIST = 128
LANES = 128
BF = jnp.bfloat16
F32 = jnp.float32
VMEM_BYTES = 56 * 1024 * 1024


def sigmoid(v):
    return 0.5 * jnp.tanh(0.5 * v) + 0.5


def dot(a, b):
    return jnp.dot(a, b, preferred_element_type=F32)


def dot_t(a, b):
    return lax.dot_general(a, b, (((1,), (1,)), ((), ())), preferred_element_type=F32)


def split3(v):
    high = v.astype(BF)
    rest = v - high.astype(F32)
    middle = rest.astype(BF)
    low = (rest - middle.astype(F32)).astype(BF)
    return high, middle, low


def prepare_kernel(nblocks, place_a, place_b, *refs):
    count = (len(refs) - 5) // 2
    halves = ((place_a, refs[:count]), (place_b, refs[count : 2 * count]))
    table, base, normed, rows_s, sems = refs[2 * count :]
    block = pl.program_id(0)
    width = base.shape[1]
    actions = table.shape[0]
    half = HIST // 2

    def fetch(which, b, source):
        return pltpu.make_async_copy(
            source, rows_s.at[b, pl.ds(which * half, half)], sems.at[which, b]
        )

    @pl.when(block == 0)
    def _():
        for b in range(nblocks):
            for which, (place, arrays) in enumerate(halves):
                for k, array in enumerate(arrays):

                    @pl.when(place[b] // 2 == k)
                    def _():
                        fetch(which, b, array.at[lax.rem(place[b], 2)]).start()

    for which, (place, arrays) in enumerate(halves):
        fetch(which, block, arrays[0].at[0]).wait()
    rows = rows_s[block]
    tail = rows[:, width:].astype(F32)
    lane = lax.broadcasted_iota(jnp.int32, (HIST, actions), 1).astype(F32)
    onehot = jnp.where(tail[:, :actions] == lane, 1.0, 0.0).astype(BF)
    value = rows[:, :width].astype(F32)
    high, middle, low = split3(table[...])
    value = value + ((dot(onehot, low) + dot(onehot, middle)) + dot(onehot, high))
    position = lax.broadcasted_iota(jnp.int32, (HIST, 1), 0).astype(F32)
    value = jnp.where(position < tail[:, LANES - 1 :], value, 0.0)
    scale = lax.rsqrt(jnp.mean(value * value, -1, keepdims=True) + 1e-06)
    base[...] = value
    normed[...] = (value * scale).astype(BF)


def prepare(place_a, place_b, halves_a, halves_b, table):
    nblocks = place_a.shape[0]
    width = table.shape[1]
    total = nblocks * HIST
    arrays = list(halves_a) + list(halves_b)
    return pl.pallas_call(
        functools.partial(prepare_kernel, nblocks),
        grid_spec=pltpu.PrefetchScalarGridSpec(
            num_scalar_prefetch=2,
            grid=(nblocks,),
            in_specs=[pl.BlockSpec(memory_space=pl.ANY)] * len(arrays)
            + [pl.BlockSpec(table.shape, lambda b, p, q: (0, 0))],
            out_specs=[
                pl.BlockSpec((HIST, width), lambda b, p, q: (b, 0)),
                pl.BlockSpec((HIST, width), lambda b, p, q: (b, 0)),
            ],
            scratch_shapes=[
                pltpu.VMEM((nblocks, HIST, arrays[0].shape[-1]), BF),
                pltpu.SemaphoreType.DMA((2, nblocks)),
            ],
        ),
        out_shape=[
            jax.ShapeDtypeStruct((total, width), F32),
            jax.ShapeDtypeStruct((total, width), BF),
        ],
        compiler_params=pltpu.CompilerParams(vmem_limit_bytes=VMEM_BYTES),
        name="prepare",
    )(place_a, place_b, *arrays, table)


ENCODE_STEPS = HEADS // 2
GROUP = 2


def attention_kernel(
    counts,
    core,
    normed,
    base,
    weights,
    queries,
    cand_t,
    score_weight,
    own,
    labels,
    scores,
    error,
    slopes,
    other,
    normed_s,
    base_s,
    mix_s,
    out_s,
    queries_s,
    cand_s,
    gate_s,
    mixed_s,
    qkv_s,
    gated_s,
    encoded_s,
    logit_s,
    weight_s,
    slope_s,
    other_s,
    sems,
    mix_sems,
    grad_sems,
):
    step = pl.program_id(0)
    total, width = normed_s.shape
    pair = 2 * LANES

    def mix_copy(i, group):
        start = pl.multiple_of(group * width + i * pair, pair)
        return pltpu.make_async_copy(
            weights.at[:, pl.ds(start, pair)], mix_s.at[i, group], mix_sems.at[i, group]
        )

    normed_copy = pltpu.make_async_copy(normed, normed_s, sems.at[0])
    base_copy = pltpu.make_async_copy(base, base_s, sems.at[1])
    out_copy = pltpu.make_async_copy(weights.at[:, pl.ds(4 * width, width)], out_s, sems.at[2])
    query_copy = pltpu.make_async_copy(queries, queries_s, sems.at[3])
    cand_copy = pltpu.make_async_copy(cand_t, cand_s, sems.at[4])

    @pl.when(step == 0)
    def _():
        normed_copy.start()
        for group in range(4):
            mix_copy(0, group).start()
        normed_copy.wait()

    @pl.when(step < ENCODE_STEPS)
    def _():
        for group in range(4):
            mix_copy(step, group).wait()

        @pl.when(step + 1 < ENCODE_STEPS)
        def _():
            for group in range(4):
                mix_copy(step + 1, group).start()

        @pl.when(step == 1)
        def _():
            base_copy.start()

        @pl.when(step == 2)
        def _():
            out_copy.start()

        @pl.when(step == 3)
        def _():
            query_copy.start()
            cand_copy.start()

        users = total // HIST
        for k in range(2):
            cols = slice(k * LANES, (k + 1) * LANES)
            columns = jnp.concatenate([mix_s[step, g, :, cols] for g in range(4)], axis=1)
            projected = dot(normed_s[...], columns)
            projected = projected * sigmoid(projected)
            gate_s[2 * step + k] = projected[:, :LANES]
            qkv_s[k] = projected[:, LANES:].astype(BF)
        units = [(k, slice(u * HIST, (u + 1) * HIST)) for k in range(2) for u in range(users)]
        for n, (k, part) in enumerate(units):
            logit_s[n] = dot_t(qkv_s[k, part, LANES : 2 * LANES], qkv_s[k, part, 2 * LANES :])
        row = lax.broadcasted_iota(jnp.int32, (HIST, HIST), 0)
        column = lax.broadcasted_iota(jnp.int32, (HIST, HIST), 1)
        causal = column <= row
        for n in range(len(units)):
            logits = logit_s[n] * (1.0 / math.sqrt(LANES))
            weight = jnp.where(causal, logits * sigmoid(logits) * (1.0 / HIST), 0.0)
            weight_s[n] = weight.astype(BF)
        for n, (k, part) in enumerate(units):
            mixed_s[2 * step + k, part] = dot(weight_s[n], qkv_s[k, part, :LANES])

    @pl.when(step == ENCODE_STEPS - 1)
    def _():
        square = mixed_s[0] * mixed_s[0]
        for h in range(1, HEADS):
            square = square + mixed_s[h] * mixed_s[h]
        scale = lax.rsqrt(jnp.sum(square, -1, keepdims=True) * (1.0 / width) + 1e-06)
        for h in range(HEADS):
            gated_s[:, h * LANES : (h + 1) * LANES] = (mixed_s[h] * scale * gate_s[h]).astype(BF)
        base_copy.wait()
        out_copy.wait()
        for n in range(width // pair):
            cols = slice(n * pair, (n + 1) * pair)
            value = (base_s[:, cols] + dot(gated_s[...], out_s[:, cols])).astype(BF)
            encoded_s[:, :, cols] = value.reshape(total // (GROUP * HIST), GROUP * HIST, pair)
        query_copy.wait()
        cand_copy.wait()

    @pl.when(step >= ENCODE_STEPS)
    def _():
        now = step - ENCODE_STEPS
        lane = lax.broadcasted_iota(jnp.int32, (HEADS, width), 1) // LANES
        head_row = lax.broadcasted_iota(jnp.int32, (HEADS, width), 0)
        spread_weight = jnp.where(lane == head_row, score_weight[...], 0.0)
        high, middle, low = split3(spread_weight)
        parts = [slice(g * HIST, (g + 1) * HIST) for g in range(GROUP)]
        units = [(h, g) for g in range(GROUP) for h in range(HEADS)]
        heads = [slice(h * LANES, (h + 1) * LANES) for h in range(HEADS)]
        for n, (h, g) in enumerate(units):
            logit_s[n] = dot_t(
                queries_s[now, parts[g], heads[h]], encoded_s[now, parts[g], heads[h]]
            )
        along = []
        for part in parts:
            keys = encoded_s[now, part]
            along.append((dot_t(low, keys) + dot_t(middle, keys)) + dot_t(high, keys))
        totals = [jnp.zeros((HIST, HIST), F32) for _ in range(GROUP)]
        for n, (h, g) in enumerate(units):
            row = along[g][h : h + 1]
            logits = logit_s[n] * (1.0 / math.sqrt(LANES))
            gate = sigmoid(logits)
            product = logits * gate
            weight = (product * (1.0 / HIST)).astype(BF).astype(F32)
            totals[g] = totals[g] + weight * row
            slope = gate + product * (1.0 - gate)
            weight_s[n] = (slope * (row * (1.0 / (HIST * math.sqrt(LANES))))).astype(BF)
        for n, (h, g) in enumerate(units):
            logit_s[n] = dot(weight_s[n], encoded_s[now, parts[g], heads[h]])
        for g, part in enumerate(parts):
            partial = jnp.sum(totals[g], -1, keepdims=True).astype(BF).astype(F32)
            partial_row = jnp.broadcast_to(partial, (HIST, HIST)).T[:1]
            block = now * GROUP + g
            active = lax.broadcasted_iota(jnp.int32, (1, HIST), 1) < counts[block]
            score = jnp.where(active, partial_row + own[block], 0.0)
            err = jnp.where(active, sigmoid(score) - labels[block], 0.0)
            scores[block] = score
            error[block] = err
            err_rows = jnp.broadcast_to(err, (HIST, HIST)).T
            for h in range(HEADS):
                direction = logit_s[g * HEADS + h].astype(BF).astype(F32)
                slope = (err_rows * direction).astype(BF)
                slopes[part, heads[h]] = slope
                slope_s[now, part, heads[h]] = slope

    @pl.when(step == pl.num_programs(0) - 1)
    def _():
        pairs, _, piece, _ = cand_s.shape
        _, _, tall, wide = other.shape
        right = width // wide
        down = piece // tall
        copies = []
        for n in range(right):
            cols = slice(n * wide, (n + 1) * wide)
            slope = slope_s[:, :, cols].reshape(-1, wide)
            rows = cand_s[:, 1 - core[0]].reshape(pairs * piece, -1)
            place_pieces(dot(rows, slope).astype(BF), other_s, n * down, piece)
            chunk = pl.ds(n * down, down)
            copy = pltpu.make_async_copy(other_s.at[chunk], other.at[chunk], grad_sems.at[n])
            copy.start()
            copies.append(copy)
        for copy in copies:
            copy.wait()


def place_pieces(grad, store, first, piece):
    tall = store.shape[2]
    for p in range(store.shape[1]):
        for a in range(piece // tall):
            start = p * piece + a * tall
            store[first + a, p] = grad[start : start + tall]


def gradient_kernel(core, cand_t, slopes, out, cand_s, slope_s, sems):
    first = pltpu.make_async_copy(slopes, slope_s, sems.at[0])
    second = pltpu.make_async_copy(cand_t.at[:, core[0]], cand_s, sems.at[1])
    first.start()
    second.start()
    first.wait()
    second.wait()
    pairs, piece, total = cand_s.shape
    _, _, tall, wide = out.shape
    for n in range(slope_s.shape[1] // wide):
        cols = slice(n * wide, (n + 1) * wide)
        grad = dot(cand_s[...].reshape(pairs * piece, total), slope_s[:, cols])
        place_pieces(grad.astype(BF), out, n * (piece // tall), piece)


def gradient(core, cand_t, slopes, users):
    pairs, _, piece, total = cand_t.shape
    width = slopes.shape[1]
    side = math.isqrt(users)
    shape = (users, pairs, piece // side, width // side)
    return pl.pallas_call(
        gradient_kernel,
        grid_spec=pltpu.PrefetchScalarGridSpec(
            num_scalar_prefetch=1,
            grid=(1,),
            in_specs=[pl.BlockSpec(memory_space=pl.ANY)] * 2,
            out_specs=pl.BlockSpec(shape, lambda n, c: (0, 0, 0, 0)),
            scratch_shapes=[
                pltpu.VMEM((pairs, piece, total), BF),
                pltpu.VMEM((total, width), BF),
                pltpu.SemaphoreType.DMA((2,)),
            ],
        ),
        out_shape=jax.ShapeDtypeStruct(shape, BF),
        cost_estimate=pl.CostEstimate(
            flops=total * width * width, bytes_accessed=3 * total * width * 2, transcendentals=0
        ),
        compiler_params=pltpu.CompilerParams(vmem_limit_bytes=16 * 1024 * 1024),
        name="gradient",
    )(core, cand_t, slopes)


def attention(
    counts,
    core,
    normed,
    base,
    weights,
    queries,
    cand_t,
    score_weight,
    own,
    labels,
    pairs,
    users,
):
    nblocks = counts.shape[0]
    total, width = queries.shape
    rows = total // nblocks
    groups = nblocks // GROUP
    side = math.isqrt(users)
    shape = (users, pairs, width // (2 * pairs * side), width // side)
    current = lambda i: jnp.maximum(i - ENCODE_STEPS, 0)
    row = pl.BlockSpec((nblocks, 1, rows), lambda i, n, c: (0, 0, 0))
    whole = lambda i, n, c: (0, 0)
    anywhere = pl.BlockSpec(memory_space=pl.ANY)
    return pl.pallas_call(
        attention_kernel,
        grid_spec=pltpu.PrefetchScalarGridSpec(
            num_scalar_prefetch=2,
            grid=(ENCODE_STEPS + groups,),
            in_specs=[anywhere] * 5
            + [
                pl.BlockSpec((1, width), whole),
                row,
                row,
            ],
            out_specs=[
                row,
                row,
                pl.BlockSpec((GROUP * rows, width), lambda i, n, c: (current(i), 0)),
                anywhere,
            ],
            scratch_shapes=[
                pltpu.VMEM((total, width), BF),
                pltpu.VMEM((total, width), F32),
                pltpu.VMEM((ENCODE_STEPS, 4, width, 2 * LANES), BF),
                pltpu.VMEM((width, width), BF),
                pltpu.VMEM((groups, GROUP * rows, width), BF),
                pltpu.VMEM((pairs, 2, width // (2 * pairs), total), BF),
                pltpu.VMEM((HEADS, total, LANES), F32),
                pltpu.VMEM((HEADS, total, LANES), F32),
                pltpu.VMEM((2, total, 3 * LANES), BF),
                pltpu.VMEM((total, width), BF),
                pltpu.VMEM((groups, GROUP * rows, width), BF),
                pltpu.VMEM((GROUP * HEADS, HIST, HIST), F32),
                pltpu.VMEM((GROUP * HEADS, HIST, HIST), BF),
                pltpu.VMEM((groups, GROUP * rows, width), BF),
                pltpu.VMEM(shape, BF),
                pltpu.SemaphoreType.DMA((5,)),
                pltpu.SemaphoreType.DMA((ENCODE_STEPS, 4)),
                pltpu.SemaphoreType.DMA((side,)),
            ],
        ),
        out_shape=[
            jax.ShapeDtypeStruct((nblocks, 1, rows), F32),
            jax.ShapeDtypeStruct((nblocks, 1, rows), F32),
            jax.ShapeDtypeStruct((total, width), BF),
            jax.ShapeDtypeStruct(shape, BF),
        ],
        compiler_params=pltpu.CompilerParams(vmem_limit_bytes=51 * 1024 * 1024),
        name="attention",
    )(
        counts,
        core,
        normed,
        base,
        weights,
        queries.reshape(groups, GROUP * rows, width),
        cand_t,
        score_weight,
        own,
        labels,
    )


def shift(array, side, dx, dy):
    moves = []
    for x in range(side):
        for y in range(side):
            moves.append(((x + dx) % side * side + (y + dy) % side, x * side + y))
    return lax.ppermute(array, "user", moves)


def spread(piece, side, x_first):
    first = lambda a, d: shift(a, side, d, 0) if x_first else shift(a, side, 0, d)
    second = lambda a, d: shift(a, side, 0, d) if x_first else shift(a, side, d, 0)
    low = jnp.stack([piece, first(piece, 1)])
    high = jnp.stack([first(piece, 2), first(piece, -1)])
    low_after, high_before = second(low, 1), second(high, -1)
    high_after, low_before = second(high, 1), second(low, -1)
    low_two, high_two = second(low_after, 1), second(high_before, -1)
    return (low, high, low_after, high_after, low_two, high_two, low_before, high_before)


def join_kernel(left, right, out):
    wide = left.shape[1]
    out[:, :wide] = left[...]
    out[:, wide:] = right[...]


def join(left, right):
    return pl.pallas_call(
        join_kernel,
        out_shape=jax.ShapeDtypeStruct((left.shape[0], left.shape[1] + right.shape[1]), left.dtype),
        name="join",
    )(left, right)


def assemble_kernel(pieces, out):
    count, tall, wide = pieces.shape
    down = out.shape[0] // tall
    for k in range(count):
        a, b = k % down, k // down
        rows, cols = slice(a * tall, (a + 1) * tall), slice(b * wide, (b + 1) * wide)
        out[rows, cols] = pieces[k].astype(F32)


def assemble(pieces, right):
    count, tall, wide = pieces.shape
    return pl.pallas_call(
        assemble_kernel,
        out_shape=jax.ShapeDtypeStruct((count // right * tall, right * wide), F32),
        name="assemble",
    )(pieces)


def body(
    history_items,
    history_events,
    history_lengths,
    action_table,
    mix_weight,
    out_weight,
    query_weight,
    score_weight,
    self_weight,
    candidates,
    block_owner,
    row_counts,
    labels,
):
    users = lax.axis_size("user")
    loaders = lax.axis_size("loader")
    pairs = loaders // 2
    nblocks, rows, width = candidates.shape

    weights = lax.all_gather(join(mix_weight, out_weight), "loader", axis=0, tiled=True)
    actions = action_table.shape[0]
    packed = jnp.concatenate(
        [
            history_items[0],
            jnp.broadcast_to(history_events[0][:, None].astype(BF), (HIST, actions)),
            jnp.broadcast_to(history_lengths[0].astype(BF), (HIST, LANES - actions)),
        ],
        axis=1,
    )
    side = math.isqrt(users)
    half = HIST // 2
    halves_a = spread(packed[:half], side, True)
    halves_b = spread(packed[half:], side, False)

    flat = candidates.reshape(-1, width)
    queries = jnp.dot(flat, query_weight, preferred_element_type=F32).astype(BF)
    cand_t = flat.T.reshape(pairs, 2, width // loaders, -1)
    own = jnp.sum(candidates.astype(F32) * self_weight, -1)

    owner = block_owner[:, 0]
    here = lax.axis_index("user").astype(jnp.int32)
    far_x = lax.rem(owner // side - here // side + side, side)
    far_y = lax.rem(lax.rem(owner, side) - lax.rem(here, side) + side, side)
    base, normed = prepare(
        far_y * side + far_x, far_x * side + far_y, halves_a, halves_b, action_table
    )
    core = lax.rem(lax.axis_index("loader").astype(jnp.int32), 2)[None]
    scores, error, slopes, other = attention(
        row_counts,
        core,
        normed,
        base,
        weights,
        queries,
        cand_t,
        score_weight[None],
        own[:, None],
        labels[:, None],
        pairs,
        users,
    )

    arrived = lax.ppermute(other, "loader", [(i, i ^ 1) for i in range(loaders)])
    mine = gradient(core, cand_t, slopes, users)
    pieces = (mine.astype(F32) + arrived.astype(F32)).astype(BF)
    pieces = lax.all_to_all(pieces, "user", 0, 0, tiled=True)
    pieces = jnp.sum(pieces.astype(F32), 0).astype(BF)
    groups = [[c + 2 * i for i in range(pairs)] for c in range(2)]
    pieces = lax.all_to_all(pieces, "loader", 0, 0, axis_index_groups=groups, tiled=True)
    piece = jnp.sum(pieces.astype(F32), 0).astype(BF)
    pieces = lax.all_to_all(
        jnp.broadcast_to(piece[None], (users,) + piece.shape), "user", 0, 0, tiled=True
    )
    query_grad = assemble(pieces, side)

    back = lax.dot_general(slopes, query_weight, (((1,), (1,)), ((), ())), preferred_element_type=F32)
    row_grads = (error.reshape(-1)[:, None] * self_weight + back).astype(BF)
    return (scores[:, 0], row_grads.reshape(nblocks, rows, width), query_grad)


def solution(mesh):
    placed = (
        P(("user", "loader"), None, None),
        P(("user", "loader"), None),
        P(("user", "loader")),
        P(),
        P("loader", None),
        P("loader", None),
        P(),
        P(),
        P(),
        P(("user", "loader"), None, None),
        P(("user", "loader"), None),
        P(("user", "loader")),
        P(("user", "loader"), None),
    )
    return jax.shard_map(
        body,
        mesh=mesh,
        in_specs=placed,
        out_specs=(
            P(("user", "loader"), None),
            P(("user", "loader"), None, None),
            P("loader", None),
        ),
        check_vma=False,
    )
```

```python
import functools
import math

import jax
import jax.numpy as jnp
from jax import lax
from jax.experimental import pallas as pl
from jax.experimental.pallas import tpu as pltpu
from jax.sharding import PartitionSpec as P

HEADS = 8
HIST = 128
LANES = 128
BF = jnp.bfloat16
F32 = jnp.float32
VMEM_BYTES = 56 * 1024 * 1024


def sigmoid(v):
    return 0.5 * jnp.tanh(0.5 * v) + 0.5


def dot(a, b):
    return jnp.dot(a, b, preferred_element_type=F32)


def dot_t(a, b):
    return lax.dot_general(a, b, (((1,), (1,)), ((), ())), preferred_element_type=F32)


def split3(v):
    high = v.astype(BF)
    rest = v - high.astype(F32)
    middle = rest.astype(BF)
    low = (rest - middle.astype(F32)).astype(BF)
    return high, middle, low


def prepare_kernel(nblocks, place_a, place_b, *refs):
    count = (len(refs) - 5) // 2
    halves = ((place_a, refs[:count]), (place_b, refs[count : 2 * count]))
    table, base, normed, rows_s, sems = refs[2 * count :]
    block = pl.program_id(0)
    width = base.shape[1]
    actions = table.shape[0]
    half = HIST // 2

    def fetch(which, b, source):
        return pltpu.make_async_copy(
            source, rows_s.at[b, pl.ds(which * half, half)], sems.at[which, b]
        )

    @pl.when(block == 0)
    def _():
        for b in range(nblocks):
            for which, (place, arrays) in enumerate(halves):
                for k, array in enumerate(arrays):

                    @pl.when(place[b] // 2 == k)
                    def _():
                        fetch(which, b, array.at[lax.rem(place[b], 2)]).start()

    for which, (place, arrays) in enumerate(halves):
        fetch(which, block, arrays[0].at[0]).wait()
    rows = rows_s[block]
    tail = rows[:, width:].astype(F32)
    lane = lax.broadcasted_iota(jnp.int32, (HIST, actions), 1).astype(F32)
    onehot = jnp.where(tail[:, :actions] == lane, 1.0, 0.0).astype(BF)
    value = rows[:, :width].astype(F32)
    high, middle, low = split3(table[...])
    value = value + ((dot(onehot, low) + dot(onehot, middle)) + dot(onehot, high))
    position = lax.broadcasted_iota(jnp.int32, (HIST, 1), 0).astype(F32)
    value = jnp.where(position < tail[:, LANES - 1 :], value, 0.0)
    scale = lax.rsqrt(jnp.mean(value * value, -1, keepdims=True) + 1e-06)
    base[...] = value
    normed[...] = (value * scale).astype(BF)


def prepare(place_a, place_b, halves_a, halves_b, table):
    nblocks = place_a.shape[0]
    width = table.shape[1]
    total = nblocks * HIST
    arrays = list(halves_a) + list(halves_b)
    return pl.pallas_call(
        functools.partial(prepare_kernel, nblocks),
        grid_spec=pltpu.PrefetchScalarGridSpec(
            num_scalar_prefetch=2,
            grid=(nblocks,),
            in_specs=[pl.BlockSpec(memory_space=pl.ANY)] * len(arrays)
            + [pl.BlockSpec(table.shape, lambda b, p, q: (0, 0))],
            out_specs=[
                pl.BlockSpec((HIST, width), lambda b, p, q: (b, 0)),
                pl.BlockSpec((HIST, width), lambda b, p, q: (b, 0)),
            ],
            scratch_shapes=[
                pltpu.VMEM((nblocks, HIST, arrays[0].shape[-1]), BF),
                pltpu.SemaphoreType.DMA((2, nblocks)),
            ],
        ),
        out_shape=[
            jax.ShapeDtypeStruct((total, width), F32),
            jax.ShapeDtypeStruct((total, width), BF),
        ],
        compiler_params=pltpu.CompilerParams(vmem_limit_bytes=VMEM_BYTES),
        name="prepare",
    )(place_a, place_b, *arrays, table)


ENCODE_STEPS = HEADS // 2
GROUP = 2


def attention_kernel(
    counts,
    core,
    normed,
    base,
    weights,
    queries,
    cand_t,
    score_weight,
    own,
    labels,
    scores,
    error,
    slopes,
    other,
    normed_s,
    base_s,
    mix_s,
    out_s,
    queries_s,
    cand_s,
    gate_s,
    mixed_s,
    qkv_s,
    gated_s,
    encoded_s,
    logit_s,
    weight_s,
    other_s,
    sems,
    mix_sems,
    grad_sems,
):
    total, width = normed_s.shape
    pair = 2 * LANES

    def mix_copy(i, group):
        start = pl.multiple_of(group * width + i * pair, pair)
        return pltpu.make_async_copy(
            weights.at[:, pl.ds(start, pair)], mix_s.at[i, group], mix_sems.at[i, group]
        )

    normed_copy = pltpu.make_async_copy(normed, normed_s, sems.at[0])
    base_copy = pltpu.make_async_copy(base, base_s, sems.at[1])
    out_copy = pltpu.make_async_copy(weights.at[:, pl.ds(4 * width, width)], out_s, sems.at[2])
    query_copy = pltpu.make_async_copy(queries, queries_s, sems.at[3])
    cand_copy = pltpu.make_async_copy(cand_t, cand_s, sems.at[4])

    normed_copy.start()
    for group in range(4):
        mix_copy(0, group).start()
    normed_copy.wait()

    @pl.loop(0, ENCODE_STEPS, unroll=True)
    def _(step):
        for group in range(4):
            mix_copy(step, group).wait()

        @pl.when(step + 1 < ENCODE_STEPS)
        def _():
            for group in range(4):
                mix_copy(step + 1, group).start()

        @pl.when(step == 1)
        def _():
            base_copy.start()

        @pl.when(step == 2)
        def _():
            out_copy.start()

        @pl.when(step == 3)
        def _():
            query_copy.start()
            cand_copy.start()

        users = total // HIST
        for k in range(2):
            cols = slice(k * LANES, (k + 1) * LANES)
            columns = jnp.concatenate([mix_s[step, g, :, cols] for g in range(4)], axis=1)
            projected = dot(normed_s[...], columns)
            projected = projected * sigmoid(projected)
            gate_s[2 * step + k] = projected[:, :LANES]
            qkv_s[k] = projected[:, LANES:].astype(BF)
        units = [(k, slice(u * HIST, (u + 1) * HIST)) for k in range(2) for u in range(users)]
        for n, (k, part) in enumerate(units):
            logit_s[n] = dot_t(qkv_s[k, part, LANES : 2 * LANES], qkv_s[k, part, 2 * LANES :])
        row = lax.broadcasted_iota(jnp.int32, (HIST, HIST), 0)
        column = lax.broadcasted_iota(jnp.int32, (HIST, HIST), 1)
        causal = column <= row
        for n in range(len(units)):
            logits = logit_s[n] * (1.0 / math.sqrt(LANES))
            weight = jnp.where(causal, logits * sigmoid(logits) * (1.0 / HIST), 0.0)
            weight_s[n] = weight.astype(BF)
        for n, (k, part) in enumerate(units):
            mixed_s[2 * step + k, part] = dot(weight_s[n], qkv_s[k, part, :LANES])

    square = mixed_s[0] * mixed_s[0]
    for h in range(1, HEADS):
        square = square + mixed_s[h] * mixed_s[h]
    scale = lax.rsqrt(jnp.sum(square, -1, keepdims=True) * (1.0 / width) + 1e-06)
    for h in range(HEADS):
        gated_s[:, h * LANES : (h + 1) * LANES] = (mixed_s[h] * scale * gate_s[h]).astype(BF)
    base_copy.wait()
    out_copy.wait()
    for n in range(width // pair):
        cols = slice(n * pair, (n + 1) * pair)
        value = (base_s[:, cols] + dot(gated_s[...], out_s[:, cols])).astype(BF)
        encoded_s[:, :, cols] = value.reshape(total // (GROUP * HIST), GROUP * HIST, pair)
    query_copy.wait()
    cand_copy.wait()

    @pl.loop(0, total // (GROUP * HIST), unroll=True)
    def _(now):
        lane = lax.broadcasted_iota(jnp.int32, (HEADS, width), 1) // LANES
        head_row = lax.broadcasted_iota(jnp.int32, (HEADS, width), 0)
        spread_weight = jnp.where(lane == head_row, score_weight[...], 0.0)
        high, middle, low = split3(spread_weight)
        parts = [slice(g * HIST, (g + 1) * HIST) for g in range(GROUP)]
        units = [(h, g) for g in range(GROUP) for h in range(HEADS)]
        heads = [slice(h * LANES, (h + 1) * LANES) for h in range(HEADS)]
        for n, (h, g) in enumerate(units):
            logit_s[n] = dot_t(
                queries_s[now, parts[g], heads[h]], encoded_s[now, parts[g], heads[h]]
            )
        along = []
        for part in parts:
            keys = encoded_s[now, part]
            along.append((dot_t(low, keys) + dot_t(middle, keys)) + dot_t(high, keys))
        totals = [jnp.zeros((HIST, HIST), F32) for _ in range(GROUP)]
        for n, (h, g) in enumerate(units):
            row = along[g][h : h + 1]
            logits = logit_s[n] * (1.0 / math.sqrt(LANES))
            gate = sigmoid(logits)
            product = logits * gate
            weight = (product * (1.0 / HIST)).astype(BF).astype(F32)
            totals[g] = totals[g] + weight * row
            slope = gate + product * (1.0 - gate)
            weight_s[n] = (slope * (row * (1.0 / (HIST * math.sqrt(LANES))))).astype(BF)
        for n, (h, g) in enumerate(units):
            logit_s[n] = dot(weight_s[n], encoded_s[now, parts[g], heads[h]])
        for g, part in enumerate(parts):
            partial = jnp.sum(totals[g], -1, keepdims=True).astype(BF).astype(F32)
            partial_row = jnp.broadcast_to(partial, (HIST, HIST)).T[:1]
            block = now * GROUP + g
            active = lax.broadcasted_iota(jnp.int32, (1, HIST), 1) < counts[block]
            score = jnp.where(active, partial_row + own[block], 0.0)
            err = jnp.where(active, sigmoid(score) - labels[block], 0.0)
            scores[block] = score
            error[block] = err
            err_rows = jnp.broadcast_to(err, (HIST, HIST)).T
            for h in range(HEADS):
                direction = logit_s[g * HEADS + h].astype(BF).astype(F32)
                slope = (err_rows * direction).astype(BF)
                slopes[now, part, heads[h]] = slope

    pairs, _, piece, _ = cand_s.shape
    _, _, tall, wide = other.shape
    right = width // wide
    down = piece // tall
    copies = []
    for n in range(right):
        cols = slice(n * wide, (n + 1) * wide)
        slope = slopes[:, :, cols].reshape(-1, wide)
        rows = cand_s[:, 1 - core[0]].reshape(pairs * piece, -1)
        place_pieces(dot(rows, slope).astype(BF), other_s, n * down, piece)
        chunk = pl.ds(n * down, down)
        copy = pltpu.make_async_copy(other_s.at[chunk], other.at[chunk], grad_sems.at[n])
        copy.start()
        copies.append(copy)
    for copy in copies:
        copy.wait()


def place_pieces(grad, store, first, piece):
    tall = store.shape[2]
    for p in range(store.shape[1]):
        for a in range(piece // tall):
            start = p * piece + a * tall
            store[first + a, p] = grad[start : start + tall]


def gradient_kernel(core, cand_t, slopes, out, cand_s, slope_s, sems):
    first = pltpu.make_async_copy(slopes, slope_s, sems.at[0])
    second = pltpu.make_async_copy(cand_t.at[:, core[0]], cand_s, sems.at[1])
    first.start()
    second.start()
    first.wait()
    second.wait()
    pairs, piece, total = cand_s.shape
    _, _, tall, wide = out.shape
    for n in range(slope_s.shape[1] // wide):
        cols = slice(n * wide, (n + 1) * wide)
        grad = dot(cand_s[...].reshape(pairs * piece, total), slope_s[:, cols])
        place_pieces(grad.astype(BF), out, n * (piece // tall), piece)


def gradient(core, cand_t, slopes, users):
    pairs, _, piece, total = cand_t.shape
    width = slopes.shape[1]
    side = math.isqrt(users)
    shape = (users, pairs, piece // side, width // side)
    return pl.pallas_call(
        gradient_kernel,
        grid_spec=pltpu.PrefetchScalarGridSpec(
            num_scalar_prefetch=1,
            grid=(1,),
            in_specs=[pl.BlockSpec(memory_space=pl.ANY)] * 2,
            out_specs=pl.BlockSpec(shape, lambda n, c: (0, 0, 0, 0)),
            scratch_shapes=[
                pltpu.VMEM((pairs, piece, total), BF),
                pltpu.VMEM((total, width), BF),
                pltpu.SemaphoreType.DMA((2,)),
            ],
        ),
        out_shape=jax.ShapeDtypeStruct(shape, BF),
        cost_estimate=pl.CostEstimate(
            flops=total * width * width, bytes_accessed=3 * total * width * 2, transcendentals=0
        ),
        compiler_params=pltpu.CompilerParams(vmem_limit_bytes=16 * 1024 * 1024),
        name="gradient",
    )(core, cand_t, slopes)


def attention(
    counts,
    core,
    normed,
    base,
    weights,
    queries,
    cand_t,
    score_weight,
    own,
    labels,
    pairs,
    users,
):
    nblocks = counts.shape[0]
    total, width = queries.shape
    rows = total // nblocks
    groups = nblocks // GROUP
    side = math.isqrt(users)
    shape = (users, pairs, width // (2 * pairs * side), width // side)
    row = pl.BlockSpec((nblocks, 1, rows), lambda i, n, c: (0, 0, 0))
    whole = lambda i, n, c: (0, 0)
    anywhere = pl.BlockSpec(memory_space=pl.ANY)
    return pl.pallas_call(
        attention_kernel,
        grid_spec=pltpu.PrefetchScalarGridSpec(
            num_scalar_prefetch=2,
            grid=(1,),
            in_specs=[anywhere] * 5
            + [
                pl.BlockSpec((1, width), whole),
                row,
                row,
            ],
            out_specs=[
                row,
                row,
                pl.BlockSpec((groups, GROUP * rows, width), lambda i, n, c: (0, 0, 0)),
                anywhere,
            ],
            scratch_shapes=[
                pltpu.VMEM((total, width), BF),
                pltpu.VMEM((total, width), F32),
                pltpu.VMEM((ENCODE_STEPS, 4, width, 2 * LANES), BF),
                pltpu.VMEM((width, width), BF),
                pltpu.VMEM((groups, GROUP * rows, width), BF),
                pltpu.VMEM((pairs, 2, width // (2 * pairs), total), BF),
                pltpu.VMEM((HEADS, total, LANES), F32),
                pltpu.VMEM((HEADS, total, LANES), F32),
                pltpu.VMEM((2, total, 3 * LANES), BF),
                pltpu.VMEM((total, width), BF),
                pltpu.VMEM((groups, GROUP * rows, width), BF),
                pltpu.VMEM((GROUP * HEADS, HIST, HIST), F32),
                pltpu.VMEM((GROUP * HEADS, HIST, HIST), BF),
                pltpu.VMEM(shape, BF),
                pltpu.SemaphoreType.DMA((5,)),
                pltpu.SemaphoreType.DMA((ENCODE_STEPS, 4)),
                pltpu.SemaphoreType.DMA((side,)),
            ],
        ),
        out_shape=[
            jax.ShapeDtypeStruct((nblocks, 1, rows), F32),
            jax.ShapeDtypeStruct((nblocks, 1, rows), F32),
            jax.ShapeDtypeStruct((groups, GROUP * rows, width), BF),
            jax.ShapeDtypeStruct(shape, BF),
        ],
        compiler_params=pltpu.CompilerParams(vmem_limit_bytes=51 * 1024 * 1024),
        name="attention",
    )(
        counts,
        core,
        normed,
        base,
        weights,
        queries.reshape(groups, GROUP * rows, width),
        cand_t,
        score_weight,
        own,
        labels,
    )


def shift(array, side, dx, dy):
    moves = []
    for x in range(side):
        for y in range(side):
            moves.append(((x + dx) % side * side + (y + dy) % side, x * side + y))
    return lax.ppermute(array, "user", moves)


def spread(piece, side, x_first):
    first = lambda a, d: shift(a, side, d, 0) if x_first else shift(a, side, 0, d)
    second = lambda a, d: shift(a, side, 0, d) if x_first else shift(a, side, d, 0)
    low = jnp.stack([piece, first(piece, 1)])
    high = jnp.stack([first(piece, 2), first(piece, -1)])
    low_after, high_before = second(low, 1), second(high, -1)
    high_after, low_before = second(high, 1), second(low, -1)
    low_two, high_two = second(low_after, 1), second(high_before, -1)
    return (low, high, low_after, high_after, low_two, high_two, low_before, high_before)


def join_kernel(left, right, out):
    wide = left.shape[1]
    out[:, :wide] = left[...]
    out[:, wide:] = right[...]


def join(left, right):
    return pl.pallas_call(
        join_kernel,
        out_shape=jax.ShapeDtypeStruct((left.shape[0], left.shape[1] + right.shape[1]), left.dtype),
        name="join",
    )(left, right)


def assemble_kernel(pieces, out):
    count, tall, wide = pieces.shape
    down = out.shape[0] // tall
    for k in range(count):
        a, b = k % down, k // down
        rows, cols = slice(a * tall, (a + 1) * tall), slice(b * wide, (b + 1) * wide)
        out[rows, cols] = pieces[k].astype(F32)


def assemble(pieces, right):
    count, tall, wide = pieces.shape
    return pl.pallas_call(
        assemble_kernel,
        out_shape=jax.ShapeDtypeStruct((count // right * tall, right * wide), F32),
        name="assemble",
    )(pieces)


def body(
    history_items,
    history_events,
    history_lengths,
    action_table,
    mix_weight,
    out_weight,
    query_weight,
    score_weight,
    self_weight,
    candidates,
    block_owner,
    row_counts,
    labels,
):
    users = lax.axis_size("user")
    loaders = lax.axis_size("loader")
    pairs = loaders // 2
    nblocks, rows, width = candidates.shape

    weights = lax.all_gather(join(mix_weight, out_weight), "loader", axis=0, tiled=True)
    actions = action_table.shape[0]
    packed = jnp.concatenate(
        [
            history_items[0],
            jnp.broadcast_to(history_events[0][:, None].astype(BF), (HIST, actions)),
            jnp.broadcast_to(history_lengths[0].astype(BF), (HIST, LANES - actions)),
        ],
        axis=1,
    )
    side = math.isqrt(users)
    half = HIST // 2
    halves_a = spread(packed[:half], side, True)
    halves_b = spread(packed[half:], side, False)

    flat = candidates.reshape(-1, width)
    queries = jnp.dot(flat, query_weight, preferred_element_type=F32).astype(BF)
    cand_t = flat.T.reshape(pairs, 2, width // loaders, -1)
    own = jnp.sum(candidates.astype(F32) * self_weight, -1)

    owner = block_owner[:, 0]
    here = lax.axis_index("user").astype(jnp.int32)
    far_x = lax.rem(owner // side - here // side + side, side)
    far_y = lax.rem(lax.rem(owner, side) - lax.rem(here, side) + side, side)
    base, normed = prepare(
        far_y * side + far_x, far_x * side + far_y, halves_a, halves_b, action_table
    )
    core = lax.rem(lax.axis_index("loader").astype(jnp.int32), 2)[None]
    scores, error, slopes, other = attention(
        row_counts,
        core,
        normed,
        base,
        weights,
        queries,
        cand_t,
        score_weight[None],
        own[:, None],
        labels[:, None],
        pairs,
        users,
    )

    arrived = lax.ppermute(other, "loader", [(i, i ^ 1) for i in range(loaders)])
    slopes = slopes.reshape(-1, width)
    mine = gradient(core, cand_t, slopes, users)
    pieces = (mine.astype(F32) + arrived.astype(F32)).astype(BF)
    pieces = lax.all_to_all(pieces, "user", 0, 0, tiled=True)
    pieces = jnp.sum(pieces.astype(F32), 0).astype(BF)
    groups = [[c + 2 * i for i in range(pairs)] for c in range(2)]
    pieces = lax.all_to_all(pieces, "loader", 0, 0, axis_index_groups=groups, tiled=True)
    piece = jnp.sum(pieces.astype(F32), 0).astype(BF)
    pieces = lax.all_to_all(
        jnp.broadcast_to(piece[None], (users,) + piece.shape), "user", 0, 0, tiled=True
    )
    query_grad = assemble(pieces, side)

    back = lax.dot_general(slopes, query_weight, (((1,), (1,)), ((), ())), preferred_element_type=F32)
    row_grads = (error.reshape(-1)[:, None] * self_weight + back).astype(BF)
    return (scores[:, 0], row_grads.reshape(nblocks, rows, width), query_grad)


def solution(mesh):
    placed = (
        P(("user", "loader"), None, None),
        P(("user", "loader"), None),
        P(("user", "loader")),
        P(),
        P("loader", None),
        P("loader", None),
        P(),
        P(),
        P(),
        P(("user", "loader"), None, None),
        P(("user", "loader"), None),
        P(("user", "loader")),
        P(("user", "loader"), None),
    )
    return jax.shard_map(
        body,
        mesh=mesh,
        in_specs=placed,
        out_specs=(
            P(("user", "loader"), None),
            P(("user", "loader"), None, None),
            P("loader", None),
        ),
        check_vma=False,
    )
```

```python
import functools
import math

import jax
import jax.numpy as jnp
from jax import lax
from jax.experimental import pallas as pl
from jax.experimental.pallas import tpu as pltpu
from jax.sharding import PartitionSpec as P

HEADS = 8
HIST = 128
LANES = 128
BF = jnp.bfloat16
F32 = jnp.float32
VMEM_BYTES = 56 * 1024 * 1024


def sigmoid(v):
    return 0.5 * jnp.tanh(0.5 * v) + 0.5


def dot(a, b):
    return jnp.dot(a, b, preferred_element_type=F32)


def dot_t(a, b):
    return lax.dot_general(a, b, (((1,), (1,)), ((), ())), preferred_element_type=F32)


def split3(v):
    high = v.astype(BF)
    rest = v - high.astype(F32)
    middle = rest.astype(BF)
    low = (rest - middle.astype(F32)).astype(BF)
    return high, middle, low


def prepare_kernel(nblocks, place_a, place_b, *refs):
    count = (len(refs) - 5) // 2
    halves = ((place_a, refs[:count]), (place_b, refs[count : 2 * count]))
    table, base, normed, rows_s, sems = refs[2 * count :]
    block = pl.program_id(0)
    width = base.shape[1]
    actions = table.shape[0]
    half = HIST // 2

    def fetch(which, b, source):
        return pltpu.make_async_copy(
            source, rows_s.at[b, pl.ds(which * half, half)], sems.at[which, b]
        )

    @pl.when(block == 0)
    def _():
        for b in range(nblocks):
            for which, (place, arrays) in enumerate(halves):
                for k, array in enumerate(arrays):

                    @pl.when(place[b] // 2 == k)
                    def _():
                        fetch(which, b, array.at[lax.rem(place[b], 2)]).start()

    for which, (place, arrays) in enumerate(halves):
        fetch(which, block, arrays[0].at[0]).wait()
    rows = rows_s[block]
    tail = rows[:, width:].astype(F32)
    lane = lax.broadcasted_iota(jnp.int32, (HIST, actions), 1).astype(F32)
    onehot = jnp.where(tail[:, :actions] == lane, 1.0, 0.0).astype(BF)
    value = rows[:, :width].astype(F32)
    high, middle, low = split3(table[...])
    value = value + ((dot(onehot, low) + dot(onehot, middle)) + dot(onehot, high))
    position = lax.broadcasted_iota(jnp.int32, (HIST, 1), 0).astype(F32)
    value = jnp.where(position < tail[:, LANES - 1 :], value, 0.0)
    scale = lax.rsqrt(jnp.mean(value * value, -1, keepdims=True) + 1e-06)
    base[...] = value
    normed[...] = (value * scale).astype(BF)


def prepare(place_a, place_b, halves_a, halves_b, table):
    nblocks = place_a.shape[0]
    width = table.shape[1]
    total = nblocks * HIST
    arrays = list(halves_a) + list(halves_b)
    return pl.pallas_call(
        functools.partial(prepare_kernel, nblocks),
        grid_spec=pltpu.PrefetchScalarGridSpec(
            num_scalar_prefetch=2,
            grid=(nblocks,),
            in_specs=[pl.BlockSpec(memory_space=pl.ANY)] * len(arrays)
            + [pl.BlockSpec(table.shape, lambda b, p, q: (0, 0))],
            out_specs=[
                pl.BlockSpec((HIST, width), lambda b, p, q: (b, 0)),
                pl.BlockSpec((HIST, width), lambda b, p, q: (b, 0)),
            ],
            scratch_shapes=[
                pltpu.VMEM((nblocks, HIST, arrays[0].shape[-1]), BF),
                pltpu.SemaphoreType.DMA((2, nblocks)),
            ],
        ),
        out_shape=[
            jax.ShapeDtypeStruct((total, width), F32),
            jax.ShapeDtypeStruct((total, width), BF),
        ],
        compiler_params=pltpu.CompilerParams(vmem_limit_bytes=VMEM_BYTES),
        name="prepare",
    )(place_a, place_b, *arrays, table)


ENCODE_STEPS = HEADS // 2
GROUP = 4


def attention_kernel(
    counts,
    core,
    normed,
    base,
    weights,
    queries,
    cand_t,
    score_weight,
    own,
    labels,
    scores,
    error,
    slopes,
    other,
    normed_s,
    base_s,
    mix_s,
    out_s,
    queries_s,
    cand_s,
    gate_s,
    mixed_s,
    qkv_s,
    gated_s,
    encoded_s,
    logit_s,
    weight_s,
    other_s,
    sems,
    mix_sems,
    grad_sems,
):
    total, width = normed_s.shape
    pair = 2 * LANES

    def mix_copy(i, group):
        start = pl.multiple_of(group * width + i * pair, pair)
        return pltpu.make_async_copy(
            weights.at[:, pl.ds(start, pair)], mix_s.at[i, group], mix_sems.at[i, group]
        )

    normed_copy = pltpu.make_async_copy(normed, normed_s, sems.at[0])
    base_copy = pltpu.make_async_copy(base, base_s, sems.at[1])
    out_copy = pltpu.make_async_copy(weights.at[:, pl.ds(4 * width, width)], out_s, sems.at[2])
    query_copy = pltpu.make_async_copy(queries, queries_s, sems.at[3])
    cand_copy = pltpu.make_async_copy(cand_t, cand_s, sems.at[4])

    normed_copy.start()
    for group in range(4):
        mix_copy(0, group).start()
    normed_copy.wait()

    @pl.loop(0, ENCODE_STEPS, unroll=True)
    def _(step):
        for group in range(4):
            mix_copy(step, group).wait()

        @pl.when(step + 1 < ENCODE_STEPS)
        def _():
            for group in range(4):
                mix_copy(step + 1, group).start()

        @pl.when(step == 1)
        def _():
            base_copy.start()

        @pl.when(step == 2)
        def _():
            out_copy.start()

        @pl.when(step == 3)
        def _():
            query_copy.start()
            cand_copy.start()

        users = total // HIST
        for k in range(2):
            cols = slice(k * LANES, (k + 1) * LANES)
            columns = jnp.concatenate([mix_s[step, g, :, cols] for g in range(4)], axis=1)
            projected = dot(normed_s[...], columns)
            projected = projected * sigmoid(projected)
            gate_s[2 * step + k] = projected[:, :LANES]
            qkv_s[k] = projected[:, LANES:].astype(BF)
        units = [(k, slice(u * HIST, (u + 1) * HIST)) for k in range(2) for u in range(users)]
        for n, (k, part) in enumerate(units):
            logit_s[n] = dot_t(qkv_s[k, part, LANES : 2 * LANES], qkv_s[k, part, 2 * LANES :])
        row = lax.broadcasted_iota(jnp.int32, (HIST, HIST), 0)
        column = lax.broadcasted_iota(jnp.int32, (HIST, HIST), 1)
        causal = column <= row
        for n in range(len(units)):
            logits = logit_s[n] * (1.0 / math.sqrt(LANES))
            weight = jnp.where(causal, logits * sigmoid(logits) * (1.0 / HIST), 0.0)
            weight_s[n] = weight.astype(BF)
        for n, (k, part) in enumerate(units):
            mixed_s[2 * step + k, part] = dot(weight_s[n], qkv_s[k, part, :LANES])

    square = mixed_s[0] * mixed_s[0]
    for h in range(1, HEADS):
        square = square + mixed_s[h] * mixed_s[h]
    scale = lax.rsqrt(jnp.sum(square, -1, keepdims=True) * (1.0 / width) + 1e-06)
    for h in range(HEADS):
        gated_s[:, h * LANES : (h + 1) * LANES] = (mixed_s[h] * scale * gate_s[h]).astype(BF)
    base_copy.wait()
    out_copy.wait()
    for n in range(width // pair):
        cols = slice(n * pair, (n + 1) * pair)
        value = (base_s[:, cols] + dot(gated_s[...], out_s[:, cols])).astype(BF)
        encoded_s[:, :, cols] = value.reshape(total // (GROUP * HIST), GROUP * HIST, pair)
    query_copy.wait()
    cand_copy.wait()

    @pl.loop(0, total // (GROUP * HIST), unroll=True)
    def _(now):
        lane = lax.broadcasted_iota(jnp.int32, (HEADS, width), 1) // LANES
        head_row = lax.broadcasted_iota(jnp.int32, (HEADS, width), 0)
        spread_weight = jnp.where(lane == head_row, score_weight[...], 0.0)
        high, middle, low = split3(spread_weight)
        parts = [slice(g * HIST, (g + 1) * HIST) for g in range(GROUP)]
        units = [(h, g) for g in range(GROUP) for h in range(HEADS)]
        heads = [slice(h * LANES, (h + 1) * LANES) for h in range(HEADS)]
        for n, (h, g) in enumerate(units):
            logit_s[n] = dot_t(
                queries_s[now, parts[g], heads[h]], encoded_s[now, parts[g], heads[h]]
            )
        along = []
        for part in parts:
            keys = encoded_s[now, part]
            along.append((dot_t(low, keys) + dot_t(middle, keys)) + dot_t(high, keys))
        totals = [jnp.zeros((HIST, HIST), F32) for _ in range(GROUP)]
        for n, (h, g) in enumerate(units):
            row = along[g][h : h + 1]
            logits = logit_s[n] * (1.0 / math.sqrt(LANES))
            gate = sigmoid(logits)
            product = logits * gate
            weight = (product * (1.0 / HIST)).astype(BF).astype(F32)
            totals[g] = totals[g] + weight * row
            slope = gate + product * (1.0 - gate)
            weight_s[n] = (slope * (row * (1.0 / (HIST * math.sqrt(LANES))))).astype(BF)
        for n, (h, g) in enumerate(units):
            logit_s[n] = dot(weight_s[n], encoded_s[now, parts[g], heads[h]])
        for g, part in enumerate(parts):
            partial = jnp.sum(totals[g], -1, keepdims=True).astype(BF).astype(F32)
            partial_row = jnp.broadcast_to(partial, (HIST, HIST)).T[:1]
            block = now * GROUP + g
            active = lax.broadcasted_iota(jnp.int32, (1, HIST), 1) < counts[block]
            score = jnp.where(active, partial_row + own[block], 0.0)
            err = jnp.where(active, sigmoid(score) - labels[block], 0.0)
            scores[block] = score
            error[block] = err
            err_rows = jnp.broadcast_to(err, (HIST, HIST)).T
            for h in range(HEADS):
                direction = logit_s[g * HEADS + h].astype(BF).astype(F32)
                slope = (err_rows * direction).astype(BF)
                slopes[now, part, heads[h]] = slope

    pairs, _, piece, _ = cand_s.shape
    _, _, tall, wide = other.shape
    right = width // wide
    down = piece // tall
    copies = []
    for n in range(right):
        cols = slice(n * wide, (n + 1) * wide)
        slope = slopes[:, :, cols].reshape(-1, wide)
        rows = cand_s[:, 1 - core[0]].reshape(pairs * piece, -1)
        place_pieces(dot(rows, slope).astype(BF), other_s, n * down, piece)
        chunk = pl.ds(n * down, down)
        copy = pltpu.make_async_copy(other_s.at[chunk], other.at[chunk], grad_sems.at[n])
        copy.start()
        copies.append(copy)
    for copy in copies:
        copy.wait()


def place_pieces(grad, store, first, piece):
    tall = store.shape[2]
    for p in range(store.shape[1]):
        for a in range(piece // tall):
            start = p * piece + a * tall
            store[first + a, p] = grad[start : start + tall]


def gradient_kernel(core, cand_t, slopes, out, cand_s, slope_s, sems):
    first = pltpu.make_async_copy(slopes, slope_s, sems.at[0])
    second = pltpu.make_async_copy(cand_t.at[:, core[0]], cand_s, sems.at[1])
    first.start()
    second.start()
    first.wait()
    second.wait()
    pairs, piece, total = cand_s.shape
    _, _, tall, wide = out.shape
    for n in range(slope_s.shape[1] // wide):
        cols = slice(n * wide, (n + 1) * wide)
        grad = dot(cand_s[...].reshape(pairs * piece, total), slope_s[:, cols])
        place_pieces(grad.astype(BF), out, n * (piece // tall), piece)


def gradient(core, cand_t, slopes, users):
    pairs, _, piece, total = cand_t.shape
    width = slopes.shape[1]
    side = math.isqrt(users)
    shape = (users, pairs, piece // side, width // side)
    return pl.pallas_call(
        gradient_kernel,
        grid_spec=pltpu.PrefetchScalarGridSpec(
            num_scalar_prefetch=1,
            grid=(1,),
            in_specs=[pl.BlockSpec(memory_space=pl.ANY)] * 2,
            out_specs=pl.BlockSpec(shape, lambda n, c: (0, 0, 0, 0)),
            scratch_shapes=[
                pltpu.VMEM((pairs, piece, total), BF),
                pltpu.VMEM((total, width), BF),
                pltpu.SemaphoreType.DMA((2,)),
            ],
        ),
        out_shape=jax.ShapeDtypeStruct(shape, BF),
        cost_estimate=pl.CostEstimate(
            flops=total * width * width, bytes_accessed=3 * total * width * 2, transcendentals=0
        ),
        compiler_params=pltpu.CompilerParams(vmem_limit_bytes=16 * 1024 * 1024),
        name="gradient",
    )(core, cand_t, slopes)


def attention(
    counts,
    core,
    normed,
    base,
    weights,
    queries,
    cand_t,
    score_weight,
    own,
    labels,
    pairs,
    users,
):
    nblocks = counts.shape[0]
    total, width = queries.shape
    rows = total // nblocks
    groups = nblocks // GROUP
    side = math.isqrt(users)
    shape = (users, pairs, width // (2 * pairs * side), width // side)
    row = pl.BlockSpec((nblocks, 1, rows), lambda i, n, c: (0, 0, 0))
    whole = lambda i, n, c: (0, 0)
    anywhere = pl.BlockSpec(memory_space=pl.ANY)
    return pl.pallas_call(
        attention_kernel,
        grid_spec=pltpu.PrefetchScalarGridSpec(
            num_scalar_prefetch=2,
            grid=(1,),
            in_specs=[anywhere] * 5
            + [
                pl.BlockSpec((1, width), whole),
                row,
                row,
            ],
            out_specs=[
                row,
                row,
                pl.BlockSpec((groups, GROUP * rows, width), lambda i, n, c: (0, 0, 0)),
                anywhere,
            ],
            scratch_shapes=[
                pltpu.VMEM((total, width), BF),
                pltpu.VMEM((total, width), F32),
                pltpu.VMEM((ENCODE_STEPS, 4, width, 2 * LANES), BF),
                pltpu.VMEM((width, width), BF),
                pltpu.VMEM((groups, GROUP * rows, width), BF),
                pltpu.VMEM((pairs, 2, width // (2 * pairs), total), BF),
                pltpu.VMEM((HEADS, total, LANES), F32),
                pltpu.VMEM((HEADS, total, LANES), F32),
                pltpu.VMEM((2, total, 3 * LANES), BF),
                pltpu.VMEM((total, width), BF),
                pltpu.VMEM((groups, GROUP * rows, width), BF),
                pltpu.VMEM((GROUP * HEADS, HIST, HIST), F32),
                pltpu.VMEM((GROUP * HEADS, HIST, HIST), BF),
                pltpu.VMEM(shape, BF),
                pltpu.SemaphoreType.DMA((5,)),
                pltpu.SemaphoreType.DMA((ENCODE_STEPS, 4)),
                pltpu.SemaphoreType.DMA((side,)),
            ],
        ),
        out_shape=[
            jax.ShapeDtypeStruct((nblocks, 1, rows), F32),
            jax.ShapeDtypeStruct((nblocks, 1, rows), F32),
            jax.ShapeDtypeStruct((groups, GROUP * rows, width), BF),
            jax.ShapeDtypeStruct(shape, BF),
        ],
        compiler_params=pltpu.CompilerParams(vmem_limit_bytes=51 * 1024 * 1024),
        name="attention",
    )(
        counts,
        core,
        normed,
        base,
        weights,
        queries.reshape(groups, GROUP * rows, width),
        cand_t,
        score_weight,
        own,
        labels,
    )


def shift(array, side, dx, dy):
    moves = []
    for x in range(side):
        for y in range(side):
            moves.append(((x + dx) % side * side + (y + dy) % side, x * side + y))
    return lax.ppermute(array, "user", moves)


def spread(piece, side, x_first):
    first = lambda a, d: shift(a, side, d, 0) if x_first else shift(a, side, 0, d)
    second = lambda a, d: shift(a, side, 0, d) if x_first else shift(a, side, d, 0)
    low = jnp.stack([piece, first(piece, 1)])
    high = jnp.stack([first(piece, 2), first(piece, -1)])
    low_after, high_before = second(low, 1), second(high, -1)
    high_after, low_before = second(high, 1), second(low, -1)
    low_two, high_two = second(low_after, 1), second(high_before, -1)
    return (low, high, low_after, high_after, low_two, high_two, low_before, high_before)


def join_kernel(left, right, out):
    wide = left.shape[1]
    out[:, :wide] = left[...]
    out[:, wide:] = right[...]


def join(left, right):
    return pl.pallas_call(
        join_kernel,
        out_shape=jax.ShapeDtypeStruct((left.shape[0], left.shape[1] + right.shape[1]), left.dtype),
        name="join",
    )(left, right)


def assemble_kernel(pieces, out):
    count, tall, wide = pieces.shape
    down = out.shape[0] // tall
    for k in range(count):
        a, b = k % down, k // down
        rows, cols = slice(a * tall, (a + 1) * tall), slice(b * wide, (b + 1) * wide)
        out[rows, cols] = pieces[k].astype(F32)


def assemble(pieces, right):
    count, tall, wide = pieces.shape
    return pl.pallas_call(
        assemble_kernel,
        out_shape=jax.ShapeDtypeStruct((count // right * tall, right * wide), F32),
        name="assemble",
    )(pieces)


def body(
    history_items,
    history_events,
    history_lengths,
    action_table,
    mix_weight,
    out_weight,
    query_weight,
    score_weight,
    self_weight,
    candidates,
    block_owner,
    row_counts,
    labels,
):
    users = lax.axis_size("user")
    loaders = lax.axis_size("loader")
    pairs = loaders // 2
    nblocks, rows, width = candidates.shape

    weights = lax.all_gather(join(mix_weight, out_weight), "loader", axis=0, tiled=True)
    actions = action_table.shape[0]
    packed = jnp.concatenate(
        [
            history_items[0],
            jnp.broadcast_to(history_events[0][:, None].astype(BF), (HIST, actions)),
            jnp.broadcast_to(history_lengths[0].astype(BF), (HIST, LANES - actions)),
        ],
        axis=1,
    )
    side = math.isqrt(users)
    half = HIST // 2
    halves_a = spread(packed[:half], side, True)
    halves_b = spread(packed[half:], side, False)

    flat = candidates.reshape(-1, width)
    queries = jnp.dot(flat, query_weight, preferred_element_type=F32).astype(BF)
    cand_t = flat.T.reshape(pairs, 2, width // loaders, -1)
    own = jnp.sum(candidates.astype(F32) * self_weight, -1)

    owner = block_owner[:, 0]
    here = lax.axis_index("user").astype(jnp.int32)
    far_x = lax.rem(owner // side - here // side + side, side)
    far_y = lax.rem(lax.rem(owner, side) - lax.rem(here, side) + side, side)
    base, normed = prepare(
        far_y * side + far_x, far_x * side + far_y, halves_a, halves_b, action_table
    )
    core = lax.rem(lax.axis_index("loader").astype(jnp.int32), 2)[None]
    scores, error, slopes, other = attention(
        row_counts,
        core,
        normed,
        base,
        weights,
        queries,
        cand_t,
        score_weight[None],
        own[:, None],
        labels[:, None],
        pairs,
        users,
    )

    arrived = lax.ppermute(other, "loader", [(i, i ^ 1) for i in range(loaders)])
    slopes = slopes.reshape(-1, width)
    mine = gradient(core, cand_t, slopes, users)
    pieces = (mine.astype(F32) + arrived.astype(F32)).astype(BF)
    pieces = lax.all_to_all(pieces, "user", 0, 0, tiled=True)
    pieces = jnp.sum(pieces.astype(F32), 0).astype(BF)
    groups = [[c + 2 * i for i in range(pairs)] for c in range(2)]
    pieces = lax.all_to_all(pieces, "loader", 0, 0, axis_index_groups=groups, tiled=True)
    piece = jnp.sum(pieces.astype(F32), 0).astype(BF)
    pieces = lax.all_to_all(
        jnp.broadcast_to(piece[None], (users,) + piece.shape), "user", 0, 0, tiled=True
    )
    query_grad = assemble(pieces, side)

    back = lax.dot_general(slopes, query_weight, (((1,), (1,)), ((), ())), preferred_element_type=F32)
    row_grads = (error.reshape(-1)[:, None] * self_weight + back).astype(BF)
    return (scores[:, 0], row_grads.reshape(nblocks, rows, width), query_grad)


def solution(mesh):
    placed = (
        P(("user", "loader"), None, None),
        P(("user", "loader"), None),
        P(("user", "loader")),
        P(),
        P("loader", None),
        P("loader", None),
        P(),
        P(),
        P(),
        P(("user", "loader"), None, None),
        P(("user", "loader"), None),
        P(("user", "loader")),
        P(("user", "loader"), None),
    )
    return jax.shard_map(
        body,
        mesh=mesh,
        in_specs=placed,
        out_specs=(
            P(("user", "loader"), None),
            P(("user", "loader"), None, None),
            P("loader", None),
        ),
        check_vma=False,
    )
```
